256 devices in a mesh: gx: 16 (over z_lo, y, core), gy: 4 (over x), grp: 4 (over z_hi).
Axes of the slice: x: 4, y: 4, z: 8 (z_hi: 4, z_lo: 2; z = z_hi * 2 + z_lo), core: 2. Of those that a mesh axis runs over, the one named last changes fastest.
Arguments:
- deflation: bfloat16 [32, 3, 128, 64, 256], P('grp', None, 'gx', 'gy'), may hold values from -3.3 to 3.3
- region: int32 [128, 64, 256], P('gx', 'gy'), may hold values from 0 to 7
- lame_table: float32 [8, 2], replicated, may hold values from 0.3 to 3
- residual: float32 [3, 128, 64, 256], P(None, 'gx', 'gy'), may hold values from -5 to 5
Outputs:
- coarse_rows: float32 [16, 4, 3, 3, 32, 32], P('gx', 'gy', None, None, 'grp')
- coarse_solution: float32 [16, 4, 32], P(None, 'gy')
- correction: float32 [3, 128, 64, 256], P(None, 'gx', 'gy', 'grp')
The draws below stay inside these ranges and needn't reach their ends.
All inputs are finite; a program needn't handle non-finite values.
Results may differ from the reference program's by a relative error of at most 0.0003.
Values may be sent and summed in bfloat16 or wider, within the bound.
A program may use at most 128 MiB of HBM per device.

```python
import math
import jax
import jax.numpy as jnp
from jax import lax

VECS = 32
CX = 8
CY = 16
CZ = 256
REGIONS = 8
NX = 128
NY = 64
N_GX = 16
N_GY = 4


def draw_deflation(key, part):
    key = jax.random.fold_in(key, 11)
    key_level, key_rough = jax.random.split(key)
    count_x = NX // CX
    count_y = NY // CY
    levels = jnp.clip(jax.random.normal(key_level, (VECS, 3, count_x, 1, count_y, 1, 1), jnp.float32), -2.5, 2.5)
    roughness = 0.2 * jnp.clip(jax.random.normal(key_rough, (VECS, 3, count_x, CX, count_y, CY, CZ), jnp.float32), -4.0, 4.0)
    return (levels + roughness).reshape(VECS, 3, NX, NY, CZ).astype(jnp.bfloat16)


def draw_residual(key, part):
    key = jax.random.fold_in(key, 12)
    key_level, key_rough = jax.random.split(key)
    count_x = NX // CX
    count_y = NY // CY
    levels = jnp.clip(jax.random.normal(key_level, (3, count_x, 1, count_y, 1, 1), jnp.float32), -3.0, 3.0)
    roughness = 0.5 * jnp.clip(jax.random.normal(key_rough, (3, count_x, CX, count_y, CY, CZ), jnp.float32), -4.0, 4.0)
    return (levels + roughness).reshape(3, NX, NY, CZ).astype(jnp.float32)


def plant(entries, rng, low, high):
    dims = entries.shape
    index_at = [jax.random.randint(jax.random.fold_in(rng, axis), (), 0, dims[axis]) for axis in range(len(dims))]
    entries = entries.at[tuple(index_at)].set(low)
    longest = dims.index(max(dims))
    index_at[longest] = (index_at[longest] + 1) % dims[longest]
    return entries.at[tuple(index_at)].set(high)


def setup_inputs(seed: int = 0) -> dict:
    key_list = jax.random.split(jax.random.key(seed), 5)
    return {
        "deflation": draw_deflation(jax.random.fold_in(key_list[4], 71), 0),
        "region": plant(jax.random.randint(key_list[1], (NX, NY, CZ), 0, REGIONS), jax.random.fold_in(key_list[1], 1), 0, REGIONS - 1).astype(jnp.int32),
        "lame_table": jnp.clip(jnp.exp(jax.random.uniform(key_list[2], (REGIONS, 2), jnp.float32, math.log(0.3), math.log(3.0))), 0.3, 3.0),
        "residual": draw_residual(jax.random.fold_in(key_list[4], 71), 0),
    }


mass_shift = 0.5
stencil_offsets = [(off_x, off_y, off_z) for off_x in (-1, 0, 1) for off_y in (-1, 0, 1) for off_z in (-1, 0, 1) if (off_x, off_y, off_z) != (0, 0, 0)]

def stencil(padded, shear_pad, bulk_pad):
    center = padded[:, :, 1:-1, 1:-1, 1:-1]
    shear_center = shear_pad[1:-1, 1:-1, 1:-1]
    size_x, size_y, size_z = (center.shape[2], center.shape[3], center.shape[4])
    summed = mass_shift * center
    for off_x, off_y, off_z in stencil_offsets:
        weight = 0.5 ** (abs(off_x) + abs(off_y) + abs(off_z) - 1)
        shear_near = shear_pad[1 + off_x:1 + off_x + size_x, 1 + off_y:1 + off_y + size_y, 1 + off_z:1 + off_z + size_z]
        neighbor = padded[:, :, 1 + off_x:1 + off_x + size_x, 1 + off_y:1 + off_y + size_y, 1 + off_z:1 + off_z + size_z]
        couple = 0.5 * weight * (shear_center + shear_near)
        summed = summed + couple * (center - neighbor)
    average = jnp.mean(center, axis=1, keepdims=True)
    return summed + bulk_pad * (center - average)

def block_products(applied, window):
    size_x = applied.shape[2] - 2
    size_y = applied.shape[3] - 2
    scale_factor = 1.0 / (3.0 * size_x * size_y * applied.shape[4])
    applied_hi = lax.optimization_barrier(applied.astype(jnp.bfloat16))
    applied_lo = (applied - applied_hi.astype(jnp.float32)).astype(jnp.bfloat16)
    window = window.astype(jnp.bfloat16)
    ranges_x = ((0, 1), (1, size_x + 1), (size_x + 1, size_x + 2))
    ranges_y = ((0, 1), (1, size_y + 1), (size_y + 1, size_y + 2))
    blocks = []
    for low_x, high_x in ranges_x:
        for low_y, high_y in ranges_y:
            piece = window[:, :, low_x:high_x, low_y:high_y, :]
            high_part = jnp.einsum('pkxyz,qkxyz->pq', applied_hi[:, :, low_x:high_x, low_y:high_y, :].astype(jnp.float32), piece.astype(jnp.float32), preferred_element_type=jnp.float32)
            low_part = jnp.einsum('pkxyz,qkxyz->pq', applied_lo[:, :, low_x:high_x, low_y:high_y, :].astype(jnp.float32), piece.astype(jnp.float32), preferred_element_type=jnp.float32)
            blocks.append(high_part + low_part)
    return (jnp.stack(blocks) * scale_factor).reshape(3, 3, applied.shape[0], window.shape[0])

def block_inverse(square):
    width = square.shape[0]
    factor = jnp.linalg.cholesky(square)
    return jax.scipy.linalg.cho_solve((factor, True), jnp.eye(width, dtype=square.dtype))

def line_solve(row_blocks, coarse_rhs):
    block_width = row_blocks.shape[2]
    lower_blocks = row_blocks[:, 0]
    diagonal_blocks = row_blocks[:, 1]
    upper_next = jnp.concatenate([lower_blocks[1:], jnp.zeros((1, block_width, block_width), jnp.float32)], axis=0)

    def forward(carry, items):
        inverse_prev, folded_prev = carry
        lower, diagonal, target = items
        multiplier = jnp.dot(lower, inverse_prev, precision=lax.Precision.HIGHEST)
        schur = diagonal - jnp.dot(multiplier, lower.T, precision=lax.Precision.HIGHEST)
        schur = jnp.tril(schur) + jnp.tril(schur, -1).T
        inverse_now = block_inverse(schur)
        folded = target - jnp.dot(multiplier, folded_prev, precision=lax.Precision.HIGHEST)
        return ((inverse_now, folded), (inverse_now, folded))
    start = (jnp.zeros((block_width, block_width), jnp.float32), jnp.zeros((block_width,), jnp.float32))
    _, (inverses, folded_all) = lax.scan(forward, start, (lower_blocks, diagonal_blocks, coarse_rhs))

    def backward(later, items):
        inverse_now, folded, upper = items
        value = jnp.dot(inverse_now, folded - jnp.dot(upper.T, later, precision=lax.Precision.HIGHEST), precision=lax.Precision.HIGHEST)
        return (value, value)
    _, solved = lax.scan(backward, jnp.zeros((block_width,), jnp.float32), (inverses, folded_all, upper_next), reverse=True)
    return solved

def reference(deflation, region, lame_table, residual):
    shear = lame_table[:, 0][region]
    bulk = lame_table[:, 1][region]
    shear_global = jnp.pad(shear, ((1, 1), (1, 1), (0, 0)))
    window_global = jnp.pad(deflation, ((0, 0), (0, 0), (1, 1), (1, 1), (0, 0)))

    def per_subdomain(sub_index):
        start_x = (sub_index // N_GY * CX).astype(jnp.int32)
        start_y = (sub_index % N_GY * CY).astype(jnp.int32)
        zero = jnp.zeros((), jnp.int32)
        own_vectors = lax.dynamic_slice(deflation, (zero, zero, start_x, start_y, zero), (VECS, 3, CX, CY, CZ)).astype(jnp.float32)
        shear_rim = lax.dynamic_slice(shear_global, (start_x, start_y, zero), (CX + 2, CY + 2, CZ))
        shear_pad = jnp.pad(shear_rim, ((1, 1), (1, 1), (1, 1)))
        bulk_pad = jnp.pad(lax.dynamic_slice(bulk, (start_x, start_y, zero), (CX, CY, CZ)), ((1, 1), (1, 1), (0, 0)))
        padded = jnp.pad(own_vectors, ((0, 0), (0, 0), (2, 2), (2, 2), (1, 1)))
        applied = stencil(padded, shear_pad, bulk_pad)
        window = lax.dynamic_slice(window_global, (zero, zero, start_x, start_y, zero), (VECS, 3, CX + 2, CY + 2, CZ))
        local_residual = lax.dynamic_slice(residual, (zero, start_x, start_y, zero), (3, CX, CY, CZ))
        coarse_rhs = jnp.einsum('pkxyz,kxyz->p', own_vectors, local_residual, precision=lax.Precision.HIGHEST) / (3.0 * CX * CY * CZ)
        return (block_products(applied, window), coarse_rhs)
    coarse_rows, coarse_rhs = lax.map(per_subdomain, jnp.arange(N_GX * N_GY, dtype=jnp.int32))
    coarse_rows = coarse_rows.reshape(N_GX, N_GY, 3, 3, VECS, VECS)
    coarse_rhs = coarse_rhs.reshape(N_GX, N_GY, VECS)
    coarse_solution = jnp.stack([line_solve(coarse_rows[:, column, :, 1], coarse_rhs[:, column]) for column in range(N_GY)], axis=1)

    def slab_correction(slab_x):
        slab_vectors = lax.dynamic_slice_in_dim(deflation, (slab_x * CX).astype(jnp.int32), CX, 2).astype(jnp.float32)
        slab_vectors = slab_vectors.reshape(VECS, 3, CX, N_GY, CY, CZ)
        weights = coarse_solution[slab_x]
        return jnp.einsum('gq,qkxgyz->kxgyz', weights, slab_vectors, precision=lax.Precision.HIGHEST).reshape(3, CX, NY, CZ)
    pieces = lax.map(slab_correction, jnp.arange(N_GX, dtype=jnp.int32))
    correction = pieces.transpose(1, 0, 2, 3, 4).reshape(3, NX, NY, CZ)
    return (coarse_rows, coarse_solution, correction)
```

```python
import functools

import jax
import jax.numpy as jnp
from jax import lax
from jax.experimental import pallas as pl
from jax.experimental.pallas import tpu as pltpu
from jax.sharding import PartitionSpec as P

MESH = pl.DeviceIdType.MESH
F32 = jnp.float32
BF16 = jnp.bfloat16
VECS = 32
OWN = 8
PARTS = 4
COMPS = 3
CX = 8
CY = 16
CZ = 256
XQ = 4
REGIONS = 8
LINE = 16
CELLS = COMPS * CX * CY * CZ
BLOCKS = ((1, 1), (0, 1), (2, 1), None, (1, 0), (1, 2), (0, 0), (0, 2), (2, 0), (2, 2))
CHUNKS = (0, 3, 1, 2)
VMEM = pl.BlockSpec(memory_space=pltpu.VMEM)
SMEM = pl.BlockSpec(memory_space=pltpu.SMEM)
LIMIT = 48 * 1024 * 1024


def lanes(rows):
    return lax.broadcasted_iota(jnp.int32, (rows, 128), 1)


def roll(x, shift):
    return pltpu.roll(x, shift % 128, x.ndim - 1)


def filter_z(v, edge):
    lane = lanes(v.shape[0]) & 63
    before = jnp.where(lane == 0, edge, roll(v, 1))
    after = jnp.where(lane == 63, edge, roll(v, -1))
    return v + 0.5 * (before + after)


def halves(a, b):
    low = lanes(a.shape[0]) < 64
    return jnp.where(low, a, b)


def pack_kernel(vec, region, lame, res, send, edge, mat, rhs, rows):
    low = lanes(8) < 64
    lane = lanes(8) & 63

    def component(k, total):
        for pair in range(2):
            acc = [jnp.zeros((8, 128), F32) for _ in range(PARTS)]
            for sub in range(2):
                xq = 2 * pair + sub
                for half in range(2):
                    for p in range(OWN):
                        plane = vec[p, k, xq + XQ * half].astype(F32)
                        for t in range(2):
                            rows[half, t, pl.ds(p, CY, stride=OWN), :] = plane[:, 128 * t : 128 * t + 128]
                for y2 in range(CY // 2):
                    both = []
                    for yy in range(2):
                        y = 2 * y2 + yy
                        blocks = []
                        for t in range(2):
                            a = rows[0, t, OWN * y : OWN * y + OWN, :]
                            b = rows[1, t, OWN * y : OWN * y + OWN, :]
                            total = total + a * res[k, xq, y : y + 1, 128 * t : 128 * t + 128]
                            total = total + b * res[k, xq + XQ, y : y + 1, 128 * t : 128 * t + 128]
                            blocks.append(jnp.where(low, a, roll(b, 64)))
                            blocks.append(jnp.where(low, roll(a, 64), b))
                        e = 2 * (CY * sub + y)
                        for g in range(PARTS):
                            if g > 0:
                                acc[g] = jnp.where(lane == e, roll(blocks[g - 1], e + 65), acc[g])
                            if g < PARTS - 1:
                                acc[g] = jnp.where(lane == ((e + 63) & 63), roll(blocks[g + 1], e + 63), acc[g])
                        both.append(blocks)
                    for g in range(PARTS):
                        send[g, k, xq, y2] = jnp.concatenate([both[0][g], both[1][g]], axis=0).astype(BF16)
            for g in range(PARTS):
                rows[2, 0, 16 * g + 8 * pair : 16 * g + 8 * pair + 8, :] = acc[g]
        for g in range(PARTS):
            edge[g, k] = rows[2, 0, 16 * g : 16 * g + 16, :].astype(BF16)
        return total

    total = lax.fori_loop(0, COMPS, component, jnp.zeros((8, 128), F32))
    rhs[...] = jnp.broadcast_to(jnp.sum(total, axis=1, keepdims=True) * (1.0 / CELLS), (8, 128))

    me = lax.axis_index("grp")
    low = lanes(CY) < 64
    lane = lanes(CY) & 63
    for xq in range(XQ):
        for which in range(2):
            tiles = []
            for half in range(2):
                kind = region[xq + XQ * half]
                value = jnp.zeros((CY, CZ), F32)
                for label in range(REGIONS):
                    value = jnp.where(kind == label, lame[label, which], value)
                tiles.append(value)
            blocks = []
            for t in range(2):
                a = tiles[0][:, 128 * t : 128 * t + 128]
                b = tiles[1][:, 128 * t : 128 * t + 128]
                blocks.append(jnp.where(low, a, roll(b, 64)))
                blocks.append(jnp.where(low, roll(a, 64), b))
            own = jnp.zeros((CY, 128), F32)
            rim = jnp.zeros((CY, 128), F32)
            for g in range(PARTS):
                own = jnp.where(me == g, blocks[g], own)
                if which == 0 and g > 0:
                    rim = jnp.where((me == g) & (lane == 0), roll(blocks[g - 1], 65), rim)
                if which == 0 and g < PARTS - 1:
                    rim = jnp.where((me == g) & (lane == 63), roll(blocks[g + 1], 63), rim)
            if which == 0:
                mat[0, xq] = own
                mat[1, xq] = rim
            else:
                mat[2, xq] = own


def pack(deflation, region, lame_table, residual):
    return pl.pallas_call(
        pack_kernel,
        name="pack",
        out_shape=(
            jax.ShapeDtypeStruct((PARTS, COMPS, XQ, CY // 2, 16, 128), BF16),
            jax.ShapeDtypeStruct((PARTS, COMPS, 16, 128), BF16),
            jax.ShapeDtypeStruct((3, XQ, CY, 128), F32),
            jax.ShapeDtypeStruct((8, 128), F32),
        ),
        in_specs=[VMEM, VMEM, SMEM, VMEM],
        out_specs=[VMEM] * 4,
        scratch_shapes=[pltpu.VMEM((3, 2, 128, 128), F32)],
        compiler_params=pltpu.CompilerParams(vmem_limit_bytes=LIMIT),
    )(deflation, region, lame_table, residual)


SIDES = ((-1, 0), (1, 0), (0, -1), (0, 1), (-1, -1), (-1, 1), (1, -1), (1, 1))


def exchange_kernel(send, edge, mat, recv, zh, xf, yf, cf, sx, sy, sc, stage, zs, zr, hs, hr, ms, mr, own_sem):
    gx, gy, g = lax.axis_index("gx"), lax.axis_index("gy"), lax.axis_index("grp")
    nx, ny = lax.axis_size("gx"), lax.axis_size("gy")
    up, down, far = lax.rem(g + 1, 4), lax.rem(g + 3, 4), lax.rem(g + 2, 4)
    near = {}
    for dx, dy in SIDES:
        near[dx, dy] = {"gx": lax.rem(gx + dx + nx, nx), "gy": lax.rem(gy + dy + ny, ny)}
    barrier = pltpu.get_barrier_semaphore()
    for side in SIDES:
        pl.semaphore_signal(barrier, inc=1, device_id=near[side], device_id_type=MESH)
    for other in (up, down, far):
        pl.semaphore_signal(barrier, inc=1, device_id={"grp": other}, device_id_type=MESH)
    pl.semaphore_wait(barrier, 11)

    def zcopy(src, dst, index, other):
        return pltpu.make_async_remote_copy(
            src_ref=src, dst_ref=dst, send_sem=zs.at[index], recv_sem=zr.at[index],
            device_id={"grp": other}, device_id_type=MESH,
        )

    far_up = [zcopy(send.at[far, :, c], stage.at[0, i], i, up) for i, c in enumerate((0, 1))]
    far_down = [zcopy(send.at[far, :, c], stage.at[1, i], 2 + i, down) for i, c in enumerate((3, 2))]
    fwd_up = [zcopy(stage.at[0, i], recv.at[down, :, c], 4 + i, up) for i, c in enumerate((0, 1))]
    fwd_down = [zcopy(stage.at[1, i], recv.at[up, :, c], 6 + i, down) for i, c in enumerate((3, 2))]
    near_up = [zcopy(send.at[up, :, c], recv.at[g, :, c], 8 + i, up) for i, c in enumerate(CHUNKS)]
    near_down = [zcopy(send.at[down, :, c], recv.at[g, :, c], 12 + i, down) for i, c in enumerate(CHUNKS)]
    edges = [zcopy(edge.at[o], zh.at[g], 16 + i, o) for i, o in enumerate((up, down, far))]
    far_up[0].start()
    far_down[0].start()
    for c in edges:
        c.start()
    own = pltpu.make_async_copy(send.at[g], recv.at[g], own_sem.at[0])
    own_edge = pltpu.make_async_copy(edge.at[g], zh.at[g], own_sem.at[1])
    own.start()
    own_edge.start()

    def mcopy(src, dst, index, side):
        return pltpu.make_async_remote_copy(
            src_ref=src, dst_ref=dst, send_sem=ms.at[index], recv_sem=mr.at[index],
            device_id=near[side], device_id_type=MESH,
        )

    tile = {-1: 0, 1: 3}
    row = {-1: 0, 1: 8}
    pair = {-1: 0, 1: 7}
    mats = []
    for dx in (-1, 1):
        slot = 1 if dx < 0 else 0
        mats.append(mcopy(mat.at[pl.ds(0, 2), tile[dx]], sx.at[slot], len(mats), (dx, 0)))
    for dy in (-1, 1):
        slot = 1 if dy < 0 else 0
        mats.append(mcopy(mat.at[pl.ds(0, 2), :, pl.ds(row[dy], 8)], sy.at[slot], len(mats), (0, dy)))
    for dx in (-1, 1):
        for dy in (-1, 1):
            slot = (2 if dx < 0 else 0) + (1 if dy < 0 else 0)
            mats.append(mcopy(mat.at[pl.ds(0, 2), tile[dx], pl.ds(row[dy], 8)], sc.at[slot], len(mats), (dx, dy)))
    for c in mats:
        c.start()
    near_up[0].start()
    near_down[0].start()
    near_up[1].start()
    near_down[1].start()
    far_up[1].start()
    far_down[1].start()
    for i in (2, 3):
        near_up[i].start()
        near_down[i].start()

    halo = []

    def rim(order, src, chunk):
        base = 14 * order

        def hcopy(a, b, index, side):
            c = pltpu.make_async_remote_copy(
                src_ref=a, dst_ref=b, send_sem=hs.at[base + index], recv_sem=hr.at[base + index],
                device_id=near[side], device_id_type=MESH,
            )
            c.start()
            halo.append(c)

        at = CHUNKS.index(chunk)
        for i, dy in enumerate((-1, 1)):
            slot = 1 if dy < 0 else 0
            hcopy(recv.at[src, :, chunk, pair[dy]], yf.at[slot, src, :, chunk], 2 * at + i, (0, dy))
        for dx in (-1, 1):
            if tile[dx] != chunk:
                continue
            slot = 1 if dx < 0 else 0
            hcopy(recv.at[src, :, chunk], xf.at[slot, src], 8 + slot, (dx, 0))
            for i, dy in enumerate((-1, 1)):
                at_c = (2 if dx < 0 else 0) + (1 if dy < 0 else 0)
                hcopy(recv.at[src, :, chunk, pair[dy]], cf.at[at_c, src], 10 + at_c, (dx, dy))

    own.wait()
    own_edge.wait()
    for c in CHUNKS:
        rim(0, g, c)
    far_up[0].wait_recv()
    fwd_up[0].start()
    far_down[0].wait_recv()
    fwd_down[0].start()
    for i in (0, 1):
        near_up[i].wait_recv()
        rim(1, down, CHUNKS[i])
        near_down[i].wait_recv()
        rim(2, up, CHUNKS[i])
    far_up[1].wait_recv()
    fwd_up[1].start()
    far_down[1].wait_recv()
    fwd_down[1].start()
    fwd_up[0].wait_recv()
    rim(3, far, 0)
    fwd_down[0].wait_recv()
    rim(3, far, 3)
    for i in (2, 3):
        near_up[i].wait_recv()
        rim(1, down, CHUNKS[i])
        near_down[i].wait_recv()
        rim(2, up, CHUNKS[i])
    fwd_up[1].wait_recv()
    rim(3, far, 1)
    fwd_down[1].wait_recv()
    rim(3, far, 2)
    for c in edges:
        c.wait_recv()
    for c in mats + halo:
        c.wait_recv()
    for c in far_up + far_down + fwd_up + fwd_down + near_up + near_down + edges + mats + halo:
        c.wait_send()


def exchange(send, edge, mat):
    return pl.pallas_call(
        exchange_kernel,
        name="exchange",
        out_shape=(
            jax.ShapeDtypeStruct((PARTS, COMPS, XQ, CY // 2, 16, 128), BF16),
            jax.ShapeDtypeStruct((PARTS, COMPS, 16, 128), BF16),
            jax.ShapeDtypeStruct((2, PARTS, COMPS, CY // 2, 16, 128), BF16),
            jax.ShapeDtypeStruct((2, PARTS, COMPS, XQ, 16, 128), BF16),
            jax.ShapeDtypeStruct((4, PARTS, COMPS, 16, 128), BF16),
            jax.ShapeDtypeStruct((2, 2, CY, 128), F32),
            jax.ShapeDtypeStruct((2, 2, XQ, 8, 128), F32),
            jax.ShapeDtypeStruct((4, 2, 8, 128), F32),
        ),
        in_specs=[VMEM] * 3,
        out_specs=[VMEM] * 8,
        scratch_shapes=[
            pltpu.VMEM((2, 2, COMPS, CY // 2, 16, 128), BF16),
            pltpu.SemaphoreType.DMA((19,)),
            pltpu.SemaphoreType.DMA((19,)),
            pltpu.SemaphoreType.DMA((56,)),
            pltpu.SemaphoreType.DMA((56,)),
            pltpu.SemaphoreType.DMA((8,)),
            pltpu.SemaphoreType.DMA((8,)),
            pltpu.SemaphoreType.DMA((2,)),
        ],
        compiler_params=pltpu.CompilerParams(
            vmem_limit_bytes=LIMIT, collective_id=0, has_side_effects=True
        ),
    )(send, edge, mat)


def split(value):
    high = value.astype(BF16)
    return high, (value - high.astype(F32)).astype(BF16)


def dot_nt(a, b):
    return lax.dot_general(a, b, (((1,), (1,)), ((), ())), preferred_element_type=F32)


def filter_x(b):
    low = lanes(b[0].shape[0]) < 64
    zero = jnp.zeros_like(b[0])
    before = [jnp.where(low, zero, roll(b[3], 64))] + b[:3]
    after = b[1:] + [jnp.where(low, roll(b[0], 64), zero)]
    return [mid + 0.5 * (lo + hi) for mid, lo, hi in zip(b, before, after)]


def gram_kernel(recv, zh, xf, yf, cf, mat, sx, sy, sc, rhs, out,
                zf, hz, hh, hy, hp, se, sh, db, hb, tmp, wide, acc_c, acc_x, acc_y, acc_n):
    gx, gy, g = lax.axis_index("gx"), lax.axis_index("gy"), lax.axis_index("grp")
    nx, ny = lax.axis_size("gx"), lax.axis_size("gy")
    live_x = (jnp.where(gx > 0, 1.0, 0.0).astype(F32), jnp.where(gx < nx - 1, 1.0, 0.0).astype(F32))
    live_y = (jnp.where(gy > 0, 1.0, 0.0).astype(F32), jnp.where(gy < ny - 1, 1.0, 0.0).astype(F32))

    for target, t in ((se, 0), (sh, 1)):
        target[...] = jnp.zeros_like(target)

        def wider(own, minus, plus):
            return roll(halves(own[3], minus), 64), roll(halves(plus, own[0]), 64)

        own = [mat[t, xq] for xq in range(XQ)]
        first, last = wider(own, sx[0, t] * live_x[0], sx[1, t] * live_x[1])
        for xq, value in enumerate([first] + own + [last]):
            target[xq, 8:24, :] = value
        for j, at, src in ((0, 7, 7), (1, 24, 0)):
            own = [sy[j, t, xq, src : src + 1, :] * live_y[j] for xq in range(XQ)]
            first, last = wider(
                own,
                sc[j, t, src : src + 1, :] * (live_x[0] * live_y[j]),
                sc[2 + j, t, src : src + 1, :] * (live_x[1] * live_y[j]),
            )
            for xq, value in enumerate([first] + own + [last]):
                target[xq, at : at + 1, :] = value
    fz = [filter_z(se[xq], sh[xq]) for xq in range(XQ + 2)]
    for xq in range(XQ):
        tmp[...] = fz[xq + 1] + 0.5 * (fz[xq] + fz[xq + 2])
        smooth = tmp[8:24, :] + 0.5 * (tmp[7:23, :] + tmp[9:25, :])
        bulk = mat[2, xq]
        db[xq] = 0.5 * (0.5 + 8.0 * mat[0, xq] + smooth + bulk)
        hb[xq] = bulk * (1.0 / 6.0)

    def cast(k, _):
        for xq in range(XQ):
            for y2 in range(CY // 2):
                for src in range(PARTS):
                    value = recv[src, k, xq, y2].astype(F32)
                    zf[k, xq, 2 * y2, 8 * src : 8 * src + 8, :] = value[:8]
                    zf[k, xq, 2 * y2 + 1, 8 * src : 8 * src + 8, :] = value[8:]
        return 0

    lax.fori_loop(0, COMPS, cast, 0)
    acc_c[...] = jnp.zeros_like(acc_c)
    acc_x[...] = jnp.zeros_like(acc_x)
    acc_y[...] = jnp.zeros_like(acc_y)
    acc_n[...] = jnp.zeros_like(acc_n)
    low = lanes(VECS) < 64
    zero = jnp.zeros((VECS, 128), F32)

    def scaled(ref, xq, y):
        return ref[xq, y + 8 : y + 9, :]

    def rows_of(ref_at, yy):
        parts = [ref_at(src)[8 * yy : 8 * yy + 8] for src in range(PARTS)]
        return jnp.concatenate(parts, axis=0)

    def component(k, _):
        for xq in range(XQ):
            for y in range(CY):
                e = 2 * (CY * (xq % 2) + y)
                blocks = []
                for src in range(PARTS):
                    blk = zh[src, k].astype(F32)[8 * (xq // 2) : 8 * (xq // 2) + 8]
                    blocks.append(roll(blk, -e))
                around = jnp.concatenate(blocks, axis=0)
                hh[xq, y] = around
                hz[xq, y] = filter_z(zf[k, xq, y], around)
        for xq in range(XQ):
            hy[xq, 0] = 0.5 * hz[xq, 0]
            hy[xq, CY + 1] = 0.5 * hz[xq, CY - 1]
            for y in range(CY):
                sides = [hz[xq, y + d] for d in (-1, 1) if 0 <= y + d < CY]
                both = sides[0] + sides[1] if len(sides) == 2 else sides[0]
                hy[xq, y + 1] = hz[xq, y] + 0.5 * both
        for y4 in range(CY // 4):
            for y in range(4 * y4, 4 * y4 + 4):
                smooth = filter_x([hy[xq, y + 1] for xq in range(XQ)])
                for xq in range(XQ):
                    v = zf[k, xq, y]
                    mean = zf[0, xq, y] + zf[1, xq, y] + zf[2, xq, y]
                    w = db[xq, y : y + 1, :] * v - hb[xq, y : y + 1, :] * mean - scaled(se, xq + 1, y) * smooth[xq]
                    high, rest = split(w)
                    at = 128 * (XQ * (y - 4 * y4) + xq)
                    wide[0:32, at : at + 128] = high
                    wide[32:64, at : at + 128] = rest
                    wide[64:96, at : at + 128] = v.astype(BF16)
            acc_c[...] += dot_nt(wide[0:64, :], wide[64:96, :])
        for j, y, inside, yy in ((0, -1, 0, 1), (1, CY, CY - 1, 0)):
            smooth = filter_x([hy[xq, y + 1] for xq in range(XQ)])
            scaled_z = []
            for xq in range(XQ):
                u = scaled(se, xq + 1, inside) * zf[k, xq, inside]
                scaled_z.append(filter_z(u, scaled(sh, xq + 1, inside) * hh[xq, inside]))
            scaled_z = filter_x(scaled_z)
            left, right = [], []
            for xq in range(XQ):
                value = -(scaled(se, xq + 1, y) * smooth[xq] + 0.5 * scaled_z[xq])
                high, rest = split(value)
                left.append(jnp.concatenate([high, rest], axis=0))
                right.append(rows_of(lambda src: yf[j, src, k, xq].astype(F32), yy).astype(BF16))
            acc_y[j] += dot_nt(jnp.concatenate(left, axis=1), jnp.concatenate(right, axis=1))
        for y in range(CY):
            u = halves(scaled(se, 1, y) * zf[k, 0, y], scaled(se, 4, y) * zf[k, 3, y])
            around = halves(scaled(sh, 1, y) * hh[0, y], scaled(sh, 4, y) * hh[3, y])
            hp[y] = filter_z(u, around)

        def beside(y):
            if y < 0:
                second = 0.5 * hp[0]
            elif y >= CY:
                second = 0.5 * hp[CY - 1]
            else:
                sides = [hp[y + d] for d in (-1, 1) if 0 <= y + d < CY]
                second = hp[y] + 0.5 * (sides[0] + sides[1] if len(sides) == 2 else sides[0])
            shear = jnp.where(lanes(1) < 64, scaled(se, 0, y), scaled(se, XQ + 1, y))
            value = roll(-0.5 * (shear * halves(hy[0, y + 1], hy[3, y + 1]) + second), 64)
            minus, plus = jnp.where(low, zero, value), jnp.where(low, value, zero)
            return jnp.concatenate([*split(minus), *split(plus)], axis=0)

        for y4 in range(CY // 4):
            for y in range(4 * y4, 4 * y4 + 4):
                at = 128 * (y - 4 * y4)
                wide[0:128, at : at + 128] = beside(y)
                minus = rows_of(lambda src: xf[0, src, k, y // 2].astype(F32), y % 2)
                plus = rows_of(lambda src: xf[1, src, k, y // 2].astype(F32), y % 2)
                wide[128:160, at : at + 128] = halves(plus, minus).astype(BF16)
            acc_x[...] += dot_nt(wide[0:128, 0:512], wide[128:160, 0:512])
        for j, y, yy in ((0, -1, 1), (1, CY, 0)):
            minus = rows_of(lambda src: cf[j, src, k].astype(F32), yy)
            plus = rows_of(lambda src: cf[2 + j, src, k].astype(F32), yy)
            acc_n[j] += dot_nt(beside(y), halves(plus, minus).astype(BF16))
        return 0

    lax.fori_loop(0, COMPS, component, 0)
    scale = 1.0 / CELLS
    inner = acc_c[0:32, :] + acc_c[32:64, :]
    found = {(1, 1): (inner + inner.T) * scale}
    found[0, 1] = (acc_x[0:32, :] + acc_x[32:64, :]) * (scale * live_x[0])
    found[2, 1] = (acc_x[64:96, :] + acc_x[96:128, :]) * (scale * live_x[1])
    for j in range(2):
        found[1, 2 * j] = (acc_y[j, 0:32, :] + acc_y[j, 32:64, :]) * (scale * live_y[j])
        found[0, 2 * j] = (acc_n[j, 0:32, :] + acc_n[j, 32:64, :]) * (scale * live_x[0] * live_y[j])
        found[2, 2 * j] = (acc_n[j, 64:96, :] + acc_n[j, 96:128, :]) * (scale * live_x[1] * live_y[j])
    out[...] = jnp.zeros_like(out)
    for at, name in enumerate(BLOCKS):
        if name is not None:
            out[:, 32 * at : 32 * at + 32] = found[name]
    for part in range(PARTS):
        @pl.when(g == part)
        def _():
            out[8 * part : 8 * part + 8, 96:128] = rhs[:, 0:32]


def gram(recv, zh, xf, yf, cf, mat, sx, sy, sc, rhs):
    field = (XQ, CY, VECS, 128)
    return pl.pallas_call(
        gram_kernel,
        name="gram",
        out_shape=jax.ShapeDtypeStruct((VECS, 384), F32),
        in_specs=[VMEM] * 10,
        out_specs=VMEM,
        scratch_shapes=[
            pltpu.VMEM((COMPS,) + field, F32),
            pltpu.VMEM(field, F32),
            pltpu.VMEM(field, F32),
            pltpu.VMEM((XQ, CY + 2, VECS, 128), F32),
            pltpu.VMEM((CY, VECS, 128), F32),
            pltpu.VMEM((XQ + 2, 32, 128), F32),
            pltpu.VMEM((XQ + 2, 32, 128), F32),
            pltpu.VMEM((XQ, CY, 128), F32),
            pltpu.VMEM((XQ, CY, 128), F32),
            pltpu.VMEM((32, 128), F32),
            pltpu.VMEM((160, 2048), BF16),
            pltpu.VMEM((64, 32), F32),
            pltpu.VMEM((128, 32), F32),
            pltpu.VMEM((2, 64, 32), F32),
            pltpu.VMEM((2, 128, 32), F32),
        ],
        compiler_params=pltpu.CompilerParams(vmem_limit_bytes=LIMIT),
    )(recv, zh, xf, yf, cf, mat, sx, sy, sc, rhs)


def collect_kernel(part, line, rows, first, second, total, s1, r1, s2, r2, s3, r3, own_sem):
    gx, g = lax.axis_index("gx"), lax.axis_index("grp")
    nx = LINE
    others = [lax.rem(g + d, 4) for d in (1, 3, 2)]
    mates = [lax.rem(gx + d, nx) for d in range(1, nx)]
    barrier = pltpu.get_barrier_semaphore()
    for other in others:
        pl.semaphore_signal(barrier, inc=1, device_id={"grp": other}, device_id_type=MESH)
    for mate in mates:
        pl.semaphore_signal(barrier, inc=1, device_id={"gx": mate}, device_id_type=MESH)
    pl.semaphore_wait(barrier, 3 + nx - 1)
    copies = []
    for i, other in enumerate(others):
        copies.append(pltpu.make_async_remote_copy(
            src_ref=part.at[:, pl.ds(0, 128)], dst_ref=first.at[g], send_sem=s1.at[i], recv_sem=r1.at[i],
            device_id={"grp": other}, device_id_type=MESH))
    for i, other in enumerate(others):
        copies.append(pltpu.make_async_remote_copy(
            src_ref=part.at[pl.ds(pl.multiple_of(8 * other, 8), 8), pl.ds(128, 256)], dst_ref=second.at[g],
            send_sem=s2.at[i], recv_sem=r2.at[i], device_id={"grp": other}, device_id_type=MESH))
    for c in copies:
        c.start()
    first[pl.ds(g, 1)] = part[:, 0:128].reshape(1, VECS, 128)
    second[pl.ds(g, 1)] = part[pl.ds(pl.multiple_of(8 * g, 8), 8), 128:384].reshape(1, 8, 256)
    for c in copies[:3]:
        c.wait_recv()
    total[...] = (first[0] + first[1]) + (first[2] + first[3])
    sends = []
    for i, mate in enumerate(mates):
        c = pltpu.make_async_remote_copy(
            src_ref=total, dst_ref=line.at[gx], send_sem=s3.at[i], recv_sem=r3.at[i],
            device_id={"gx": mate}, device_id_type=MESH)
        c.start()
        sends.append(c)
    line[pl.ds(gx, 1)] = total[...].reshape(1, VECS, 128)
    for c in copies[3:]:
        c.wait_recv()
    rows[:, 0:128] = total[pl.ds(pl.multiple_of(8 * g, 8), 8), :]
    rows[:, 128:384] = (second[0] + second[1]) + (second[2] + second[3])
    for c in sends:
        c.wait_recv()
    for c in copies + sends:
        c.wait_send()


def collect(part):
    return pl.pallas_call(
        collect_kernel,
        name="collect",
        out_shape=(
            jax.ShapeDtypeStruct((LINE, VECS, 128), F32),
            jax.ShapeDtypeStruct((8, 384), F32),
        ),
        in_specs=[VMEM],
        out_specs=[VMEM, VMEM],
        scratch_shapes=[
            pltpu.VMEM((PARTS, VECS, 128), F32),
            pltpu.VMEM((PARTS, 8, 256), F32),
            pltpu.VMEM((VECS, 128), F32),
            pltpu.SemaphoreType.DMA((3,)),
            pltpu.SemaphoreType.DMA((3,)),
            pltpu.SemaphoreType.DMA((3,)),
            pltpu.SemaphoreType.DMA((3,)),
            pltpu.SemaphoreType.DMA((LINE - 1,)),
            pltpu.SemaphoreType.DMA((LINE - 1,)),
            pltpu.SemaphoreType.DMA((1,)),
        ],
        compiler_params=pltpu.CompilerParams(
            vmem_limit_bytes=LIMIT, collective_id=1, has_side_effects=True
        ),
    )(part)


def eliminate(m):
    sub = lax.broadcasted_iota(jnp.int32, m.shape, 1)
    for j in range(VECS):
        column = jnp.broadcast_to(m[:, :, j : j + 1], m.shape)
        pivot = m[:, j : j + 1, :] * (1.0 / column[:, j : j + 1, :])
        m = jnp.where(sub == j, pivot, m - column * pivot)
    return m


def solve_kernel(line, rows, recv, blocks, solved, corr, table, weights, corr_rows):
    lane = lanes(VECS)
    sub = lax.broadcasted_iota(jnp.int32, (VECS, 128), 0)

    def reduce_level(system):
        odd = eliminate(jnp.stack(system[1::2]))
        odd = [odd[i] for i in range(odd.shape[0])]
        rest = []
        for i, m in enumerate(system[0::2]):
            coeff = roll(m, -32)[:, 0:64]
            if i > 0:
                b = odd[i - 1]
                left = jnp.where(lane < 32, roll(b, 64), jnp.where((lane >= 64) & (lane < 96), 0.0, b))
            else:
                left = jnp.zeros((VECS, 128), F32)
            b = odd[i]
            right = jnp.where(lane < 32, roll(b, -32), jnp.where((lane >= 32) & (lane < 64), 0.0, b))
            change = lax.dot_general(
                coeff, jnp.concatenate([left, right], axis=0), (((1,), (0,)), ((), ())),
                precision=lax.Precision.HIGHEST, preferred_element_type=F32)
            rest.append(jnp.where((lane >= 32) & (lane < 96), 0.0, m) - change)
        return odd, rest

    levels = []
    system = [line[a] for a in range(LINE)]
    while len(system) > 1:
        odd, system = reduce_level(system)
        levels.append(odd)
    last = eliminate(system[0][None])[0]

    def spread(column):
        return jnp.broadcast_to(column, (VECS, 128))

    def as_row(full, shift):
        return jnp.sum(jnp.where(lane == sub + shift, full, 0.0), axis=0, keepdims=True)

    values = [spread(last[:, 96:97])]
    for odd in reversed(levels):
        new = []
        for i, m in enumerate(odd):
            row = as_row(values[i], 32)
            if i + 1 < len(values):
                row = row + as_row(values[i + 1], 64)
            picked = jnp.where(lane == 96, m, jnp.where((lane >= 32) & (lane < 96), -m * row, 0.0))
            new.append(spread(jnp.sum(picked, axis=1, keepdims=True)))
        values = [v for pair in zip(values, new) for v in pair]
    for a in range(LINE):
        table[a] = values[a]
        solved[a : a + 1, :] = as_row(values[a], 0)[:, 0:32]

    weights[...] = table[lax.axis_index("gx")]

    def component(k, _):
        for xq in range(XQ):
            for y2 in range(CY // 2):
                even = jnp.zeros((8, 128), F32)
                odd = jnp.zeros((8, 128), F32)
                for src in range(PARTS):
                    v = recv[src, k, xq, y2].astype(F32)
                    w = weights[8 * src : 8 * src + 8, :]
                    even = even + w * v[:8]
                    odd = odd + w * v[8:]
                corr_rows[2 * y2 : 2 * y2 + 1, :] = jnp.sum(even, axis=0, keepdims=True)
                corr_rows[2 * y2 + 1 : 2 * y2 + 2, :] = jnp.sum(odd, axis=0, keepdims=True)
            whole = corr_rows[...]
            corr[k, xq] = whole[:, 0:64]
            corr[k, xq + XQ] = roll(whole, 64)[:, 0:64]
        return 0

    lax.fori_loop(0, COMPS, component, 0)
    for at, name in enumerate(BLOCKS):
        if name is not None:
            blocks[name[0], name[1]] = rows[:, 32 * at : 32 * at + 32]


def solve(line, rows, recv):
    return pl.pallas_call(
        solve_kernel,
        name="solve",
        out_shape=(
            jax.ShapeDtypeStruct((3, 3, OWN, VECS), F32),
            jax.ShapeDtypeStruct((LINE, VECS), F32),
            jax.ShapeDtypeStruct((COMPS, CX, CY, CZ // PARTS), F32),
        ),
        in_specs=[VMEM] * 3,
        out_specs=[VMEM] * 3,
        scratch_shapes=[
            pltpu.VMEM((LINE, VECS, 128), F32),
            pltpu.VMEM((VECS, 128), F32),
            pltpu.VMEM((CY, 128), F32),
        ],
        compiler_params=pltpu.CompilerParams(vmem_limit_bytes=LIMIT),
    )(line, rows, recv)


def on_device(deflation, region, lame_table, residual):
    send, edge, mat, rhs = pack(deflation, region, lame_table, residual)
    recv, zh, xf, yf, cf, sx, sy, sc = exchange(send, edge, mat)
    part = gram(recv, zh, xf, yf, cf, mat, sx, sy, sc, rhs)
    line, rows = collect(part)
    blocks, solved, corr = solve(line, rows, recv)
    return blocks[None, None], solved[:, None, :], corr


def solution(mesh):
    placed = (P("grp", None, "gx", "gy", None), P("gx", "gy", None), P(), P(None, "gx", "gy", None))
    return jax.shard_map(
        on_device,
        mesh=mesh,
        in_specs=placed,
        out_specs=(
            P("gx", "gy", None, None, "grp", None),
            P(None, "gy", None),
            P(None, "gx", "gy", "grp"),
        ),
        check_vma=False,
    )
```

```python
import functools

import jax
import jax.numpy as jnp
from jax import lax
from jax.experimental import pallas as pl
from jax.experimental.pallas import tpu as pltpu
from jax.sharding import PartitionSpec as P

MESH = pl.DeviceIdType.MESH
F32 = jnp.float32
BF16 = jnp.bfloat16
VECS = 32
OWN = 8
PARTS = 4
COMPS = 3
CX = 8
CY = 16
CZ = 256
XQ = 4
REGIONS = 8
LINE = 16
CELLS = COMPS * CX * CY * CZ
RING = (8, 9, 7, 10, 6, 11, 5, 12, 4, 13, 3, 14, 2, 15, 1)
ANY = pl.BlockSpec(memory_space=pl.ANY)
VMEM = pl.BlockSpec(memory_space=pltpu.VMEM)
LIMIT = 60 * 1024 * 1024


def lanes(rows):
    return lax.broadcasted_iota(jnp.int32, (rows, 128), 1)


def roll(x, shift):
    return pltpu.roll(x, shift % 128, x.ndim - 1)


def filter_z(v, edge):
    lane = lanes(v.shape[0]) & 63
    before = jnp.where(lane == 0, edge, roll(v, 1))
    after = jnp.where(lane == 63, edge, roll(v, -1))
    return v + 0.5 * (before + after)


def halves(a, b):
    low = lanes(a.shape[0]) < 64
    return jnp.where(low, a, b)

def split(value):
    high = value.astype(BF16)
    return high, (value - high.astype(F32)).astype(BF16)


def split_rows(value):
    return jnp.concatenate(split(value), axis=0)


def dot_nt(a, b):
    return lax.dot_general(a, b, (((1,), (1,)), ((), ())), preferred_element_type=F32)


def filter_x(b):
    low = lanes(b[0].shape[0]) < 64
    zero = jnp.zeros_like(b[0])
    before = [jnp.where(low, zero, roll(b[3], 64))] + b[:3]
    after = b[1:] + [jnp.where(low, roll(b[0], 64), zero)]
    return [mid + 0.5 * (lo + hi) for mid, lo, hi in zip(b, before, after)]


def fold(a, b):
    low = lanes(a.shape[0]) < 64
    blocks = []
    for t in range(2):
        ta, tb = a[:, 128 * t : 128 * t + 128], b[:, 128 * t : 128 * t + 128]
        blocks.append(jnp.where(low, ta, roll(tb, 64)))
        blocks.append(jnp.where(low, roll(ta, 64), tb))
    return blocks


def fill_order(order):
    r = lax.broadcasted_iota(jnp.int32, (128, 128), 0)
    c = lax.broadcasted_iota(jnp.int32, (128, 128), 1)
    order[...] = jnp.where(c == (r & 7) * 16 + (r >> 3), 1.0, 0.0).astype(BF16)


def pack(k, vec, order, rows, send, edge):
    lane = lanes(8) & 63
    acc = [[jnp.zeros((8, 128), F32) for _ in range(2)] for _ in range(PARTS)]
    for xq in range(XQ):
        for half in range(2):
            plane = vec[:, k, xq + XQ * half].reshape(OWN * CY, CZ)
            rows[half] = jnp.dot(order[...], plane, preferred_element_type=F32)
        for y2 in range(CY // 2):
            both = []
            for yy in range(2):
                y = 2 * y2 + yy
                blocks = fold(rows[0, 8 * y : 8 * y + 8, :], rows[1, 8 * y : 8 * y + 8, :])
                e = 2 * (CY * (xq % 2) + y)
                for g in range(PARTS):
                    value = acc[g][xq // 2]
                    if g > 0:
                        value = jnp.where(lane == e, roll(blocks[g - 1], e + 65), value)
                    if g < PARTS - 1:
                        value = jnp.where(lane == ((e + 63) & 63), roll(blocks[g + 1], e + 63), value)
                    acc[g][xq // 2] = value
                both.append(blocks)
            for g in range(PARTS):
                send[g, k, xq, y2] = jnp.concatenate([both[0][g], both[1][g]], axis=0).astype(BF16)
    for g in range(PARTS):
        edge[g, k] = jnp.concatenate(acc[g], axis=0).astype(BF16)


def material(me, region, lame, mat):
    lane = lanes(CY) & 63
    for xq in range(XQ):
        for which in range(2):
            tiles = []
            for half in range(2):
                kind = region[xq + XQ * half]
                value = jnp.zeros((CY, CZ), F32)
                for label in range(REGIONS):
                    entry = jnp.broadcast_to(lame[which : which + 1, label : label + 1], (CY, CZ))
                    value = jnp.where(kind == label, entry, value)
                tiles.append(value)
            blocks = fold(*tiles)
            own = jnp.zeros((CY, 128), F32)
            rim = jnp.zeros((CY, 128), F32)
            for g in range(PARTS):
                here = jnp.full((CY, 128), me, jnp.int32) == g
                own = jnp.where(here, blocks[g], own)
                if which == 0 and g > 0:
                    rim = jnp.where(here & (lane == 0), roll(blocks[g - 1], 65), rim)
                if which == 0 and g < PARTS - 1:
                    rim = jnp.where(here & (lane == 63), roll(blocks[g + 1], 63), rim)
            if which == 0:
                mat[0, xq] = own
                mat[1, xq] = rim
            else:
                mat[2, xq] = own


def right_side(vec, res, rhs):
    def component(i, totals):
        k, x = i // CX, i % CX
        new = []
        for p in range(OWN):
            value = vec[p, k, x].astype(F32) * res[k, x]
            value = (value[0:8, 0:128] + value[0:8, 128:256]) + (value[8:16, 0:128] + value[8:16, 128:256])
            new.append(totals[p] + value)
        return tuple(new)

    totals = lax.fori_loop(0, COMPS * CX, component, tuple(jnp.zeros((8, 128), F32) for _ in range(OWN)))
    for p in range(OWN):
        value = jnp.sum(jnp.sum(totals[p], axis=0, keepdims=True), axis=1, keepdims=True)
        rhs[p : p + 1, :] = jnp.broadcast_to(value * (1.0 / CELLS), (1, 128))


def coefficients(live_x, live_y, mat, sx, sy, sc, se, sh, db, hb, tmp):
    for target, t in ((se, 0), (sh, 1)):
        target[...] = jnp.zeros_like(target)

        def wider(own, minus, plus):
            return roll(halves(own[3], minus), 64), roll(halves(plus, own[0]), 64)

        own = [mat[t, xq] for xq in range(XQ)]
        first, last = wider(own, sx[0, t] * live_x[0], sx[1, t] * live_x[1])
        for xq, value in enumerate([first] + own + [last]):
            target[xq, 8:24, :] = value
        for j, at, src in ((0, 7, 7), (1, 24, 0)):
            own = [sy[j, t, xq, src : src + 1, :] * live_y[j] for xq in range(XQ)]
            first, last = wider(
                own,
                sc[j, t, src : src + 1, :] * (live_x[0] * live_y[j]),
                sc[2 + j, t, src : src + 1, :] * (live_x[1] * live_y[j]),
            )
            for xq, value in enumerate([first] + own + [last]):
                target[xq, at : at + 1, :] = value
    fz = [filter_z(se[xq], sh[xq]) for xq in range(XQ + 2)]
    for xq in range(XQ):
        tmp[...] = fz[xq + 1] + 0.5 * (fz[xq] + fz[xq + 2])
        smooth = tmp[8:24, :] + 0.5 * (tmp[7:23, :] + tmp[9:25, :])
        bulk = mat[2, xq]
        db[xq] = 0.5 * (0.5 + 8.0 * mat[0, xq] + smooth + bulk)
        hb[xq] = bulk * (1.0 / 6.0)


def rows_of(ref_at, yy):
    return jnp.concatenate([ref_at(src).astype(F32)[8 * yy : 8 * yy + 8] for src in range(PARTS)], axis=0)


def inside(k, recv, zh, zf, zsum, hz, hx, hr, hy, se, db, hb, wide, acc):
    for xq in range(XQ):
        for y2 in range(CY // 2):
            parts = [recv[src, k, xq, y2].astype(F32) for src in range(PARTS)]
            for yy in range(2):
                y = 2 * y2 + yy
                value = jnp.concatenate([p[8 * yy : 8 * yy + 8] for p in parts], axis=0)
                zf[xq, y] = value
                e = 2 * (CY * (xq % 2) + y)
                blocks = [
                    roll(zh[src, k].astype(F32)[8 * (xq // 2) : 8 * (xq // 2) + 8], -e) for src in range(PARTS)
                ]
                around = jnp.concatenate(blocks, axis=0)
                if xq == 0:
                    hx[y] = around
                if y == 0:
                    hr[0, xq] = around
                if y == CY - 1:
                    hr[1, xq] = around
                hz[xq, y] = filter_z(value, around)
    for xq in range(XQ):
        hy[xq, 0] = 0.5 * hz[xq, 0]
        hy[xq, CY + 1] = 0.5 * hz[xq, CY - 1]
        for y in range(CY):
            sides = [hz[xq, y + d] for d in (-1, 1) if 0 <= y + d < CY]
            both = sides[0] + sides[1] if len(sides) == 2 else sides[0]
            hy[xq, y + 1] = hz[xq, y] + 0.5 * both
    for y4 in range(CY // 4):
        for y in range(4 * y4, 4 * y4 + 4):
            smooth = filter_x([hy[xq, y + 1] for xq in range(XQ)])
            for xq in range(XQ):
                v = zf[xq, y]
                before = zsum[xq, y]
                zsum[xq, y] = before + v
                w = db[xq, y : y + 1, :] * v - hb[xq, y : y + 1, :] * (v + 2.0 * before)
                w = w - se[xq + 1, y + 8 : y + 9, :] * smooth[xq]
                high, rest = split(w)
                at = 128 * (XQ * (y - 4 * y4) + xq)
                wide[0:32, at : at + 128] = high
                wide[32:64, at : at + 128] = rest
                wide[64:96, at : at + 128] = v.astype(BF16)
        acc[...] += dot_nt(wide[0:64, :], wide[64:96, :])


def beside(k, zf, hx, hr, hy, hp, se, sh, xf, yf, cf, wide, acc_x, acc_y, acc_n):
    low = lanes(VECS) < 64
    zero = jnp.zeros((VECS, 128), F32)
    smooth = filter_x([hy[xq, 0] for xq in range(XQ)])
    scaled = []
    for xq in range(XQ):
        u = se[xq + 1, 8:9, :] * zf[xq, 0]
        scaled.append(filter_z(u, sh[xq + 1, 8:9, :] * hr[0, xq]))
    scaled = filter_x(scaled)
    left, right = [], []
    for xq in range(XQ):
        left.append(split_rows(-(se[xq + 1, 7:8, :] * smooth[xq] + 0.5 * scaled[xq])))
        right.append(rows_of(lambda src: yf[src, k, xq], 1).astype(BF16))
    acc_y[...] += dot_nt(jnp.concatenate(left, axis=1), jnp.concatenate(right, axis=1))
    for y in range(CY):
        hp[y] = filter_z(se[1, y + 8 : y + 9, :] * zf[0, y], sh[1, y + 8 : y + 9, :] * hx[y])

    def plane(y):
        if y < 0:
            second = 0.5 * hp[0]
        elif y >= CY:
            second = 0.5 * hp[CY - 1]
        else:
            sides = [hp[y + d] for d in (-1, 1) if 0 <= y + d < CY]
            second = hp[y] + 0.5 * (sides[0] + sides[1] if len(sides) == 2 else sides[0])
        value = -0.5 * (se[0, y + 8 : y + 9, :] * hy[0, y + 1] + second)
        return split_rows(jnp.where(low, zero, roll(value, 64)))

    for y in range(CY):
        wide[0:64, 128 * y : 128 * y + 128] = plane(y)
        wide[64:96, 128 * y : 128 * y + 128] = rows_of(lambda src: xf[src, k, y // 2], y % 2).astype(BF16)
    acc_x[...] += dot_nt(wide[0:64, :], wide[64:96, :])
    for j, y, yy in ((0, -1, 1), (1, CY, 0)):
        acc_n[j] += dot_nt(plane(y), rows_of(lambda src: cf[j, src, k], yy).astype(BF16))


SIDES = ((-1, 0), (1, 0), (0, -1), (0, 1), (-1, -1), (-1, 1), (1, -1), (1, 1))
TILE = {-1: 0, 1: 3}
ROW = {-1: 0, 1: 8}


def main_kernel(
    vec_hbm, region_hbm, lame_hbm, res_hbm, keep, line, rows,
    vec, region, lame, res, order, planes, send, edge, mat, rhs, recv, zh, xf, yf, cf, sx, sy, sc, stage,
    zf, zsum, hz, hx, hr, hy, hp, se, sh, db, hb, tmp, wide, acc_c, acc_x, acc_y, acc_n,
    part, first, second, total, corner,
    in_sem, zs, zr, hs, hv, ms, mr, own_sem, keep_sem, s1, r1, s2, r2, s3, r3, s4, r4,
):
    gx, gy, g = lax.axis_index("gx"), lax.axis_index("gy"), lax.axis_index("grp")
    nx, ny = LINE, 4
    up, down, far = lax.rem(g + 1, 4), lax.rem(g + 3, 4), lax.rem(g + 2, 4)
    near = {}
    for dx, dy in SIDES:
        near[dx, dy] = {"gx": lax.rem(gx + dx + nx, nx), "gy": lax.rem(gy + dy + ny, ny)}

    def remote(src, dst, send_sem, recv_sem, device):
        return pltpu.make_async_remote_copy(
            src_ref=src, dst_ref=dst, send_sem=send_sem, recv_sem=recv_sem,
            device_id=device, device_id_type=MESH,
        )

    def load(k):
        return pltpu.make_async_copy(vec_hbm.at[:, k], vec.at[:, k], in_sem.at[k])

    loads = [
        pltpu.make_async_copy(region_hbm, region, in_sem.at[3]),
        pltpu.make_async_copy(lame_hbm, lame, in_sem.at[4]),
        pltpu.make_async_copy(res_hbm, res, in_sem.at[5]),
    ]
    for k in range(COMPS):
        load(k).start()
    for c in loads:
        c.start()
    barrier = pltpu.get_barrier_semaphore()
    for other in (up, down, far):
        pl.semaphore_signal(barrier, inc=1, device_id={"grp": other}, device_id_type=MESH)
    for side in SIDES:
        if side[1] != 0:
            pl.semaphore_signal(barrier, inc=1, device_id=near[side], device_id_type=MESH)
    for d in RING:
        pl.semaphore_signal(barrier, inc=1, device_id={"gx": lax.rem(gx + d, nx)}, device_id_type=MESH)
    fill_order(order)

    def zcopy(src, dst, kind, k, other):
        return remote(src, dst, zs.at[kind, k], zr.at[kind, k], {"grp": other})

    first_two, last_two = pl.ds(0, 2), pl.ds(2, 2)

    def far_up(k):
        return zcopy(send.at[far, k, first_two], stage.at[0, k], 0, k, up)

    def far_down(k):
        return zcopy(send.at[far, k, last_two], stage.at[1, k], 1, k, down)

    def on_up(k):
        return zcopy(stage.at[0, k], recv.at[down, k, first_two], 2, k, up)

    def on_down(k):
        return zcopy(stage.at[1, k], recv.at[up, k, last_two], 3, k, down)

    def near_up(k):
        return zcopy(send.at[up, k], recv.at[g, k], 4, k, up)

    def near_down(k):
        return zcopy(send.at[down, k], recv.at[g, k], 5, k, down)

    def edges(k):
        return [zcopy(edge.at[o, k], zh.at[g, k], 6 + i, k, o) for i, o in enumerate((up, down, far))]

    def own(k):
        return [
            pltpu.make_async_copy(send.at[g, k], recv.at[g, k], own_sem.at[0, k]),
            pltpu.make_async_copy(edge.at[g, k], zh.at[g, k], own_sem.at[1, k]),
        ]

    def start(k):
        for c in [far_up(k), far_down(k), near_up(k), near_down(k)] + edges(k) + own(k):
            c.start()

    load(0).wait()
    pack(0, vec, order, planes, send, edge)
    pl.semaphore_wait(barrier, 3 + 6 + nx - 1)
    start(0)

    def pack_more(k, _):
        load(k).wait()
        pack(k, vec, order, planes, send, edge)
        start(k)
        return 0

    lax.fori_loop(1, COMPS, pack_more, 0)
    for c in loads:
        c.wait()
    material(g, region, lame, mat)
    mats = []

    def mcopy(src, dst, side):
        i = len(mats)
        mats.append(remote(src, dst, ms.at[i], mr.at[i], near[side]))

    for dx in (-1, 1):
        mcopy(mat.at[pl.ds(0, 2), TILE[dx]], sx.at[1 if dx < 0 else 0], (dx, 0))
    for dy in (-1, 1):
        mcopy(mat.at[pl.ds(0, 2), :, pl.ds(ROW[dy], 8)], sy.at[1 if dy < 0 else 0], (0, dy))
    for dx in (-1, 1):
        for dy in (-1, 1):
            slot = (2 if dx < 0 else 0) + (1 if dy < 0 else 0)
            mcopy(mat.at[pl.ds(0, 2), TILE[dx], pl.ds(ROW[dy], 8)], sc.at[slot], (dx, dy))
    for c in mats:
        c.start()
    right_side(vec, res, rhs)
    for c in mats:
        c.wait_recv()
    one = jnp.ones((1, 128), F32)
    none = jnp.zeros((1, 128), F32)
    live_x = (jnp.where(gx > 0, one, none), jnp.where(gx < nx - 1, one, none))
    live_y = (jnp.where(gy > 0, one, none), jnp.where(gy < ny - 1, one, none))
    coefficients(live_x, live_y, mat, sx, sy, sc, se, sh, db, hb, tmp)
    for ref in (zsum, acc_c, acc_x, acc_y, acc_n):
        ref[...] = jnp.zeros_like(ref)

    def rim(k, place, src):
        def hcopy(a, b, i, side):
            return remote(a, b, hs.at[k, 4 * place + i], hv.at[k, 4 * place + i], near[side])

        return [
            hcopy(recv.at[src, k, 3], xf.at[src, k], 0, (1, 0)),
            hcopy(recv.at[src, k, :, 7], yf.at[src, k], 1, (0, 1)),
            hcopy(recv.at[src, k, 3, 7], cf.at[0, src, k], 2, (1, 1)),
            hcopy(recv.at[src, k, 3, 0], cf.at[1, src, k], 3, (1, -1)),
        ]

    def forward(k):
        far_up(k).wait_recv()
        on_up(k).start()
        far_down(k).wait_recv()
        on_down(k).start()

    def start_rim(k, place, src):
        for c in rim(k, place, src):
            c.start()

    places = ((0, g), (1, down), (2, up), (3, far))
    forward(0)

    def component(k, _):
        for c in own(k):
            c.wait()
        start_rim(k, 0, g)
        near_up(k).wait_recv()
        start_rim(k, 1, down)
        near_down(k).wait_recv()
        start_rim(k, 2, up)

        @pl.when(k < COMPS - 1)
        def _():
            forward(k + 1)

        on_up(k).wait_recv()
        on_down(k).wait_recv()
        start_rim(k, 3, far)
        pltpu.make_async_copy(recv.at[:, k], keep.at[:, k], keep_sem.at[k]).start()
        for c in edges(k):
            c.wait_recv()
        inside(k, recv, zh, zf, zsum, hz, hx, hr, hy, se, db, hb, wide, acc_c)
        for place, src in places:
            for c in rim(k, place, src):
                c.wait_recv()
        beside(k, zf, hx, hr, hy, hp, se, sh, xf, yf, cf, wide, acc_x, acc_y, acc_n)
        return 0

    lax.fori_loop(0, COMPS, component, 0)

    scale = 1.0 / CELLS
    inner = acc_c[0:32, :] + acc_c[32:64, :]
    lower = (acc_x[0:32, :] + acc_x[32:64, :]) * (scale * live_x[0][:, 0:32])
    side = (acc_y[0:32, :] + acc_y[32:64, :]) * (scale * live_y[0][:, 0:32])
    part[...] = jnp.zeros_like(part)
    part[:, 0:32] = (inner + inner.T) * scale
    part[:, 32:64] = lower
    part[:, 64:96] = lower.T
    part[:, 128:160] = side
    part[:, 256:288] = side.T
    for j in range(2):
        value = (acc_n[j, 0:32, :] + acc_n[j, 32:64, :]) * (scale * (live_x[0] * live_y[j])[:, 0:32])
        part[:, 160 + 32 * j : 192 + 32 * j] = value
        part[:, 288 + 32 * j : 320 + 32 * j] = value.T
    mine = pl.ds(pl.multiple_of(8 * g, 8), 8)
    part[mine, 96:128] = rhs[:, 0:32]

    sums = []
    for i, other in enumerate((far, up, down)):
        sums.append(remote(part.at[:, pl.ds(0, 128)], first.at[g], s1.at[i], r1.at[i], {"grp": other}))
    for i, other in enumerate((far, up, down)):
        theirs = pl.ds(pl.multiple_of(8 * other, 8), 8)
        sums.append(remote(part.at[theirs, pl.ds(128, 256)], second.at[g], s2.at[i], r2.at[i], {"grp": other}))
    for c in sums:
        c.start()
    first[pl.ds(g, 1)] = part[:, 0:128].reshape(1, VECS, 128)
    second[pl.ds(g, 1)] = part[mine, 128:384].reshape(1, 8, 256)
    for c in sums[:3]:
        c.wait_recv()
    total[...] = (first[0] + first[1]) + (first[2] + first[3])
    sends = []
    for i, d in enumerate(RING):
        c = remote(total, line.at[gx], s3.at[i], r3.at[i], {"gx": lax.rem(gx + d, nx)})
        c.start()
        sends.append(c)
    line[pl.ds(gx, 1)] = total[...].reshape(1, VECS, 128)
    rows[0] = total[mine, :]
    for c in sums[3:]:
        c.wait_recv()
    both = (second[0] + second[1]) + (second[2] + second[3])
    rows[1] = both[:, 0:128]
    corner[...] = both[:, 128:256]
    for i, to in enumerate(((0, -1), (-1, -1), (-1, 1))):
        c = remote(corner, rows.at[2 + i], s4.at[i], r4.at[i], near[to])
        c.start()
        sends.append(c)

    def finish(k, _):
        for c in [far_up(k), far_down(k), on_up(k), on_down(k), near_up(k), near_down(k)] + edges(k):
            c.wait_send()
        for place, src in places:
            for c in rim(k, place, src):
                c.wait_send()
        pltpu.make_async_copy(recv.at[:, k], keep.at[:, k], keep_sem.at[k]).wait()
        return 0

    lax.fori_loop(0, COMPS, finish, 0)
    for c in mats + sums:
        c.wait_send()
    for c in sends:
        c.wait_recv()
    for c in sends:
        c.wait_send()


def main(deflation, region, lame_table, residual):
    field = (XQ, CY, VECS, 128)
    packed = (PARTS, COMPS, XQ, CY // 2, 16, 128)
    dma = pltpu.SemaphoreType.DMA
    return pl.pallas_call(
        main_kernel,
        name="main",
        out_shape=(
            jax.ShapeDtypeStruct(packed, BF16),
            jax.ShapeDtypeStruct((LINE, VECS, 128), F32),
            jax.ShapeDtypeStruct((5, 8, 128), F32),
        ),
        in_specs=[ANY] * 4,
        out_specs=[ANY, VMEM, VMEM],
        scratch_shapes=[
            pltpu.VMEM((OWN, COMPS, CX, CY, CZ), BF16),
            pltpu.VMEM((CX, CY, CZ), jnp.int32),
            pltpu.VMEM((2, REGIONS), F32),
            pltpu.VMEM((COMPS, CX, CY, CZ), F32),
            pltpu.VMEM((128, 128), BF16),
            pltpu.VMEM((2, 128, 256), F32),
            pltpu.VMEM(packed, BF16),
            pltpu.VMEM((PARTS, COMPS, 16, 128), BF16),
            pltpu.VMEM((3, XQ, CY, 128), F32),
            pltpu.VMEM((8, 128), F32),
            pltpu.VMEM(packed, BF16),
            pltpu.VMEM((PARTS, COMPS, 16, 128), BF16),
            pltpu.VMEM((PARTS, COMPS, CY // 2, 16, 128), BF16),
            pltpu.VMEM((PARTS, COMPS, XQ, 16, 128), BF16),
            pltpu.VMEM((2, PARTS, COMPS, 16, 128), BF16),
            pltpu.VMEM((2, 2, CY, 128), F32),
            pltpu.VMEM((2, 2, XQ, 8, 128), F32),
            pltpu.VMEM((4, 2, 8, 128), F32),
            pltpu.VMEM((2, COMPS, 2, CY // 2, 16, 128), BF16),
            pltpu.VMEM(field, F32),
            pltpu.VMEM(field, F32),
            pltpu.VMEM(field, F32),
            pltpu.VMEM((CY, VECS, 128), F32),
            pltpu.VMEM((2, XQ, VECS, 128), F32),
            pltpu.VMEM((XQ, CY + 2, VECS, 128), F32),
            pltpu.VMEM((CY, VECS, 128), F32),
            pltpu.VMEM((XQ + 2, 32, 128), F32),
            pltpu.VMEM((XQ + 2, 32, 128), F32),
            pltpu.VMEM((XQ, CY, 128), F32),
            pltpu.VMEM((XQ, CY, 128), F32),
            pltpu.VMEM((32, 128), F32),
            pltpu.VMEM((96, 2048), BF16),
            pltpu.VMEM((64, 32), F32),
            pltpu.VMEM((64, 32), F32),
            pltpu.VMEM((64, 32), F32),
            pltpu.VMEM((2, 64, 32), F32),
            pltpu.VMEM((VECS, 384), F32),
            pltpu.VMEM((PARTS, VECS, 128), F32),
            pltpu.VMEM((PARTS, 8, 256), F32),
            pltpu.VMEM((VECS, 128), F32),
            pltpu.VMEM((8, 128), F32),
            dma((6,)),
            dma((9, COMPS)),
            dma((9, COMPS)),
            dma((COMPS, 16)),
            dma((COMPS, 16)),
            dma((8,)),
            dma((8,)),
            dma((2, COMPS)),
            dma((COMPS,)),
            dma((3,)),
            dma((3,)),
            dma((3,)),
            dma((3,)),
            dma((LINE - 1,)),
            dma((LINE - 1,)),
            dma((3,)),
            dma((3,)),
        ],
        compiler_params=pltpu.CompilerParams(
            vmem_limit_bytes=LIMIT, collective_id=0, has_side_effects=True
        ),
    )(deflation, region, lame_table, residual)


def eliminate(blocks):
    m = [jnp.stack([b[8 * i : 8 * i + 8] for b in blocks]) for i in range(4)]
    sub = lax.broadcasted_iota(jnp.int32, m[0].shape, 1)

    def take(x, column, j, pivot):
        new = []
        for i in range(4):
            value = x[i] - column[i] * pivot
            new.append(jnp.where(sub == j % 8, pivot, value) if i == j // 8 else value)
        return new

    for start in range(0, VECS, 4):
        columns = [[jnp.broadcast_to(x[:, :, j : j + 1], x.shape) for x in m] for j in range(start, start + 4)]
        for i in range(4):
            j = start + i
            at, row = j // 8, j % 8
            column = columns[i]
            inverse = 1.0 / column[at][:, row : row + 1, :]
            for other in range(i + 1, 4):
                pivot = columns[other][at][:, row : row + 1, :] * inverse
                columns[other] = take(columns[other], column, j, pivot)
            m = take(m, column, j, m[at][:, row : row + 1, :] * inverse)
    return [jnp.concatenate([m[i][b] for i in range(4)], axis=0) for b in range(len(blocks))]


def solve_kernel(line, rows, keep, blocks, solved, corr, recv, table, weights, corr_rows, sem):
    fetch = pltpu.make_async_copy(keep, recv, sem.at[0])
    fetch.start()
    gx, g = lax.axis_index("gx"), lax.axis_index("grp")
    lane = lanes(VECS)
    sub = lax.broadcasted_iota(jnp.int32, (VECS, 128), 0)

    def reduce_level(system):
        odd = eliminate(system[1::2])
        rest = []
        for i, m in enumerate(system[0::2]):
            coeff = roll(m, -32)[:, 0:64]
            if i > 0:
                b = odd[i - 1]
                left = jnp.where(lane < 32, roll(b, 64), jnp.where((lane >= 64) & (lane < 96), 0.0, b))
            else:
                left = jnp.zeros((VECS, 128), F32)
            b = odd[i]
            right = jnp.where(lane < 32, roll(b, -32), jnp.where((lane >= 32) & (lane < 64), 0.0, b))
            change = lax.dot_general(
                coeff, jnp.concatenate([left, right], axis=0), (((1,), (0,)), ((), ())),
                precision=lax.Precision.HIGHEST, preferred_element_type=F32)
            rest.append(jnp.where((lane >= 32) & (lane < 96), 0.0, m) - change)
        return odd, rest

    levels = []
    after = (lane >= 64) & (lane < 96)
    system = [jnp.where(after, line[(a + 1) % LINE], line[a]) for a in range(LINE)]
    while len(system) > 1:
        odd, system = reduce_level(system)
        levels.append(odd)
    last = eliminate(system)[0]

    def spread(column):
        return jnp.broadcast_to(column, (VECS, 128))

    def as_row(full, shift):
        return jnp.sum(jnp.where(lane == sub + shift, full, 0.0), axis=0, keepdims=True)

    values = [spread(last[:, 96:97])]
    for odd in reversed(levels):
        new = []
        for i, m in enumerate(odd):
            row = as_row(values[i], 32)
            if i + 1 < len(values):
                row = row + as_row(values[i + 1], 64)
            picked = jnp.where(lane == 96, m, jnp.where((lane >= 32) & (lane < 96), -m * row, 0.0))
            new.append(spread(jnp.sum(picked, axis=1, keepdims=True)))
        values = [v for pair in zip(values, new) for v in pair]
    for a in range(LINE):
        table[a] = values[a]
        solved[a : a + 1, :] = as_row(values[a], 0)[:, 0:32]

    weights[...] = table[gx]
    fetch.wait()

    def component(k, _):
        for xq in range(XQ):
            for y2 in range(CY // 2):
                even = jnp.zeros((8, 128), F32)
                odd = jnp.zeros((8, 128), F32)
                for src in range(PARTS):
                    v = recv[src, k, xq, y2].astype(F32)
                    w = weights[8 * src : 8 * src + 8, :]
                    even = even + w * v[:8]
                    odd = odd + w * v[8:]
                corr_rows[2 * y2 : 2 * y2 + 1, :] = jnp.sum(even, axis=0, keepdims=True)
                corr_rows[2 * y2 + 1 : 2 * y2 + 2, :] = jnp.sum(odd, axis=0, keepdims=True)
            whole = corr_rows[...]
            corr[k, xq] = whole[:, 0:64]
            corr[k, xq + XQ] = roll(whole, 64)[:, 0:64]
        return 0

    lax.fori_loop(0, COMPS, component, 0)
    mine = pl.ds(pl.multiple_of(8 * g, 8), 8)
    blocks[1, 1] = rows[0, :, 0:32]
    blocks[0, 1] = rows[0, :, 32:64]
    blocks[2, 1] = line[lax.rem(gx + 1, LINE), mine, :][:, 64:96]
    blocks[1, 0] = rows[1, :, 0:32]
    blocks[0, 0] = rows[1, :, 32:64]
    blocks[0, 2] = rows[1, :, 64:96]
    blocks[1, 2] = rows[2, :, 0:32]
    blocks[2, 2] = rows[3, :, 32:64]
    blocks[2, 0] = rows[4, :, 64:96]


def solve(line, rows, keep):
    return pl.pallas_call(
        solve_kernel,
        name="solve",
        out_shape=(
            jax.ShapeDtypeStruct((3, 3, OWN, VECS), F32),
            jax.ShapeDtypeStruct((LINE, VECS), F32),
            jax.ShapeDtypeStruct((COMPS, CX, CY, CZ // PARTS), F32),
        ),
        in_specs=[VMEM, VMEM, ANY],
        out_specs=[VMEM] * 3,
        scratch_shapes=[
            pltpu.VMEM((PARTS, COMPS, XQ, CY // 2, 16, 128), BF16),
            pltpu.VMEM((LINE, VECS, 128), F32),
            pltpu.VMEM((VECS, 128), F32),
            pltpu.VMEM((CY, 128), F32),
            pltpu.SemaphoreType.DMA((1,)),
        ],
        compiler_params=pltpu.CompilerParams(vmem_limit_bytes=LIMIT),
    )(line, rows, keep)


def on_device(deflation, region, lame_table, residual):
    keep, line, rows = main(deflation, region, lame_table.T, residual)
    blocks, solved, corr = solve(line, rows, keep)
    return blocks[None, None], solved[:, None, :], corr


def solution(mesh):
    placed = (P("grp", None, "gx", "gy", None), P("gx", "gy", None), P(), P(None, "gx", "gy", None))
    return jax.shard_map(
        on_device,
        mesh=mesh,
        in_specs=placed,
        out_specs=(
            P("gx", "gy", None, None, "grp", None),
            P(None, "gy", None),
            P(None, "gx", "gy", "grp"),
        ),
        check_vma=False,
    )
```

```python
import functools

import jax
import jax.numpy as jnp
from jax import lax
from jax.experimental import pallas as pl
from jax.experimental.pallas import tpu as pltpu
from jax.sharding import PartitionSpec as P

MESH = pl.DeviceIdType.MESH
F32 = jnp.float32
BF16 = jnp.bfloat16
VECS = 32
OWN = 8
PARTS = 4
COMPS = 3
CX = 8
CY = 16
CZ = 256
XQ = 4
REGIONS = 8
LINE = 16
CELLS = COMPS * CX * CY * CZ
COLUMNS = {8: 4, 4: 8, 2: 16, 1: 16}
RING = (8, 9, 7, 10, 6, 11, 5, 12, 4, 13, 3, 14, 2, 15, 1)
ANY = pl.BlockSpec(memory_space=pl.ANY)
VMEM = pl.BlockSpec(memory_space=pltpu.VMEM)
LIMIT = 60 * 1024 * 1024


def lanes(rows):
    return lax.broadcasted_iota(jnp.int32, (rows, 128), 1)


def roll(x, shift):
    return pltpu.roll(x, shift % 128, x.ndim - 1)


def filter_z(v, edge):
    lane = lanes(v.shape[0]) & 63
    before = jnp.where(lane == 0, edge, roll(v, 1))
    after = jnp.where(lane == 63, edge, roll(v, -1))
    return v + 0.5 * (before + after)


def halves(a, b):
    low = lanes(a.shape[0]) < 64
    return jnp.where(low, a, b)

def split(value):
    high = value.astype(BF16)
    return high, (value - high.astype(F32)).astype(BF16)


def split_rows(value):
    return jnp.concatenate(split(value), axis=0)


def dot_nt(a, b):
    return lax.dot_general(a, b, (((1,), (1,)), ((), ())), preferred_element_type=F32)


def filter_x(b):
    low = lanes(b[0].shape[0]) < 64
    zero = jnp.zeros_like(b[0])
    before = [jnp.where(low, zero, roll(b[3], 64))] + b[:3]
    after = b[1:] + [jnp.where(low, roll(b[0], 64), zero)]
    return [mid + 0.5 * (lo + hi) for mid, lo, hi in zip(b, before, after)]


def fold(a, b):
    low = lanes(a.shape[0]) < 64
    blocks = []
    for t in range(2):
        ta, tb = a[:, 128 * t : 128 * t + 128], b[:, 128 * t : 128 * t + 128]
        blocks.append(jnp.where(low, ta, roll(tb, 64)))
        blocks.append(jnp.where(low, roll(ta, 64), tb))
    return blocks


def fill_order(order):
    r = lax.broadcasted_iota(jnp.int32, (128, 128), 0)
    c = lax.broadcasted_iota(jnp.int32, (128, 128), 1)
    order[...] = jnp.where(c == (r & 7) * 16 + (r >> 3), 1.0, 0.0).astype(BF16)


def pack(k, vec, order, rows, send, edge):
    lane = lanes(8) & 63
    acc = [[jnp.zeros((8, 128), F32) for _ in range(2)] for _ in range(PARTS)]
    for xq in range(XQ):
        for half in range(2):
            plane = vec[:, k, xq + XQ * half].reshape(OWN * CY, CZ)
            rows[half] = jnp.dot(order[...], plane, preferred_element_type=F32)
        for y2 in range(CY // 2):
            both = []
            for yy in range(2):
                y = 2 * y2 + yy
                blocks = fold(rows[0, 8 * y : 8 * y + 8, :], rows[1, 8 * y : 8 * y + 8, :])
                e = 2 * (CY * (xq % 2) + y)
                for g in range(PARTS):
                    value = acc[g][xq // 2]
                    if g > 0:
                        value = jnp.where(lane == e, roll(blocks[g - 1], e + 65), value)
                    if g < PARTS - 1:
                        value = jnp.where(lane == ((e + 63) & 63), roll(blocks[g + 1], e + 63), value)
                    acc[g][xq // 2] = value
                both.append(blocks)
            for g in range(PARTS):
                send[g, k, xq, y2] = jnp.concatenate([both[0][g], both[1][g]], axis=0).astype(BF16)
    for g in range(PARTS):
        edge[g, k] = jnp.concatenate(acc[g], axis=0).astype(BF16)


def material(me, region, lame, mat):
    lane = lanes(CY) & 63
    for xq in range(XQ):
        for which in range(2):
            tiles = []
            for half in range(2):
                kind = region[xq + XQ * half]
                value = jnp.zeros((CY, CZ), F32)
                for label in range(REGIONS):
                    entry = jnp.broadcast_to(lame[which : which + 1, label : label + 1], (CY, CZ))
                    value = jnp.where(kind == label, entry, value)
                tiles.append(value)
            blocks = fold(*tiles)
            own = jnp.zeros((CY, 128), F32)
            rim = jnp.zeros((CY, 128), F32)
            for g in range(PARTS):
                here = jnp.full((CY, 128), me, jnp.int32) == g
                own = jnp.where(here, blocks[g], own)
                if which == 0 and g > 0:
                    rim = jnp.where(here & (lane == 0), roll(blocks[g - 1], 65), rim)
                if which == 0 and g < PARTS - 1:
                    rim = jnp.where(here & (lane == 63), roll(blocks[g + 1], 63), rim)
            if which == 0:
                mat[0, xq] = own
                mat[1, xq] = rim
            else:
                mat[2, xq] = own


def right_side(vec, res, rhs):
    def component(i, totals):
        k, x = i // CX, i % CX
        new = []
        for p in range(OWN):
            value = vec[p, k, x].astype(F32) * res[k, x]
            value = (value[0:8, 0:128] + value[0:8, 128:256]) + (value[8:16, 0:128] + value[8:16, 128:256])
            new.append(totals[p] + value)
        return tuple(new)

    totals = lax.fori_loop(0, COMPS * CX, component, tuple(jnp.zeros((8, 128), F32) for _ in range(OWN)))
    for p in range(OWN):
        value = jnp.sum(jnp.sum(totals[p], axis=0, keepdims=True), axis=1, keepdims=True)
        rhs[p : p + 1, :] = jnp.broadcast_to(value * (1.0 / CELLS), (1, 128))


def coefficients(live_x, live_y, mat, sx, sy, sc, se, sh, db, hb, tmp):
    for target, t in ((se, 0), (sh, 1)):
        target[...] = jnp.zeros_like(target)

        def wider(own, minus, plus):
            return roll(halves(own[3], minus), 64), roll(halves(plus, own[0]), 64)

        own = [mat[t, xq] for xq in range(XQ)]
        first, last = wider(own, sx[0, t] * live_x[0], sx[1, t] * live_x[1])
        for xq, value in enumerate([first] + own + [last]):
            target[xq, 8:24, :] = value
        for j, at, src in ((0, 7, 7), (1, 24, 0)):
            own = [sy[j, t, xq, src : src + 1, :] * live_y[j] for xq in range(XQ)]
            first, last = wider(
                own,
                sc[j, t, src : src + 1, :] * (live_x[0] * live_y[j]),
                sc[2 + j, t, src : src + 1, :] * (live_x[1] * live_y[j]),
            )
            for xq, value in enumerate([first] + own + [last]):
                target[xq, at : at + 1, :] = value
    fz = [filter_z(se[xq], sh[xq]) for xq in range(XQ + 2)]
    for xq in range(XQ):
        tmp[...] = fz[xq + 1] + 0.5 * (fz[xq] + fz[xq + 2])
        smooth = tmp[8:24, :] + 0.5 * (tmp[7:23, :] + tmp[9:25, :])
        bulk = mat[2, xq]
        db[xq] = 0.5 * (0.5 + 8.0 * mat[0, xq] + smooth + bulk)
        hb[xq] = bulk * (1.0 / 6.0)


def rows_of(ref_at, yy):
    return jnp.concatenate([ref_at(src).astype(F32)[8 * yy : 8 * yy + 8] for src in range(PARTS)], axis=0)


def prepare(k, xqs, recv, zh, zf, hz, hx, hr, hy):
    for xq in xqs:
        for y2 in range(CY // 2):
            parts = [recv[src, k, xq, y2].astype(F32) for src in range(PARTS)]
            for yy in range(2):
                y = 2 * y2 + yy
                value = jnp.concatenate([p[8 * yy : 8 * yy + 8] for p in parts], axis=0)
                zf[xq, y] = value
                e = 2 * (CY * (xq % 2) + y)
                blocks = [
                    roll(zh[src, k].astype(F32)[8 * (xq // 2) : 8 * (xq // 2) + 8], -e) for src in range(PARTS)
                ]
                around = jnp.concatenate(blocks, axis=0)
                if xq == 0:
                    hx[y] = around
                if y == 0:
                    hr[xq] = around
                hz[xq, y] = filter_z(value, around)
    for xq in xqs:
        hy[xq, 0] = 0.5 * hz[xq, 0]
        hy[xq, CY + 1] = 0.5 * hz[xq, CY - 1]
        for y in range(CY):
            sides = [hz[xq, y + d] for d in (-1, 1) if 0 <= y + d < CY]
            both = sides[0] + sides[1] if len(sides) == 2 else sides[0]
            hy[xq, y + 1] = hz[xq, y] + 0.5 * both


def combine(zf, zsum, hy, se, db, hb, wide, acc):
    for y4 in range(CY // 4):
        for y in range(4 * y4, 4 * y4 + 4):
            smooth = filter_x([hy[xq, y + 1] for xq in range(XQ)])
            for xq in range(XQ):
                v = zf[xq, y]
                before = zsum[xq, y]
                zsum[xq, y] = before + v
                w = db[xq, y : y + 1, :] * v - hb[xq, y : y + 1, :] * (v + 2.0 * before)
                w = w - se[xq + 1, y + 8 : y + 9, :] * smooth[xq]
                high, rest = split(w)
                at = 128 * (XQ * (y - 4 * y4) + xq)
                wide[0:32, at : at + 128] = high
                wide[32:64, at : at + 128] = rest
                wide[64:96, at : at + 128] = v.astype(BF16)
        acc[...] += dot_nt(wide[0:64, :], wide[64:96, :])


def row_before(k, zf, hr, hy, se, sh, ly):
    smooth = filter_x([hy[xq, 0] for xq in range(XQ)])
    scaled = []
    for xq in range(XQ):
        u = se[xq + 1, 8:9, :] * zf[xq, 0]
        scaled.append(filter_z(u, sh[xq + 1, 8:9, :] * hr[xq]))
    scaled = filter_x(scaled)
    for xq in range(XQ):
        ly[k, :, 128 * xq : 128 * xq + 128] = split_rows(-(se[xq + 1, 7:8, :] * smooth[xq] + 0.5 * scaled[xq]))


def plane_before(k, zf, hx, hy, hp, se, sh, lx, lc):
    low = lanes(VECS) < 64
    zero = jnp.zeros((VECS, 128), F32)
    for y in range(CY):
        hp[y] = filter_z(se[1, y + 8 : y + 9, :] * zf[0, y], sh[1, y + 8 : y + 9, :] * hx[y])

    def plane(y):
        if y < 0:
            second = 0.5 * hp[0]
        elif y >= CY:
            second = 0.5 * hp[CY - 1]
        else:
            sides = [hp[y + d] for d in (-1, 1) if 0 <= y + d < CY]
            second = hp[y] + 0.5 * (sides[0] + sides[1] if len(sides) == 2 else sides[0])
        return -0.5 * (se[0, y + 8 : y + 9, :] * hy[0, y + 1] + second)

    for y in range(CY // 2):
        lx[k, :, 128 * y : 128 * y + 128] = split_rows(jnp.where(low, plane(y), roll(plane(y + CY // 2), 64)))
    lc[k, 0] = split_rows(jnp.where(low, zero, roll(plane(-1), 64)))
    lc[k, 1] = split_rows(jnp.where(low, plane(CY), zero))


def both_parts(value):
    return value[0:32, :] + value[32:64, :]


def plane_products(lx, xf):
    def component(k, total):
        right = [rows_of(lambda src: xf[k, src, y // 2], y % 2).astype(BF16) for y in range(CY // 2)]
        return total + dot_nt(lx[k], jnp.concatenate(right, axis=1))

    return both_parts(lax.fori_loop(0, COMPS, component, jnp.zeros((64, 32), F32)))


def other_products(ly, lc, yf, cf):
    def component(k, sums):
        right = [rows_of(lambda src: yf[k, src, xq // 2], xq % 2).astype(BF16) for xq in range(XQ)]
        new = [dot_nt(ly[k], jnp.concatenate(right, axis=1))]
        for j, yy in ((0, 1), (1, 0)):
            new.append(dot_nt(lc[k, j], rows_of(lambda src: cf[j, k, src], yy).astype(BF16)))
        return tuple(a + b for a, b in zip(sums, new))

    sums = lax.fori_loop(0, COMPS, component, tuple(jnp.zeros((64, 32), F32) for _ in range(3)))
    return [both_parts(v) for v in sums]


def pack_plane(k, recv, xs):
    low = lanes(16) < 64
    for src in range(PARTS):
        for j in range(CY // 4):
            a = recv[src, k, 3, j].astype(F32)
            b = recv[src, k, 3, j + CY // 4].astype(F32)
            xs[k, src, j] = jnp.where(low, roll(a, 64), b).astype(BF16)


def pack_row(k, recv, ys):
    for src in range(PARTS):
        for j in range(XQ // 2):
            pair = [recv[src, k, 2 * j + i, CY // 2 - 1].astype(F32)[8:16] for i in range(2)]
            ys[k, src, j] = jnp.concatenate(pair, axis=0).astype(BF16)


SIDES = ((-1, 0), (1, 0), (0, -1), (0, 1), (-1, -1), (-1, 1), (1, -1), (1, 1))
TILE = {-1: 0, 1: 3}
ROW = {-1: 0, 1: 8}


def main_kernel(
    vec_hbm, region_hbm, lame_hbm, res_hbm, keep, line, rows,
    vec, region, lame, res, order, planes, send, edge, mat, rhs, recv, zh, xf, yf, cf, sx, sy, sc, xs, ys,
    zf, zsum, hz, hx, hr, hy, hp, se, sh, db, hb, tmp, wide, acc_c, lx, ly, lc,
    part, rest, first_in, second_in, total, corner,
    in_sem, zs, zr, hs, hv, ms, mr, own_sem, keep_sem, s1, r1, s2, r2, s3, r3, s4, r4,
):
    gx, gy, g = lax.axis_index("gx"), lax.axis_index("gy"), lax.axis_index("grp")
    nx, ny = LINE, 4
    up, down, far = lax.rem(g + 1, 4), lax.rem(g + 3, 4), lax.rem(g + 2, 4)
    near = {}
    for dx, dy in SIDES:
        near[dx, dy] = {"gx": lax.rem(gx + dx + nx, nx), "gy": lax.rem(gy + dy + ny, ny)}

    def remote(src, dst, send_sem, recv_sem, device):
        return pltpu.make_async_remote_copy(
            src_ref=src, dst_ref=dst, send_sem=send_sem, recv_sem=recv_sem,
            device_id=device, device_id_type=MESH,
        )

    def load(k):
        return pltpu.make_async_copy(vec_hbm.at[:, k], vec.at[:, k], in_sem.at[k])

    loads = [
        pltpu.make_async_copy(region_hbm, region, in_sem.at[3]),
        pltpu.make_async_copy(lame_hbm, lame, in_sem.at[4]),
        pltpu.make_async_copy(res_hbm, res, in_sem.at[5]),
    ]
    for k in range(COMPS):
        load(k).start()
    for c in loads:
        c.start()
    barrier = pltpu.get_barrier_semaphore()
    for other in (up, down, far):
        pl.semaphore_signal(barrier, inc=1, device_id={"grp": other}, device_id_type=MESH)
    for side in SIDES:
        if side[1] != 0:
            pl.semaphore_signal(barrier, inc=1, device_id=near[side], device_id_type=MESH)
    for d in RING:
        pl.semaphore_signal(barrier, inc=1, device_id={"gx": lax.rem(gx + d, nx)}, device_id_type=MESH)
    fill_order(order)

    def zcopy(src, dst, kind, k, other):
        return remote(src, dst, zs.at[kind, k], zr.at[kind, k], {"grp": other})

    def ahead(k):
        last = pl.ds(XQ - 1, 1)
        return [zcopy(send.at[o, k, last], recv.at[g, k, last], i, k, o) for i, o in enumerate((far, up, down))]

    def second(k):
        part = pl.ds(0, 2)
        return [zcopy(send.at[o, k, part], recv.at[g, k, part], 3 + i, k, o) for i, o in enumerate((far, up, down))]

    def third(k):
        part = pl.ds(2, 1)
        return [zcopy(send.at[o, k, part], recv.at[g, k, part], 9 + i, k, o) for i, o in enumerate((far, up, down))]

    def edges(k):
        return [zcopy(edge.at[o, k], zh.at[g, k], 6 + i, k, o) for i, o in enumerate((far, up, down))]

    def own(k):
        return [
            pltpu.make_async_copy(send.at[g, k], recv.at[g, k], own_sem.at[0, k]),
            pltpu.make_async_copy(edge.at[g, k], zh.at[g, k], own_sem.at[1, k]),
        ]

    def start(copies):
        for c in copies:
            c.start()

    load(0).wait()
    pack(0, vec, order, planes, send, edge)
    pl.semaphore_wait(barrier, 3 + 6 + nx - 1)
    start(ahead(0) + edges(0) + second(0) + third(0) + own(0))

    def pack_more(k, _):
        load(k).wait()
        pack(k, vec, order, planes, send, edge)
        start(ahead(k) + edges(k) + own(k))
        return 0

    lax.fori_loop(1, COMPS, pack_more, 0)
    for c in loads:
        c.wait()
    material(g, region, lame, mat)
    mats = []

    def mcopy(src, dst, side):
        i = len(mats)
        mats.append(remote(src, dst, ms.at[i], mr.at[i], near[side]))

    for dx in (-1, 1):
        mcopy(mat.at[pl.ds(0, 2), TILE[dx]], sx.at[1 if dx < 0 else 0], (dx, 0))
    for dy in (-1, 1):
        mcopy(mat.at[pl.ds(0, 2), :, pl.ds(ROW[dy], 8)], sy.at[1 if dy < 0 else 0], (0, dy))
    for dx in (-1, 1):
        for dy in (-1, 1):
            slot = (2 if dx < 0 else 0) + (1 if dy < 0 else 0)
            mcopy(mat.at[pl.ds(0, 2), TILE[dx], pl.ds(ROW[dy], 8)], sc.at[slot], (dx, dy))
    for c in mats:
        c.start()
    right_side(vec, res, rhs)
    for c in mats:
        c.wait_recv()
    one = jnp.ones((1, 128), F32)
    none = jnp.zeros((1, 128), F32)
    live_x = (jnp.where(gx > 0, one, none), jnp.where(gx < nx - 1, one, none))
    live_y = (jnp.where(gy > 0, one, none), jnp.where(gy < ny - 1, one, none))
    coefficients(live_x, live_y, mat, sx, sy, sc, se, sh, db, hb, tmp)
    for ref in (zsum, acc_c):
        ref[...] = jnp.zeros_like(ref)

    def hcopy(a, b, i, k, side):
        return remote(a, b, hs.at[k, i], hv.at[k, i], near[side])

    def early(k):
        return [hcopy(xs.at[k], xf.at[k], 0, k, (1, 0))]

    def corners(k):
        return [
            hcopy(xf.at[k, :, 3], cf.at[0, k], 1, k, (0, 1)),
            hcopy(xf.at[k, :, 0], cf.at[1, k], 2, k, (0, -1)),
        ]

    def late(k):
        return [hcopy(ys.at[k], yf.at[k], 3, k, (0, 1))]

    def planes_first(k, _):
        for c in own(k):
            c.wait()
        for c in ahead(k):
            c.wait_recv()
        pack_plane(k, recv, xs)
        start(early(k))
        return 0

    planes_first(0, 0)

    def component(k, _):
        for c in second(k) + edges(k):
            c.wait_recv()
        prepare(k, (3, 0, 1), recv, zh, zf, hz, hx, hr, hy)
        plane_before(k, zf, hx, hy, hp, se, sh, lx, lc)

        @pl.when(k == 0)
        def _():
            start(second(1))
            lax.fori_loop(1, COMPS, planes_first, 0)
            start(third(1) + second(2) + third(2))

        @pl.when(k == 1)
        def _():
            for i in range(COMPS):
                early(i)[0].wait_recv()
                start(corners(i))

        for c in third(k):
            c.wait_recv()
        pack_row(k, recv, ys)
        start(late(k))
        pltpu.make_async_copy(recv.at[:, k], keep.at[:, k], keep_sem.at[k]).start()
        prepare(k, (2,), recv, zh, zf, hz, hx, hr, hy)
        combine(zf, zsum, hy, se, db, hb, wide, acc_c)

        @pl.when(k < COMPS - 1)
        def _():
            row_before(k, zf, hr, hy, se, sh, ly)

        return 0

    lax.fori_loop(0, COMPS, component, 0)

    scale = 1.0 / CELLS
    inner = both_parts(acc_c[...])
    lower = plane_products(lx, xf) * (scale * live_x[0][:, 0:32])
    part[...] = jnp.zeros_like(part)
    part[:, 0:32] = (inner + inner.T) * scale
    part[:, 32:64] = lower
    part[:, 64:96] = lower.T
    mine = pl.ds(pl.multiple_of(8 * g, 8), 8)
    part[mine, 96:128] = rhs[:, 0:32]

    sums = []
    for i, other in enumerate((far, up, down)):
        sums.append(remote(part, first_in.at[g], s1.at[i], r1.at[i], {"grp": other}))
    start(sums)
    row_before(COMPS - 1, zf, hr, hy, se, sh, ly)
    for k in range(COMPS):
        for c in corners(k) + late(k):
            c.wait_recv()
    side, *diagonal = other_products(ly, lc, yf, cf)
    side = side * (scale * live_y[0][:, 0:32])
    rest[...] = jnp.zeros_like(rest)
    rest[:, 0:32] = side
    rest[:, 128:160] = side.T
    for j in range(2):
        value = diagonal[j] * (scale * (live_x[0] * live_y[j])[:, 0:32])
        rest[:, 32 + 32 * j : 64 + 32 * j] = value
        rest[:, 160 + 32 * j : 192 + 32 * j] = value.T
    for i, other in enumerate((far, up, down)):
        theirs = pl.ds(pl.multiple_of(8 * other, 8), 8)
        sums.append(remote(rest.at[theirs], second_in.at[g], s2.at[i], r2.at[i], {"grp": other}))
    first_in[pl.ds(g, 1)] = part[...].reshape(1, VECS, 128)
    second_in[pl.ds(g, 1)] = rest[mine, :].reshape(1, 8, 256)
    for c in sums[:3]:
        c.wait_recv()
    total[...] = (first_in[0] + first_in[1]) + (first_in[2] + first_in[3])
    sends = []
    for i, d in enumerate(RING):
        c = remote(total, line.at[gx], s3.at[i], r3.at[i], {"gx": lax.rem(gx + d, nx)})
        c.start()
        sends.append(c)
    start(sums[3:])
    line[pl.ds(gx, 1)] = total[...].reshape(1, VECS, 128)
    rows[0] = total[mine, :]
    for c in sums[3:]:
        c.wait_recv()
    both = (second_in[0] + second_in[1]) + (second_in[2] + second_in[3])
    rows[1] = both[:, 0:128]
    corner[...] = both[:, 128:256]
    for i, to in enumerate(((0, -1), (-1, -1), (-1, 1))):
        c = remote(corner, rows.at[2 + i], s4.at[i], r4.at[i], near[to])
        c.start()
        sends.append(c)

    def finish(k, _):
        for c in ahead(k) + second(k) + third(k) + edges(k) + early(k) + corners(k) + late(k):
            c.wait_send()
        pltpu.make_async_copy(recv.at[:, k], keep.at[:, k], keep_sem.at[k]).wait()
        return 0

    lax.fori_loop(0, COMPS, finish, 0)
    for c in mats + sums:
        c.wait_send()
    for c in sends:
        c.wait_recv()
    for c in sends:
        c.wait_send()


def main(deflation, region, lame_table, residual):
    field = (XQ, CY, VECS, 128)
    packed = (PARTS, COMPS, XQ, CY // 2, 16, 128)
    dma = pltpu.SemaphoreType.DMA
    return pl.pallas_call(
        main_kernel,
        name="main",
        out_shape=(
            jax.ShapeDtypeStruct(packed, BF16),
            jax.ShapeDtypeStruct((LINE, VECS, 128), F32),
            jax.ShapeDtypeStruct((5, 8, 128), F32),
        ),
        in_specs=[ANY] * 4,
        out_specs=[ANY, VMEM, VMEM],
        scratch_shapes=[
            pltpu.VMEM((OWN, COMPS, CX, CY, CZ), BF16),
            pltpu.VMEM((CX, CY, CZ), jnp.int32),
            pltpu.VMEM((2, REGIONS), F32),
            pltpu.VMEM((COMPS, CX, CY, CZ), F32),
            pltpu.VMEM((128, 128), BF16),
            pltpu.VMEM((2, 128, 256), F32),
            pltpu.VMEM(packed, BF16),
            pltpu.VMEM((PARTS, COMPS, 16, 128), BF16),
            pltpu.VMEM((3, XQ, CY, 128), F32),
            pltpu.VMEM((8, 128), F32),
            pltpu.VMEM(packed, BF16),
            pltpu.VMEM((PARTS, COMPS, 16, 128), BF16),
            pltpu.VMEM((COMPS, PARTS, CY // 4, 16, 128), BF16),
            pltpu.VMEM((COMPS, PARTS, XQ // 2, 16, 128), BF16),
            pltpu.VMEM((2, COMPS, PARTS, 16, 128), BF16),
            pltpu.VMEM((2, 2, CY, 128), F32),
            pltpu.VMEM((2, 2, XQ, 8, 128), F32),
            pltpu.VMEM((4, 2, 8, 128), F32),
            pltpu.VMEM((COMPS, PARTS, CY // 4, 16, 128), BF16),
            pltpu.VMEM((COMPS, PARTS, XQ // 2, 16, 128), BF16),
            pltpu.VMEM(field, F32),
            pltpu.VMEM(field, F32),
            pltpu.VMEM(field, F32),
            pltpu.VMEM((CY, VECS, 128), F32),
            pltpu.VMEM((XQ, VECS, 128), F32),
            pltpu.VMEM((XQ, CY + 2, VECS, 128), F32),
            pltpu.VMEM((CY, VECS, 128), F32),
            pltpu.VMEM((XQ + 2, 32, 128), F32),
            pltpu.VMEM((XQ + 2, 32, 128), F32),
            pltpu.VMEM((XQ, CY, 128), F32),
            pltpu.VMEM((XQ, CY, 128), F32),
            pltpu.VMEM((32, 128), F32),
            pltpu.VMEM((96, 2048), BF16),
            pltpu.VMEM((64, 32), F32),
            pltpu.VMEM((COMPS, 64, 1024), BF16),
            pltpu.VMEM((COMPS, 64, 512), BF16),
            pltpu.VMEM((COMPS, 2, 64, 128), BF16),
            pltpu.VMEM((VECS, 128), F32),
            pltpu.VMEM((VECS, 256), F32),
            pltpu.VMEM((PARTS, VECS, 128), F32),
            pltpu.VMEM((PARTS, 8, 256), F32),
            pltpu.VMEM((VECS, 128), F32),
            pltpu.VMEM((8, 128), F32),
            dma((6,)),
            dma((12, COMPS)),
            dma((12, COMPS)),
            dma((COMPS, 4)),
            dma((COMPS, 4)),
            dma((8,)),
            dma((8,)),
            dma((2, COMPS)),
            dma((COMPS,)),
            dma((3,)),
            dma((3,)),
            dma((3,)),
            dma((3,)),
            dma((LINE - 1,)),
            dma((LINE - 1,)),
            dma((3,)),
            dma((3,)),
        ],
        compiler_params=pltpu.CompilerParams(
            vmem_limit_bytes=LIMIT, collective_id=0, has_side_effects=True
        ),
    )(deflation, region, lame_table, residual)


def eliminate(blocks):
    step = COLUMNS[len(blocks)]
    m = [jnp.stack([b[8 * i : 8 * i + 8] for b in blocks]) for i in range(4)]
    sub = lax.broadcasted_iota(jnp.int32, m[0].shape, 1)

    def take(x, column, j, pivot):
        new = []
        for i in range(4):
            value = x[i] - column[i] * pivot
            new.append(jnp.where(sub == j % 8, pivot, value) if i == j // 8 else value)
        return new

    for start in range(0, VECS, step):
        columns = [[jnp.broadcast_to(x[:, :, j : j + 1], x.shape) for x in m] for j in range(start, start + step)]
        for i in range(step):
            j = start + i
            at, row = j // 8, j % 8
            column = columns[i]
            inverse = 1.0 / column[at][:, row : row + 1, :]
            for other in range(i + 1, step):
                pivot = columns[other][at][:, row : row + 1, :] * inverse
                columns[other] = take(columns[other], column, j, pivot)
            m = take(m, column, j, m[at][:, row : row + 1, :] * inverse)
    return [jnp.concatenate([m[i][b] for i in range(4)], axis=0) for b in range(len(blocks))]


def solve_kernel(line, rows, keep, blocks, solved, corr, recv, table, weights, corr_rows, sem):
    fetch = pltpu.make_async_copy(keep, recv, sem.at[0])
    fetch.start()
    gx, g = lax.axis_index("gx"), lax.axis_index("grp")
    lane = lanes(VECS)
    sub = lax.broadcasted_iota(jnp.int32, (VECS, 128), 0)

    def reduce_level(system):
        odd = eliminate(system[1::2])
        rest = []
        for i, m in enumerate(system[0::2]):
            coeff = roll(m, -32)[:, 0:64]
            if i > 0:
                b = odd[i - 1]
                left = jnp.where(lane < 32, roll(b, 64), jnp.where((lane >= 64) & (lane < 96), 0.0, b))
            else:
                left = jnp.zeros((VECS, 128), F32)
            b = odd[i]
            right = jnp.where(lane < 32, roll(b, -32), jnp.where((lane >= 32) & (lane < 64), 0.0, b))
            change = lax.dot_general(
                coeff, jnp.concatenate([left, right], axis=0), (((1,), (0,)), ((), ())),
                precision=lax.Precision.HIGHEST, preferred_element_type=F32)
            rest.append(jnp.where((lane >= 32) & (lane < 96), 0.0, m) - change)
        return odd, rest

    levels = []
    after = (lane >= 64) & (lane < 96)
    system = [jnp.where(after, line[(a + 1) % LINE], line[a]) for a in range(LINE)]
    while len(system) > 1:
        odd, system = reduce_level(system)
        levels.append(odd)
    last = eliminate(system)[0]

    def spread(column):
        return jnp.broadcast_to(column, (VECS, 128))

    def as_row(full, shift):
        return jnp.sum(jnp.where(lane == sub + shift, full, 0.0), axis=0, keepdims=True)

    values = [spread(last[:, 96:97])]
    for odd in reversed(levels):
        new = []
        for i, m in enumerate(odd):
            row = as_row(values[i], 32)
            if i + 1 < len(values):
                row = row + as_row(values[i + 1], 64)
            picked = jnp.where(lane == 96, m, jnp.where((lane >= 32) & (lane < 96), -m * row, 0.0))
            new.append(spread(jnp.sum(picked, axis=1, keepdims=True)))
        values = [v for pair in zip(values, new) for v in pair]
    for a in range(LINE):
        table[a] = values[a]
        solved[a : a + 1, :] = as_row(values[a], 0)[:, 0:32]

    weights[...] = table[gx]
    fetch.wait()

    def component(k, _):
        for xq in range(XQ):
            for y2 in range(CY // 2):
                even = jnp.zeros((8, 128), F32)
                odd = jnp.zeros((8, 128), F32)
                for src in range(PARTS):
                    v = recv[src, k, xq, y2].astype(F32)
                    w = weights[8 * src : 8 * src + 8, :]
                    even = even + w * v[:8]
                    odd = odd + w * v[8:]
                corr_rows[2 * y2 : 2 * y2 + 1, :] = jnp.sum(even, axis=0, keepdims=True)
                corr_rows[2 * y2 + 1 : 2 * y2 + 2, :] = jnp.sum(odd, axis=0, keepdims=True)
            whole = corr_rows[...]
            corr[k, xq] = whole[:, 0:64]
            corr[k, xq + XQ] = roll(whole, 64)[:, 0:64]
        return 0

    lax.fori_loop(0, COMPS, component, 0)
    mine = pl.ds(pl.multiple_of(8 * g, 8), 8)
    blocks[1, 1] = rows[0, :, 0:32]
    blocks[0, 1] = rows[0, :, 32:64]
    blocks[2, 1] = line[lax.rem(gx + 1, LINE), mine, :][:, 64:96]
    blocks[1, 0] = rows[1, :, 0:32]
    blocks[0, 0] = rows[1, :, 32:64]
    blocks[0, 2] = rows[1, :, 64:96]
    blocks[1, 2] = rows[2, :, 0:32]
    blocks[2, 2] = rows[3, :, 32:64]
    blocks[2, 0] = rows[4, :, 64:96]


def solve(line, rows, keep):
    return pl.pallas_call(
        solve_kernel,
        name="solve",
        out_shape=(
            jax.ShapeDtypeStruct((3, 3, OWN, VECS), F32),
            jax.ShapeDtypeStruct((LINE, VECS), F32),
            jax.ShapeDtypeStruct((COMPS, CX, CY, CZ // PARTS), F32),
        ),
        in_specs=[VMEM, VMEM, ANY],
        out_specs=[VMEM] * 3,
        scratch_shapes=[
            pltpu.VMEM((PARTS, COMPS, XQ, CY // 2, 16, 128), BF16),
            pltpu.VMEM((LINE, VECS, 128), F32),
            pltpu.VMEM((VECS, 128), F32),
            pltpu.VMEM((CY, 128), F32),
            pltpu.SemaphoreType.DMA((1,)),
        ],
        compiler_params=pltpu.CompilerParams(vmem_limit_bytes=LIMIT),
    )(line, rows, keep)


def on_device(deflation, region, lame_table, residual):
    keep, line, rows = main(deflation, region, lame_table.T, residual)
    blocks, solved, corr = solve(line, rows, keep)
    return blocks[None, None], solved[:, None, :], corr


def solution(mesh):
    placed = (P("grp", None, "gx", "gy", None), P("gx", "gy", None), P(), P(None, "gx", "gy", None))
    return jax.shard_map(
        on_device,
        mesh=mesh,
        in_specs=placed,
        out_specs=(
            P("gx", "gy", None, None, "grp", None),
            P(None, "gy", None),
            P(None, "gx", "gy", "grp"),
        ),
        check_vma=False,
    )
```

```python
import functools

import jax
import jax.numpy as jnp
from jax import lax
from jax.experimental import pallas as pl
from jax.experimental.pallas import tpu as pltpu
from jax.sharding import PartitionSpec as P

MESH = pl.DeviceIdType.MESH
F32 = jnp.float32
BF16 = jnp.bfloat16
VECS = 32
OWN = 8
PARTS = 4
COMPS = 3
CX = 8
CY = 16
CZ = 256
XQ = 4
REGIONS = 8
LINE = 16
CELLS = COMPS * CX * CY * CZ
COLUMNS = {8: 4, 4: 8, 2: 16, 1: 16}
RING = (8, 9, 7, 10, 6, 11, 5, 12, 4, 13, 3, 14, 2, 15, 1)
ANY = pl.BlockSpec(memory_space=pl.ANY)
VMEM = pl.BlockSpec(memory_space=pltpu.VMEM)
LIMIT = 60 * 1024 * 1024


def lanes(rows):
    return lax.broadcasted_iota(jnp.int32, (rows, 128), 1)


def roll(x, shift):
    return pltpu.roll(x, shift % 128, x.ndim - 1)


def filter_z(v, edge):
    lane = lanes(v.shape[0]) & 63
    before = jnp.where(lane == 0, edge, roll(v, 1))
    after = jnp.where(lane == 63, edge, roll(v, -1))
    return v + 0.5 * (before + after)


def halves(a, b):
    low = lanes(a.shape[0]) < 64
    return jnp.where(low, a, b)

def split(value):
    high = value.astype(BF16)
    return high, (value - high.astype(F32)).astype(BF16)


def split_rows(value):
    return jnp.concatenate(split(value), axis=0)


def dot_nt(a, b):
    return lax.dot_general(a, b, (((1,), (1,)), ((), ())), preferred_element_type=F32)


def filter_x(b):
    low = lanes(b[0].shape[0]) < 64
    zero = jnp.zeros_like(b[0])
    before = [jnp.where(low, zero, roll(b[3], 64))] + b[:3]
    after = b[1:] + [jnp.where(low, roll(b[0], 64), zero)]
    return [mid + 0.5 * (lo + hi) for mid, lo, hi in zip(b, before, after)]


def fold(a, b):
    low = lanes(a.shape[0]) < 64
    blocks = []
    for t in range(2):
        ta, tb = a[:, 128 * t : 128 * t + 128], b[:, 128 * t : 128 * t + 128]
        blocks.append(jnp.where(low, ta, roll(tb, 64)))
        blocks.append(jnp.where(low, roll(ta, 64), tb))
    return blocks


def fill_order(order):
    r = lax.broadcasted_iota(jnp.int32, (128, 128), 0)
    c = lax.broadcasted_iota(jnp.int32, (128, 128), 1)
    order[...] = jnp.where(c == (r & 7) * 16 + (r >> 3), 1.0, 0.0).astype(BF16)


def pack(k, vec, order, rows, send, edge):
    lane = lanes(8) & 63
    acc = [[jnp.zeros((8, 128), F32) for _ in range(2)] for _ in range(PARTS)]
    for xq in range(XQ):
        for half in range(2):
            plane = vec[:, k, xq + XQ * half].reshape(OWN * CY, CZ)
            rows[half] = jnp.dot(order[...], plane, preferred_element_type=F32)
        for y2 in range(CY // 2):
            both = []
            for yy in range(2):
                y = 2 * y2 + yy
                blocks = fold(rows[0, 8 * y : 8 * y + 8, :], rows[1, 8 * y : 8 * y + 8, :])
                e = 2 * (CY * (xq % 2) + y)
                for g in range(PARTS):
                    value = acc[g][xq // 2]
                    if g > 0:
                        value = jnp.where(lane == e, roll(blocks[g - 1], e + 65), value)
                    if g < PARTS - 1:
                        value = jnp.where(lane == ((e + 63) & 63), roll(blocks[g + 1], e + 63), value)
                    acc[g][xq // 2] = value
                both.append(blocks)
            for g in range(PARTS):
                send[g, k, xq, y2] = jnp.concatenate([both[0][g], both[1][g]], axis=0).astype(BF16)
    for g in range(PARTS):
        edge[g, k] = jnp.concatenate(acc[g], axis=0).astype(BF16)


def material(me, region, lame, mat):
    lane = lanes(CY) & 63
    for xq in range(XQ):
        for which in range(2):
            tiles = []
            for half in range(2):
                kind = region[xq + XQ * half]
                value = jnp.zeros((CY, CZ), F32)
                for label in range(REGIONS):
                    entry = jnp.broadcast_to(lame[which : which + 1, label : label + 1], (CY, CZ))
                    value = jnp.where(kind == label, entry, value)
                tiles.append(value)
            blocks = fold(*tiles)
            own = jnp.zeros((CY, 128), F32)
            rim = jnp.zeros((CY, 128), F32)
            for g in range(PARTS):
                here = jnp.full((CY, 128), me, jnp.int32) == g
                own = jnp.where(here, blocks[g], own)
                if which == 0 and g > 0:
                    rim = jnp.where(here & (lane == 0), roll(blocks[g - 1], 65), rim)
                if which == 0 and g < PARTS - 1:
                    rim = jnp.where(here & (lane == 63), roll(blocks[g + 1], 63), rim)
            if which == 0:
                mat[0, xq] = own
                mat[1, xq] = rim
            else:
                mat[2, xq] = own


def right_side(vec, res, rhs):
    def component(i, totals):
        k, x = i // CX, i % CX
        new = []
        for p in range(OWN):
            value = vec[p, k, x].astype(F32) * res[k, x]
            value = (value[0:8, 0:128] + value[0:8, 128:256]) + (value[8:16, 0:128] + value[8:16, 128:256])
            new.append(totals[p] + value)
        return tuple(new)

    totals = lax.fori_loop(0, COMPS * CX, component, tuple(jnp.zeros((8, 128), F32) for _ in range(OWN)))
    for p in range(OWN):
        value = jnp.sum(jnp.sum(totals[p], axis=0, keepdims=True), axis=1, keepdims=True)
        rhs[p : p + 1, :] = jnp.broadcast_to(value * (1.0 / CELLS), (1, 128))


def coefficients(live_x, live_y, mat, sx, sy, sc, se, sh, db, hb, tmp):
    for target, t in ((se, 0), (sh, 1)):
        target[...] = jnp.zeros_like(target)

        def wider(own, minus, plus):
            return roll(halves(own[3], minus), 64), roll(halves(plus, own[0]), 64)

        own = [mat[t, xq] for xq in range(XQ)]
        first, last = wider(own, sx[0, t] * live_x[0], sx[1, t] * live_x[1])
        for xq, value in enumerate([first] + own + [last]):
            target[xq, 8:24, :] = value
        for j, at, src in ((0, 7, 7), (1, 24, 0)):
            own = [sy[j, t, xq, src : src + 1, :] * live_y[j] for xq in range(XQ)]
            first, last = wider(
                own,
                sc[j, t, src : src + 1, :] * (live_x[0] * live_y[j]),
                sc[2 + j, t, src : src + 1, :] * (live_x[1] * live_y[j]),
            )
            for xq, value in enumerate([first] + own + [last]):
                target[xq, at : at + 1, :] = value
    fz = [filter_z(se[xq], sh[xq]) for xq in range(XQ + 2)]
    for xq in range(XQ):
        tmp[...] = fz[xq + 1] + 0.5 * (fz[xq] + fz[xq + 2])
        smooth = tmp[8:24, :] + 0.5 * (tmp[7:23, :] + tmp[9:25, :])
        bulk = mat[2, xq]
        db[xq] = 0.5 * (0.5 + 8.0 * mat[0, xq] + smooth + bulk)
        hb[xq] = bulk * (1.0 / 6.0)


def rows_of(ref_at, yy):
    return jnp.concatenate([ref_at(src).astype(F32)[8 * yy : 8 * yy + 8] for src in range(PARTS)], axis=0)


def prepare(k, xqs, recv, zh, zf, hz, hx, hr, hy):
    for xq in xqs:
        for y2 in range(CY // 2):
            parts = [recv[src, k, xq, y2].astype(F32) for src in range(PARTS)]
            for yy in range(2):
                y = 2 * y2 + yy
                value = jnp.concatenate([p[8 * yy : 8 * yy + 8] for p in parts], axis=0)
                zf[xq, y] = value
                e = 2 * (CY * (xq % 2) + y)
                blocks = [
                    roll(zh[src, k].astype(F32)[8 * (xq // 2) : 8 * (xq // 2) + 8], -e) for src in range(PARTS)
                ]
                around = jnp.concatenate(blocks, axis=0)
                if xq == 0:
                    hx[y] = around
                if y == 0:
                    hr[xq] = around
                hz[xq, y] = filter_z(value, around)
    for xq in xqs:
        hy[xq, 0] = 0.5 * hz[xq, 0]
        hy[xq, CY + 1] = 0.5 * hz[xq, CY - 1]
        for y in range(CY):
            sides = [hz[xq, y + d] for d in (-1, 1) if 0 <= y + d < CY]
            both = sides[0] + sides[1] if len(sides) == 2 else sides[0]
            hy[xq, y + 1] = hz[xq, y] + 0.5 * both


def combine(zf, zsum, hy, se, db, hb, wide, acc):
    for y4 in range(CY // 4):
        for y in range(4 * y4, 4 * y4 + 4):
            smooth = filter_x([hy[xq, y + 1] for xq in range(XQ)])
            for xq in range(XQ):
                v = zf[xq, y]
                before = zsum[xq, y]
                zsum[xq, y] = before + v
                w = db[xq, y : y + 1, :] * v - hb[xq, y : y + 1, :] * (v + 2.0 * before)
                w = w - se[xq + 1, y + 8 : y + 9, :] * smooth[xq]
                high, rest = split(w)
                at = 128 * (XQ * (y - 4 * y4) + xq)
                wide[0:32, at : at + 128] = high
                wide[32:64, at : at + 128] = rest
                wide[64:96, at : at + 128] = v.astype(BF16)
        acc[...] += dot_nt(wide[0:64, :], wide[64:96, :])


def row_before(k, zf, hr, hy, se, sh, ly):
    smooth = filter_x([hy[xq, 0] for xq in range(XQ)])
    scaled = []
    for xq in range(XQ):
        u = se[xq + 1, 8:9, :] * zf[xq, 0]
        scaled.append(filter_z(u, sh[xq + 1, 8:9, :] * hr[xq]))
    scaled = filter_x(scaled)
    for xq in range(XQ):
        ly[k, :, 128 * xq : 128 * xq + 128] = split_rows(-(se[xq + 1, 7:8, :] * smooth[xq] + 0.5 * scaled[xq]))


def plane_before(k, zf, hx, hy, hp, se, sh, lx, lc):
    low = lanes(VECS) < 64
    zero = jnp.zeros((VECS, 128), F32)
    for y in range(CY):
        hp[y] = filter_z(se[1, y + 8 : y + 9, :] * zf[0, y], sh[1, y + 8 : y + 9, :] * hx[y])

    def plane(y):
        if y < 0:
            second = 0.5 * hp[0]
        elif y >= CY:
            second = 0.5 * hp[CY - 1]
        else:
            sides = [hp[y + d] for d in (-1, 1) if 0 <= y + d < CY]
            second = hp[y] + 0.5 * (sides[0] + sides[1] if len(sides) == 2 else sides[0])
        return -0.5 * (se[0, y + 8 : y + 9, :] * hy[0, y + 1] + second)

    for y in range(CY // 2):
        lx[k, :, 128 * y : 128 * y + 128] = split_rows(jnp.where(low, plane(y), roll(plane(y + CY // 2), 64)))
    lc[k, 0] = split_rows(jnp.where(low, zero, roll(plane(-1), 64)))
    lc[k, 1] = split_rows(jnp.where(low, plane(CY), zero))


def both_parts(value):
    return value[0:32, :] + value[32:64, :]


def plane_products(lx, xf):
    def component(k, total):
        right = [rows_of(lambda src: xf[k, src, y // 2], y % 2).astype(BF16) for y in range(CY // 2)]
        return total + dot_nt(lx[k], jnp.concatenate(right, axis=1))

    return both_parts(lax.fori_loop(0, COMPS, component, jnp.zeros((64, 32), F32)))


def other_products(ly, lc, yf, cf):
    def component(k, sums):
        right = [rows_of(lambda src: yf[k, src, xq // 2], xq % 2).astype(BF16) for xq in range(XQ)]
        new = [dot_nt(ly[k], jnp.concatenate(right, axis=1))]
        for j, yy in ((0, 1), (1, 0)):
            new.append(dot_nt(lc[k, j], rows_of(lambda src: cf[j, k, src], yy).astype(BF16)))
        return tuple(a + b for a, b in zip(sums, new))

    sums = lax.fori_loop(0, COMPS, component, tuple(jnp.zeros((64, 32), F32) for _ in range(3)))
    return [both_parts(v) for v in sums]


def pack_plane(k, recv, xs):
    low = lanes(16) < 64
    for src in range(PARTS):
        for j in range(CY // 4):
            a = recv[src, k, 3, j].astype(F32)
            b = recv[src, k, 3, j + CY // 4].astype(F32)
            xs[k, src, j] = jnp.where(low, roll(a, 64), b).astype(BF16)


def pack_row(k, recv, ys):
    for src in range(PARTS):
        for j in range(XQ // 2):
            pair = [recv[src, k, 2 * j + i, CY // 2 - 1].astype(F32)[8:16] for i in range(2)]
            ys[k, src, j] = jnp.concatenate(pair, axis=0).astype(BF16)


SIDES = ((-1, 0), (1, 0), (0, -1), (0, 1), (-1, -1), (-1, 1), (1, -1), (1, 1))
TILE = {-1: 0, 1: 3}
ROW = {-1: 0, 1: 8}


def main_kernel(
    vec_hbm, region_hbm, lame_hbm, res_hbm, keep, line, rows,
    vec, region, lame, res, order, planes, send, edge, mat, rhs, recv, zh, xf, yf, cf, sx, sy, sc, xs, ys,
    zf, zsum, hz, hx, hr, hy, hp, se, sh, db, hb, tmp, wide, acc_c, lx, ly, lc,
    part, rest, first_in, second_in, total, corner,
    in_sem, zs, zr, hs, hv, ms, mr, own_sem, keep_sem, s1, r1, s2, r2, s3, r3, s4, r4,
):
    gx, gy, g = lax.axis_index("gx"), lax.axis_index("gy"), lax.axis_index("grp")
    nx, ny = LINE, 4
    up, down, far = lax.rem(g + 1, 4), lax.rem(g + 3, 4), lax.rem(g + 2, 4)
    near = {}
    for dx, dy in SIDES:
        near[dx, dy] = {"gx": lax.rem(gx + dx + nx, nx), "gy": lax.rem(gy + dy + ny, ny)}

    def remote(src, dst, send_sem, recv_sem, device):
        return pltpu.make_async_remote_copy(
            src_ref=src, dst_ref=dst, send_sem=send_sem, recv_sem=recv_sem,
            device_id=device, device_id_type=MESH,
        )

    barrier = pltpu.get_barrier_semaphore()
    for other in (far, up, down):
        pl.semaphore_signal(barrier, inc=1, device_id={"grp": other}, device_id_type=MESH)
    for side in SIDES:
        if side[1] != 0:
            pl.semaphore_signal(barrier, inc=1, device_id=near[side], device_id_type=MESH)
    for d in RING:
        pl.semaphore_signal(barrier, inc=1, device_id={"gx": lax.rem(gx + d, nx)}, device_id_type=MESH)

    def load(k):
        return pltpu.make_async_copy(vec_hbm.at[:, k], vec.at[:, k], in_sem.at[k])

    loads = [
        pltpu.make_async_copy(region_hbm, region, in_sem.at[3]),
        pltpu.make_async_copy(lame_hbm, lame, in_sem.at[4]),
        pltpu.make_async_copy(res_hbm, res, in_sem.at[5]),
    ]
    for k in range(COMPS):
        load(k).start()
    for c in loads:
        c.start()
    fill_order(order)

    def zcopy(src, dst, kind, k, other):
        return remote(src, dst, zs.at[kind, k], zr.at[kind, k], {"grp": other})

    def ahead(k):
        last = pl.ds(XQ - 1, 1)
        return [zcopy(send.at[o, k, last], recv.at[g, k, last], i, k, o) for i, o in enumerate((far, up, down))]

    def second(k):
        part = pl.ds(0, 2)
        return [zcopy(send.at[o, k, part], recv.at[g, k, part], 3 + i, k, o) for i, o in enumerate((far, up, down))]

    def third(k):
        part = pl.ds(2, 1)
        return [zcopy(send.at[o, k, part], recv.at[g, k, part], 9 + i, k, o) for i, o in enumerate((far, up, down))]

    def edges(k):
        return [zcopy(edge.at[o, k], zh.at[g, k], 6 + i, k, o) for i, o in enumerate((far, up, down))]

    def own(k):
        return [
            pltpu.make_async_copy(send.at[g, k], recv.at[g, k], own_sem.at[0, k]),
            pltpu.make_async_copy(edge.at[g, k], zh.at[g, k], own_sem.at[1, k]),
        ]

    def start(copies):
        for c in copies:
            c.start()

    load(0).wait()
    pack(0, vec, order, planes, send, edge)
    pl.semaphore_wait(barrier, 3 + 6 + nx - 1)
    start(ahead(0) + edges(0) + second(0) + third(0) + own(0))

    def pack_more(k, _):
        load(k).wait()
        pack(k, vec, order, planes, send, edge)
        start(ahead(k) + edges(k) + own(k))
        return 0

    lax.fori_loop(1, COMPS, pack_more, 0)
    for c in loads:
        c.wait()
    material(g, region, lame, mat)
    mats = []

    def mcopy(src, dst, side):
        i = len(mats)
        mats.append(remote(src, dst, ms.at[i], mr.at[i], near[side]))

    for dx in (-1, 1):
        mcopy(mat.at[pl.ds(0, 2), TILE[dx]], sx.at[1 if dx < 0 else 0], (dx, 0))
    for dy in (-1, 1):
        mcopy(mat.at[pl.ds(0, 2), :, pl.ds(ROW[dy], 8)], sy.at[1 if dy < 0 else 0], (0, dy))
    for dx in (-1, 1):
        for dy in (-1, 1):
            slot = (2 if dx < 0 else 0) + (1 if dy < 0 else 0)
            mcopy(mat.at[pl.ds(0, 2), TILE[dx], pl.ds(ROW[dy], 8)], sc.at[slot], (dx, dy))
    for c in mats:
        c.start()
    right_side(vec, res, rhs)
    for c in mats:
        c.wait_recv()
    one = jnp.ones((1, 128), F32)
    none = jnp.zeros((1, 128), F32)
    live_x = (jnp.where(gx > 0, one, none), jnp.where(gx < nx - 1, one, none))
    live_y = (jnp.where(gy > 0, one, none), jnp.where(gy < ny - 1, one, none))
    coefficients(live_x, live_y, mat, sx, sy, sc, se, sh, db, hb, tmp)
    for ref in (zsum, acc_c):
        ref[...] = jnp.zeros_like(ref)

    def hcopy(a, b, i, k, side):
        return remote(a, b, hs.at[k, i], hv.at[k, i], near[side])

    def early(k):
        return [hcopy(xs.at[k], xf.at[k], 0, k, (1, 0))]

    def corners(k):
        return [
            hcopy(xf.at[k, :, 3], cf.at[0, k], 1, k, (0, 1)),
            hcopy(xf.at[k, :, 0], cf.at[1, k], 2, k, (0, -1)),
        ]

    def late(k):
        return [hcopy(ys.at[k], yf.at[k], 3, k, (0, 1))]

    def planes_first(k, _):
        for c in own(k):
            c.wait()
        for c in ahead(k):
            c.wait_recv()
        pack_plane(k, recv, xs)
        start(early(k))
        return 0

    scale = 1.0 / CELLS
    mine = pl.ds(pl.multiple_of(8 * g, 8), 8)
    planes_first(0, 0)

    def component(k, _):
        for c in second(k) + edges(k):
            c.wait_recv()
        prepare(k, (3, 0, 1), recv, zh, zf, hz, hx, hr, hy)
        plane_before(k, zf, hx, hy, hp, se, sh, lx, lc)

        @pl.when(k == 0)
        def _():
            start(second(1))
            lax.fori_loop(1, COMPS, planes_first, 0)
            start(third(1) + second(2) + third(2))

        @pl.when(k == 1)
        def _():
            for i in range(COMPS):
                early(i)[0].wait_recv()
                start(corners(i))

        @pl.when(k == COMPS - 1)
        def _():
            lower = plane_products(lx, xf) * (scale * live_x[0][:, 0:32])
            part[...] = jnp.zeros_like(part)
            part[:, 32:64] = lower
            part[:, 64:96] = lower.T
            part[mine, 96:128] = rhs[:, 0:32]

        for c in third(k):
            c.wait_recv()
        pack_row(k, recv, ys)
        start(late(k))
        pltpu.make_async_copy(recv.at[:, k], keep.at[:, k], keep_sem.at[k]).start()
        prepare(k, (2,), recv, zh, zf, hz, hx, hr, hy)
        combine(zf, zsum, hy, se, db, hb, wide, acc_c)

        @pl.when(k < COMPS - 1)
        def _():
            row_before(k, zf, hr, hy, se, sh, ly)

        return 0

    lax.fori_loop(0, COMPS, component, 0)

    inner = both_parts(acc_c[...])
    part[:, 0:32] = (inner + inner.T) * scale

    sums = []
    for i, other in enumerate((far, up, down)):
        sums.append(remote(part, first_in.at[g], s1.at[i], r1.at[i], {"grp": other}))
    start(sums)
    row_before(COMPS - 1, zf, hr, hy, se, sh, ly)
    for k in range(COMPS):
        for c in corners(k) + late(k):
            c.wait_recv()
    side, *diagonal = other_products(ly, lc, yf, cf)
    side = side * (scale * live_y[0][:, 0:32])
    rest[...] = jnp.zeros_like(rest)
    rest[:, 0:32] = side
    rest[:, 128:160] = side.T
    for j in range(2):
        value = diagonal[j] * (scale * (live_x[0] * live_y[j])[:, 0:32])
        rest[:, 32 + 32 * j : 64 + 32 * j] = value
        rest[:, 160 + 32 * j : 192 + 32 * j] = value.T
    for i, other in enumerate((far, up, down)):
        theirs = pl.ds(pl.multiple_of(8 * other, 8), 8)
        sums.append(remote(rest.at[theirs], second_in.at[g], s2.at[i], r2.at[i], {"grp": other}))
    start(sums[3:])
    first_in[pl.ds(g, 1)] = part[...].reshape(1, VECS, 128)
    second_in[pl.ds(g, 1)] = rest[mine, :].reshape(1, 8, 256)
    for c in sums[:3]:
        c.wait_recv()
    total[...] = (first_in[0] + first_in[1]) + (first_in[2] + first_in[3])
    sends = []
    for i, d in enumerate(RING):
        c = remote(total, line.at[gx], s3.at[i], r3.at[i], {"gx": lax.rem(gx + d, nx)})
        c.start()
        sends.append(c)
    line[pl.ds(gx, 1)] = total[...].reshape(1, VECS, 128)
    rows[0] = total[mine, :]
    for c in sums[3:]:
        c.wait_recv()
    both = (second_in[0] + second_in[1]) + (second_in[2] + second_in[3])
    rows[1] = both[:, 0:128]
    corner[...] = both[:, 128:256]
    for i, to in enumerate(((0, -1), (-1, -1), (-1, 1))):
        c = remote(corner, rows.at[2 + i], s4.at[i], r4.at[i], near[to])
        c.start()
        sends.append(c)

    def finish(k, _):
        for c in ahead(k) + second(k) + third(k) + edges(k) + early(k) + corners(k) + late(k):
            c.wait_send()
        pltpu.make_async_copy(recv.at[:, k], keep.at[:, k], keep_sem.at[k]).wait()
        return 0

    lax.fori_loop(0, COMPS, finish, 0)
    for c in mats + sums:
        c.wait_send()
    for c in sends:
        c.wait_recv()
    for c in sends:
        c.wait_send()


def main(deflation, region, lame_table, residual):
    field = (XQ, CY, VECS, 128)
    packed = (PARTS, COMPS, XQ, CY // 2, 16, 128)
    dma = pltpu.SemaphoreType.DMA
    return pl.pallas_call(
        main_kernel,
        name="main",
        out_shape=(
            jax.ShapeDtypeStruct(packed, BF16),
            jax.ShapeDtypeStruct((LINE, VECS, 128), F32),
            jax.ShapeDtypeStruct((5, 8, 128), F32),
        ),
        in_specs=[ANY] * 4,
        out_specs=[ANY, VMEM, VMEM],
        scratch_shapes=[
            pltpu.VMEM((OWN, COMPS, CX, CY, CZ), BF16),
            pltpu.VMEM((CX, CY, CZ), jnp.int32),
            pltpu.VMEM((2, REGIONS), F32),
            pltpu.VMEM((COMPS, CX, CY, CZ), F32),
            pltpu.VMEM((128, 128), BF16),
            pltpu.VMEM((2, 128, 256), F32),
            pltpu.VMEM(packed, BF16),
            pltpu.VMEM((PARTS, COMPS, 16, 128), BF16),
            pltpu.VMEM((3, XQ, CY, 128), F32),
            pltpu.VMEM((8, 128), F32),
            pltpu.VMEM(packed, BF16),
            pltpu.VMEM((PARTS, COMPS, 16, 128), BF16),
            pltpu.VMEM((COMPS, PARTS, CY // 4, 16, 128), BF16),
            pltpu.VMEM((COMPS, PARTS, XQ // 2, 16, 128), BF16),
            pltpu.VMEM((2, COMPS, PARTS, 16, 128), BF16),
            pltpu.VMEM((2, 2, CY, 128), F32),
            pltpu.VMEM((2, 2, XQ, 8, 128), F32),
            pltpu.VMEM((4, 2, 8, 128), F32),
            pltpu.VMEM((COMPS, PARTS, CY // 4, 16, 128), BF16),
            pltpu.VMEM((COMPS, PARTS, XQ // 2, 16, 128), BF16),
            pltpu.VMEM(field, F32),
            pltpu.VMEM(field, F32),
            pltpu.VMEM(field, F32),
            pltpu.VMEM((CY, VECS, 128), F32),
            pltpu.VMEM((XQ, VECS, 128), F32),
            pltpu.VMEM((XQ, CY + 2, VECS, 128), F32),
            pltpu.VMEM((CY, VECS, 128), F32),
            pltpu.VMEM((XQ + 2, 32, 128), F32),
            pltpu.VMEM((XQ + 2, 32, 128), F32),
            pltpu.VMEM((XQ, CY, 128), F32),
            pltpu.VMEM((XQ, CY, 128), F32),
            pltpu.VMEM((32, 128), F32),
            pltpu.VMEM((96, 2048), BF16),
            pltpu.VMEM((64, 32), F32),
            pltpu.VMEM((COMPS, 64, 1024), BF16),
            pltpu.VMEM((COMPS, 64, 512), BF16),
            pltpu.VMEM((COMPS, 2, 64, 128), BF16),
            pltpu.VMEM((VECS, 128), F32),
            pltpu.VMEM((VECS, 256), F32),
            pltpu.VMEM((PARTS, VECS, 128), F32),
            pltpu.VMEM((PARTS, 8, 256), F32),
            pltpu.VMEM((VECS, 128), F32),
            pltpu.VMEM((8, 128), F32),
            dma((6,)),
            dma((12, COMPS)),
            dma((12, COMPS)),
            dma((COMPS, 4)),
            dma((COMPS, 4)),
            dma((8,)),
            dma((8,)),
            dma((2, COMPS)),
            dma((COMPS,)),
            dma((3,)),
            dma((3,)),
            dma((3,)),
            dma((3,)),
            dma((LINE - 1,)),
            dma((LINE - 1,)),
            dma((3,)),
            dma((3,)),
        ],
        compiler_params=pltpu.CompilerParams(
            vmem_limit_bytes=LIMIT, collective_id=0, has_side_effects=True
        ),
    )(deflation, region, lame_table, residual)


def eliminate(blocks):
    step = COLUMNS[len(blocks)]
    m = [jnp.stack([b[8 * i : 8 * i + 8] for b in blocks]) for i in range(4)]
    sub = lax.broadcasted_iota(jnp.int32, m[0].shape, 1)

    def take(x, column, j, pivot):
        new = []
        for i in range(4):
            value = x[i] - column[i] * pivot
            new.append(jnp.where(sub == j % 8, pivot, value) if i == j // 8 else value)
        return new

    for start in range(0, VECS, step):
        columns = [[jnp.broadcast_to(x[:, :, j : j + 1], x.shape) for x in m] for j in range(start, start + step)]
        for i in range(step):
            j = start + i
            at, row = j // 8, j % 8
            column = columns[i]
            inverse = 1.0 / column[at][:, row : row + 1, :]
            for other in range(i + 1, step):
                pivot = columns[other][at][:, row : row + 1, :] * inverse
                columns[other] = take(columns[other], column, j, pivot)
            m = take(m, column, j, m[at][:, row : row + 1, :] * inverse)
    return [jnp.concatenate([m[i][b] for i in range(4)], axis=0) for b in range(len(blocks))]


def solve_kernel(line, rows, keep, blocks, solved, corr, recv, table, weights, corr_rows, sem):
    fetch = pltpu.make_async_copy(keep, recv, sem.at[0])
    fetch.start()
    gx, g = lax.axis_index("gx"), lax.axis_index("grp")
    lane = lanes(VECS)
    sub = lax.broadcasted_iota(jnp.int32, (VECS, 128), 0)

    def reduce_level(system):
        odd = eliminate(system[1::2])
        rest = []
        for i, m in enumerate(system[0::2]):
            coeff = roll(m, -32)[:, 0:64]
            if i > 0:
                b = odd[i - 1]
                left = jnp.where(lane < 32, roll(b, 64), jnp.where((lane >= 64) & (lane < 96), 0.0, b))
            else:
                left = jnp.zeros((VECS, 128), F32)
            b = odd[i]
            right = jnp.where(lane < 32, roll(b, -32), jnp.where((lane >= 32) & (lane < 64), 0.0, b))
            change = lax.dot_general(
                coeff, jnp.concatenate([left, right], axis=0), (((1,), (0,)), ((), ())),
                precision=lax.Precision.HIGHEST, preferred_element_type=F32)
            rest.append(jnp.where((lane >= 32) & (lane < 96), 0.0, m) - change)
        return odd, rest

    levels = []
    after = (lane >= 64) & (lane < 96)
    system = [jnp.where(after, line[(a + 1) % LINE], line[a]) for a in range(LINE)]
    while len(system) > 1:
        odd, system = reduce_level(system)
        levels.append(odd)
    last = eliminate(system)[0]

    def spread(column):
        return jnp.broadcast_to(column, (VECS, 128))

    def as_row(full, shift):
        return jnp.sum(jnp.where(lane == sub + shift, full, 0.0), axis=0, keepdims=True)

    values = [spread(last[:, 96:97])]
    for odd in reversed(levels):
        new = []
        for i, m in enumerate(odd):
            row = as_row(values[i], 32)
            if i + 1 < len(values):
                row = row + as_row(values[i + 1], 64)
            picked = jnp.where(lane == 96, m, jnp.where((lane >= 32) & (lane < 96), -m * row, 0.0))
            new.append(spread(jnp.sum(picked, axis=1, keepdims=True)))
        values = [v for pair in zip(values, new) for v in pair]
    for a in range(LINE):
        table[a] = values[a]
        solved[a : a + 1, :] = as_row(values[a], 0)[:, 0:32]

    weights[...] = table[gx]
    fetch.wait()

    def component(k, _):
        for xq in range(XQ):
            for y2 in range(CY // 2):
                even = jnp.zeros((8, 128), F32)
                odd = jnp.zeros((8, 128), F32)
                for src in range(PARTS):
                    v = recv[src, k, xq, y2].astype(F32)
                    w = weights[8 * src : 8 * src + 8, :]
                    even = even + w * v[:8]
                    odd = odd + w * v[8:]
                corr_rows[2 * y2 : 2 * y2 + 1, :] = jnp.sum(even, axis=0, keepdims=True)
                corr_rows[2 * y2 + 1 : 2 * y2 + 2, :] = jnp.sum(odd, axis=0, keepdims=True)
            whole = corr_rows[...]
            corr[k, xq] = whole[:, 0:64]
            corr[k, xq + XQ] = roll(whole, 64)[:, 0:64]
        return 0

    lax.fori_loop(0, COMPS, component, 0)
    mine = pl.ds(pl.multiple_of(8 * g, 8), 8)
    blocks[1, 1] = rows[0, :, 0:32]
    blocks[0, 1] = rows[0, :, 32:64]
    blocks[2, 1] = line[lax.rem(gx + 1, LINE), mine, :][:, 64:96]
    blocks[1, 0] = rows[1, :, 0:32]
    blocks[0, 0] = rows[1, :, 32:64]
    blocks[0, 2] = rows[1, :, 64:96]
    blocks[1, 2] = rows[2, :, 0:32]
    blocks[2, 2] = rows[3, :, 32:64]
    blocks[2, 0] = rows[4, :, 64:96]


def solve(line, rows, keep):
    return pl.pallas_call(
        solve_kernel,
        name="solve",
        out_shape=(
            jax.ShapeDtypeStruct((3, 3, OWN, VECS), F32),
            jax.ShapeDtypeStruct((LINE, VECS), F32),
            jax.ShapeDtypeStruct((COMPS, CX, CY, CZ // PARTS), F32),
        ),
        in_specs=[VMEM, VMEM, ANY],
        out_specs=[VMEM] * 3,
        scratch_shapes=[
            pltpu.VMEM((PARTS, COMPS, XQ, CY // 2, 16, 128), BF16),
            pltpu.VMEM((LINE, VECS, 128), F32),
            pltpu.VMEM((VECS, 128), F32),
            pltpu.VMEM((CY, 128), F32),
            pltpu.SemaphoreType.DMA((1,)),
        ],
        compiler_params=pltpu.CompilerParams(vmem_limit_bytes=LIMIT),
    )(line, rows, keep)


def on_device(deflation, region, lame_table, residual):
    keep, line, rows = main(deflation, region, lame_table.T, residual)
    blocks, solved, corr = solve(line, rows, keep)
    return blocks[None, None], solved[:, None, :], corr


def solution(mesh):
    placed = (P("grp", None, "gx", "gy", None), P("gx", "gy", None), P(), P(None, "gx", "gy", None))
    return jax.shard_map(
        on_device,
        mesh=mesh,
        in_specs=placed,
        out_specs=(
            P("gx", "gy", None, None, "grp", None),
            P(None, "gy", None),
            P(None, "gx", "gy", "grp"),
        ),
        check_vma=False,
    )
```

```python
import functools

import jax
import jax.numpy as jnp
from jax import lax
from jax.experimental import pallas as pl
from jax.experimental.pallas import tpu as pltpu
from jax.sharding import PartitionSpec as P

MESH = pl.DeviceIdType.MESH
F32 = jnp.float32
BF16 = jnp.bfloat16
VECS = 32
OWN = 8
PARTS = 4
COMPS = 3
CX = 8
CY = 16
CZ = 256
XQ = 4
REGIONS = 8
LINE = 16
CELLS = COMPS * CX * CY * CZ
COLUMNS = {8: 4, 4: 8, 2: 16, 1: 16}
AROUND = (4, 5, 3, 6, 2, 7, 1)
ANY = pl.BlockSpec(memory_space=pl.ANY)
VMEM = pl.BlockSpec(memory_space=pltpu.VMEM)
LIMIT = 60 * 1024 * 1024


def lanes(rows):
    return lax.broadcasted_iota(jnp.int32, (rows, 128), 1)


def roll(x, shift):
    return pltpu.roll(x, shift % 128, x.ndim - 1)


def filter_z(v, edge):
    lane = lanes(v.shape[0]) & 63
    before = jnp.where(lane == 0, edge, roll(v, 1))
    after = jnp.where(lane == 63, edge, roll(v, -1))
    return v + 0.5 * (before + after)


def halves(a, b):
    low = lanes(a.shape[0]) < 64
    return jnp.where(low, a, b)

def split(value):
    high = value.astype(BF16)
    return high, (value - high.astype(F32)).astype(BF16)


def split_rows(value):
    return jnp.concatenate(split(value), axis=0)


def dot_nt(a, b):
    return lax.dot_general(a, b, (((1,), (1,)), ((), ())), preferred_element_type=F32)


def filter_x(b):
    low = lanes(b[0].shape[0]) < 64
    zero = jnp.zeros_like(b[0])
    before = [jnp.where(low, zero, roll(b[3], 64))] + b[:3]
    after = b[1:] + [jnp.where(low, roll(b[0], 64), zero)]
    return [mid + 0.5 * (lo + hi) for mid, lo, hi in zip(b, before, after)]


def fold(a, b):
    low = lanes(a.shape[0]) < 64
    blocks = []
    for t in range(2):
        ta, tb = a[:, 128 * t : 128 * t + 128], b[:, 128 * t : 128 * t + 128]
        blocks.append(jnp.where(low, ta, roll(tb, 64)))
        blocks.append(jnp.where(low, roll(ta, 64), tb))
    return blocks


def fill_order(order):
    r = lax.broadcasted_iota(jnp.int32, (128, 128), 0)
    c = lax.broadcasted_iota(jnp.int32, (128, 128), 1)
    order[...] = jnp.where(c == (r & 7) * 16 + (r >> 3), 1.0, 0.0).astype(BF16)


def pack(k, vec, order, rows, send, edge):
    lane = lanes(8) & 63
    acc = [[jnp.zeros((8, 128), F32) for _ in range(2)] for _ in range(PARTS)]
    for xq in range(XQ):
        for half in range(2):
            plane = vec[:, k, xq + XQ * half].reshape(OWN * CY, CZ)
            rows[half] = jnp.dot(order[...], plane, preferred_element_type=F32)
        for y2 in range(CY // 2):
            both = []
            for yy in range(2):
                y = 2 * y2 + yy
                blocks = fold(rows[0, 8 * y : 8 * y + 8, :], rows[1, 8 * y : 8 * y + 8, :])
                e = 2 * (CY * (xq % 2) + y)
                for g in range(PARTS):
                    value = acc[g][xq // 2]
                    if g > 0:
                        value = jnp.where(lane == e, roll(blocks[g - 1], e + 65), value)
                    if g < PARTS - 1:
                        value = jnp.where(lane == ((e + 63) & 63), roll(blocks[g + 1], e + 63), value)
                    acc[g][xq // 2] = value
                both.append(blocks)
            for g in range(PARTS):
                send[g, k, xq, y2] = jnp.concatenate([both[0][g], both[1][g]], axis=0).astype(BF16)
    for g in range(PARTS):
        edge[g, k] = jnp.concatenate(acc[g], axis=0).astype(BF16)


def material(me, region, lame, mat):
    lane = lanes(CY) & 63
    for xq in range(XQ):
        for which in range(2):
            tiles = []
            for half in range(2):
                kind = region[xq + XQ * half]
                value = jnp.zeros((CY, CZ), F32)
                for label in range(REGIONS):
                    entry = jnp.broadcast_to(lame[which : which + 1, label : label + 1], (CY, CZ))
                    value = jnp.where(kind == label, entry, value)
                tiles.append(value)
            blocks = fold(*tiles)
            own = jnp.zeros((CY, 128), F32)
            rim = jnp.zeros((CY, 128), F32)
            for g in range(PARTS):
                here = jnp.full((CY, 128), me, jnp.int32) == g
                own = jnp.where(here, blocks[g], own)
                if which == 0 and g > 0:
                    rim = jnp.where(here & (lane == 0), roll(blocks[g - 1], 65), rim)
                if which == 0 and g < PARTS - 1:
                    rim = jnp.where(here & (lane == 63), roll(blocks[g + 1], 63), rim)
            if which == 0:
                mat[0, xq] = own
                mat[1, xq] = rim
            else:
                mat[2, xq] = own


def right_side(vec, res, rhs):
    def component(i, totals):
        k, x = i // CX, i % CX
        new = []
        for p in range(OWN):
            value = vec[p, k, x].astype(F32) * res[k, x]
            value = (value[0:8, 0:128] + value[0:8, 128:256]) + (value[8:16, 0:128] + value[8:16, 128:256])
            new.append(totals[p] + value)
        return tuple(new)

    totals = lax.fori_loop(0, COMPS * CX, component, tuple(jnp.zeros((8, 128), F32) for _ in range(OWN)))
    for p in range(OWN):
        value = jnp.sum(jnp.sum(totals[p], axis=0, keepdims=True), axis=1, keepdims=True)
        rhs[p : p + 1, :] = jnp.broadcast_to(value * (1.0 / CELLS), (1, 128))


def coefficients(live_x, live_y, mat, sx, sy, sc, se, sh, db, hb, tmp):
    for target, t in ((se, 0), (sh, 1)):
        target[...] = jnp.zeros_like(target)

        def wider(own, minus, plus):
            return roll(halves(own[3], minus), 64), roll(halves(plus, own[0]), 64)

        own = [mat[t, xq] for xq in range(XQ)]
        first, last = wider(own, sx[0, t] * live_x[0], sx[1, t] * live_x[1])
        for xq, value in enumerate([first] + own + [last]):
            target[xq, 8:24, :] = value
        for j, at, src in ((0, 7, 7), (1, 24, 0)):
            own = [sy[j, t, xq, src : src + 1, :] * live_y[j] for xq in range(XQ)]
            first, last = wider(
                own,
                sc[j, t, src : src + 1, :] * (live_x[0] * live_y[j]),
                sc[2 + j, t, src : src + 1, :] * (live_x[1] * live_y[j]),
            )
            for xq, value in enumerate([first] + own + [last]):
                target[xq, at : at + 1, :] = value
    fz = [filter_z(se[xq], sh[xq]) for xq in range(XQ + 2)]
    for xq in range(XQ):
        tmp[...] = fz[xq + 1] + 0.5 * (fz[xq] + fz[xq + 2])
        smooth = tmp[8:24, :] + 0.5 * (tmp[7:23, :] + tmp[9:25, :])
        bulk = mat[2, xq]
        db[xq] = 0.5 * (0.5 + 8.0 * mat[0, xq] + smooth + bulk)
        hb[xq] = bulk * (1.0 / 6.0)


def rows_of(ref_at, yy):
    return jnp.concatenate([ref_at(src).astype(F32)[8 * yy : 8 * yy + 8] for src in range(PARTS)], axis=0)


def prepare(k, xqs, recv, zh, zf, hz, hx, hr, hy):
    for xq in xqs:
        for y2 in range(CY // 2):
            parts = [recv[src, k, xq, y2].astype(F32) for src in range(PARTS)]
            for yy in range(2):
                y = 2 * y2 + yy
                value = jnp.concatenate([p[8 * yy : 8 * yy + 8] for p in parts], axis=0)
                zf[xq, y] = value
                e = 2 * (CY * (xq % 2) + y)
                blocks = [
                    roll(zh[src, k].astype(F32)[8 * (xq // 2) : 8 * (xq // 2) + 8], -e) for src in range(PARTS)
                ]
                around = jnp.concatenate(blocks, axis=0)
                if xq == 0:
                    hx[y] = around
                if y == 0:
                    hr[xq] = around
                hz[xq, y] = filter_z(value, around)
    for xq in xqs:
        hy[xq, 0] = 0.5 * hz[xq, 0]
        hy[xq, CY + 1] = 0.5 * hz[xq, CY - 1]
        for y in range(CY):
            sides = [hz[xq, y + d] for d in (-1, 1) if 0 <= y + d < CY]
            both = sides[0] + sides[1] if len(sides) == 2 else sides[0]
            hy[xq, y + 1] = hz[xq, y] + 0.5 * both


def combine(zf, zsum, hy, se, db, hb, wide, acc):
    for y4 in range(CY // 4):
        for y in range(4 * y4, 4 * y4 + 4):
            smooth = filter_x([hy[xq, y + 1] for xq in range(XQ)])
            for xq in range(XQ):
                v = zf[xq, y]
                before = zsum[xq, y]
                zsum[xq, y] = before + v
                w = db[xq, y : y + 1, :] * v - hb[xq, y : y + 1, :] * (v + 2.0 * before)
                w = w - se[xq + 1, y + 8 : y + 9, :] * smooth[xq]
                high, rest = split(w)
                at = 128 * (XQ * (y - 4 * y4) + xq)
                wide[0:32, at : at + 128] = high
                wide[32:64, at : at + 128] = rest
                wide[64:96, at : at + 128] = v.astype(BF16)
        acc[...] += dot_nt(wide[0:64, :], wide[64:96, :])


def row_before(k, zf, hr, hy, se, sh, ly):
    smooth = filter_x([hy[xq, 0] for xq in range(XQ)])
    scaled = []
    for xq in range(XQ):
        u = se[xq + 1, 8:9, :] * zf[xq, 0]
        scaled.append(filter_z(u, sh[xq + 1, 8:9, :] * hr[xq]))
    scaled = filter_x(scaled)
    for xq in range(XQ):
        ly[k, :, 128 * xq : 128 * xq + 128] = split_rows(-(se[xq + 1, 7:8, :] * smooth[xq] + 0.5 * scaled[xq]))


def plane_before(k, zf, hx, hy, hp, se, sh, lx, lc):
    low = lanes(VECS) < 64
    zero = jnp.zeros((VECS, 128), F32)
    for y in range(CY):
        hp[y] = filter_z(se[1, y + 8 : y + 9, :] * zf[0, y], sh[1, y + 8 : y + 9, :] * hx[y])

    def plane(y):
        if y < 0:
            second = 0.5 * hp[0]
        elif y >= CY:
            second = 0.5 * hp[CY - 1]
        else:
            sides = [hp[y + d] for d in (-1, 1) if 0 <= y + d < CY]
            second = hp[y] + 0.5 * (sides[0] + sides[1] if len(sides) == 2 else sides[0])
        return -0.5 * (se[0, y + 8 : y + 9, :] * hy[0, y + 1] + second)

    for y in range(CY // 2):
        lx[k, :, 128 * y : 128 * y + 128] = split_rows(jnp.where(low, plane(y), roll(plane(y + CY // 2), 64)))
    lc[k, 0] = split_rows(jnp.where(low, zero, roll(plane(-1), 64)))
    lc[k, 1] = split_rows(jnp.where(low, plane(CY), zero))


def both_parts(value):
    return value[0:32, :] + value[32:64, :]


def plane_products(lx, xf):
    def component(k, total):
        right = [rows_of(lambda src: xf[k, src, y // 2], y % 2).astype(BF16) for y in range(CY // 2)]
        return total + dot_nt(lx[k], jnp.concatenate(right, axis=1))

    return both_parts(lax.fori_loop(0, COMPS, component, jnp.zeros((64, 32), F32)))


def other_products(ly, lc, yf, cf):
    def component(k, sums):
        right = [rows_of(lambda src: yf[k, src, xq // 2], xq % 2).astype(BF16) for xq in range(XQ)]
        new = [dot_nt(ly[k], jnp.concatenate(right, axis=1))]
        for j, yy in ((0, 1), (1, 0)):
            new.append(dot_nt(lc[k, j], rows_of(lambda src: cf[j, k, src], yy).astype(BF16)))
        return tuple(a + b for a, b in zip(sums, new))

    sums = lax.fori_loop(0, COMPS, component, tuple(jnp.zeros((64, 32), F32) for _ in range(3)))
    return [both_parts(v) for v in sums]


def pack_plane(k, recv, xs):
    low = lanes(16) < 64
    for src in range(PARTS):
        for j in range(CY // 4):
            a = recv[src, k, 3, j].astype(F32)
            b = recv[src, k, 3, j + CY // 4].astype(F32)
            xs[k, src, j] = jnp.where(low, roll(a, 64), b).astype(BF16)


def pack_row(k, recv, ys):
    for src in range(PARTS):
        for j in range(XQ // 2):
            pair = [recv[src, k, 2 * j + i, CY // 2 - 1].astype(F32)[8:16] for i in range(2)]
            ys[k, src, j] = jnp.concatenate(pair, axis=0).astype(BF16)


SIDES = ((-1, 0), (1, 0), (0, -1), (0, 1), (-1, -1), (-1, 1), (1, -1), (1, 1))
TILE = {-1: 0, 1: 3}
ROW = {-1: 0, 1: 8}


def main_kernel(
    vec_hbm, region_hbm, lame_hbm, res_hbm, keep, line, rows,
    vec, region, lame, res, order, planes, send, edge, mat, rhs, recv, zh, xf, yf, cf, sx, sy, sc, xs, ys,
    zf, zsum, hz, hx, hr, hy, hp, se, sh, db, hb, tmp, wide, acc_c, lx, ly, lc,
    part, rest, first_in, second_in, total, corner,
    in_sem, zs, zr, hs, hv, ms, mr, own_sem, keep_sem, last_sem, s1, r1, s2, r2, s3, r3, s4, r4,
):
    gx, gy, g = lax.axis_index("gx"), lax.axis_index("gy"), lax.axis_index("grp")
    nx, ny = LINE, 4
    up, down, far = lax.rem(g + 1, 4), lax.rem(g + 3, 4), lax.rem(g + 2, 4)
    near = {}
    for dx, dy in SIDES:
        near[dx, dy] = {"gx": lax.rem(gx + dx + nx, nx), "gy": lax.rem(gy + dy + ny, ny)}

    def remote(src, dst, send_sem, recv_sem, device):
        return pltpu.make_async_remote_copy(
            src_ref=src, dst_ref=dst, send_sem=send_sem, recv_sem=recv_sem,
            device_id=device, device_id_type=MESH,
        )

    barrier = pltpu.get_barrier_semaphore()
    for other in (far, up, down):
        pl.semaphore_signal(barrier, inc=1, device_id={"grp": other}, device_id_type=MESH)
    for side in SIDES:
        if side[1] != 0:
            pl.semaphore_signal(barrier, inc=1, device_id=near[side], device_id_type=MESH)
    half, place = gx // 8, lax.rem(gx, 8)
    mates = [8 * (1 - half) + lax.rem(place + i, 8) for i in (*AROUND, 0)]
    mates += [8 * half + lax.rem(place + i, 8) for i in AROUND]
    for mate in mates:
        pl.semaphore_signal(barrier, inc=1, device_id={"gx": mate}, device_id_type=MESH)

    def load(k):
        return pltpu.make_async_copy(vec_hbm.at[:, k], vec.at[:, k], in_sem.at[k])

    loads = [
        pltpu.make_async_copy(region_hbm, region, in_sem.at[3]),
        pltpu.make_async_copy(lame_hbm, lame, in_sem.at[4]),
        pltpu.make_async_copy(res_hbm, res, in_sem.at[5]),
    ]
    for k in range(COMPS):
        load(k).start()
    for c in loads:
        c.start()
    fill_order(order)

    def zcopy(src, dst, kind, k, other):
        return remote(src, dst, zs.at[kind, k], zr.at[kind, k], {"grp": other})

    def ahead(k):
        last = pl.ds(XQ - 1, 1)
        return [zcopy(send.at[o, k, last], recv.at[g, k, last], i, k, o) for i, o in enumerate((far, up, down))]

    def second(k):
        part = pl.ds(0, 2)
        return [zcopy(send.at[o, k, part], recv.at[g, k, part], 3 + i, k, o) for i, o in enumerate((far, up, down))]

    def third(k):
        part = pl.ds(2, 1)
        return [zcopy(send.at[o, k, part], recv.at[g, k, part], 9 + i, k, o) for i, o in enumerate((far, up, down))]

    def edges(k):
        return [zcopy(edge.at[o, k], zh.at[g, k], 6 + i, k, o) for i, o in enumerate((far, up, down))]

    def own(k):
        return [
            pltpu.make_async_copy(send.at[g, k], recv.at[g, k], own_sem.at[0, k]),
            pltpu.make_async_copy(edge.at[g, k], zh.at[g, k], own_sem.at[1, k]),
        ]

    def start(copies):
        for c in copies:
            c.start()

    load(0).wait()
    pack(0, vec, order, planes, send, edge)
    pl.semaphore_wait(barrier, 3 + 6 + nx - 1)
    start(ahead(0) + edges(0) + second(0) + third(0) + own(0))

    def pack_more(k, _):
        load(k).wait()
        pack(k, vec, order, planes, send, edge)
        start(ahead(k) + edges(k) + own(k))
        return 0

    lax.fori_loop(1, COMPS, pack_more, 0)
    for c in loads:
        c.wait()
    material(g, region, lame, mat)
    mats = []

    def mcopy(src, dst, side):
        i = len(mats)
        mats.append(remote(src, dst, ms.at[i], mr.at[i], near[side]))

    for dx in (-1, 1):
        mcopy(mat.at[pl.ds(0, 2), TILE[dx]], sx.at[1 if dx < 0 else 0], (dx, 0))
    for dy in (-1, 1):
        mcopy(mat.at[pl.ds(0, 2), :, pl.ds(ROW[dy], 8)], sy.at[1 if dy < 0 else 0], (0, dy))
    for dx in (-1, 1):
        for dy in (-1, 1):
            slot = (2 if dx < 0 else 0) + (1 if dy < 0 else 0)
            mcopy(mat.at[pl.ds(0, 2), TILE[dx], pl.ds(ROW[dy], 8)], sc.at[slot], (dx, dy))
    for c in mats:
        c.start()
    right_side(vec, res, rhs)
    for c in mats:
        c.wait_recv()
    one = jnp.ones((1, 128), F32)
    none = jnp.zeros((1, 128), F32)
    live_x = (jnp.where(gx > 0, one, none), jnp.where(gx < nx - 1, one, none))
    live_y = (jnp.where(gy > 0, one, none), jnp.where(gy < ny - 1, one, none))
    coefficients(live_x, live_y, mat, sx, sy, sc, se, sh, db, hb, tmp)
    for ref in (zsum, acc_c):
        ref[...] = jnp.zeros_like(ref)

    def hcopy(a, b, i, k, side):
        return remote(a, b, hs.at[k, i], hv.at[k, i], near[side])

    def early(k):
        return [hcopy(xs.at[k], xf.at[k], 0, k, (1, 0))]

    def corners(k):
        return [
            hcopy(xf.at[k, :, 3], cf.at[0, k], 1, k, (0, 1)),
            hcopy(xf.at[k, :, 0], cf.at[1, k], 2, k, (0, -1)),
        ]

    def late(k):
        return [hcopy(ys.at[k], yf.at[k], 3, k, (0, 1))]

    def planes_first(k, _):
        for c in own(k):
            c.wait()
        for c in ahead(k):
            c.wait_recv()
        pack_plane(k, recv, xs)
        start(early(k))
        return 0

    scale = 1.0 / CELLS
    mine = pl.ds(pl.multiple_of(8 * g, 8), 8)
    planes_first(0, 0)

    def component(k, _):
        for c in second(k) + edges(k):
            c.wait_recv()
        prepare(k, (3, 0, 1), recv, zh, zf, hz, hx, hr, hy)
        plane_before(k, zf, hx, hy, hp, se, sh, lx, lc)

        @pl.when(k == 0)
        def _():
            start(second(1))
            lax.fori_loop(1, COMPS, planes_first, 0)
            start(third(1) + second(2) + third(2))

        @pl.when(k == 1)
        def _():
            for i in range(COMPS):
                early(i)[0].wait_recv()
                start(corners(i))

        @pl.when(k == COMPS - 1)
        def _():
            lower = plane_products(lx, xf) * (scale * live_x[0][:, 0:32])
            part[...] = jnp.zeros_like(part)
            part[:, 32:64] = lower
            part[:, 64:96] = lower.T
            part[mine, 96:128] = rhs[:, 0:32]

        for c in third(k):
            c.wait_recv()
        pack_row(k, recv, ys)
        start(late(k))
        pltpu.make_async_copy(recv.at[:, k], keep.at[:, k], keep_sem.at[k]).start()
        prepare(k, (2,), recv, zh, zf, hz, hx, hr, hy)
        combine(zf, zsum, hy, se, db, hb, wide, acc_c)

        @pl.when(k < COMPS - 1)
        def _():
            row_before(k, zf, hr, hy, se, sh, ly)

        return 0

    lax.fori_loop(0, COMPS, component, 0)

    inner = both_parts(acc_c[...])
    part[:, 0:32] = (inner + inner.T) * scale

    sums = []
    for i, other in enumerate((far, up, down)):
        sums.append(remote(part, first_in.at[g], s1.at[i], r1.at[i], {"grp": other}))
    start(sums)
    row_before(COMPS - 1, zf, hr, hy, se, sh, ly)
    for k in range(COMPS):
        for c in corners(k) + late(k):
            c.wait_recv()
    side, *diagonal = other_products(ly, lc, yf, cf)
    side = side * (scale * live_y[0][:, 0:32])
    rest[...] = jnp.zeros_like(rest)
    rest[:, 0:32] = side
    rest[:, 128:160] = side.T
    for j in range(2):
        value = diagonal[j] * (scale * (live_x[0] * live_y[j])[:, 0:32])
        rest[:, 32 + 32 * j : 64 + 32 * j] = value
        rest[:, 160 + 32 * j : 192 + 32 * j] = value.T
    for i, other in enumerate((far, up, down)):
        theirs = pl.ds(pl.multiple_of(8 * other, 8), 8)
        sums.append(remote(rest.at[theirs], second_in.at[g], s2.at[i], r2.at[i], {"grp": other}))
    start(sums[3:])
    first_in[pl.ds(g, 1)] = part[...].reshape(1, VECS, 128)
    second_in[pl.ds(g, 1)] = rest[mine, :].reshape(1, 8, 256)
    for c in sums[:3]:
        c.wait_recv()
    total[...] = (first_in[0] + first_in[1]) + (first_in[2] + first_in[3])
    sends = []
    for i, mate in enumerate(mates):
        c = remote(total, line.at[gx], s3.at[i], r3.at[i], {"gx": mate})
        c.start()
        sends.append(c)
    kept = [
        pltpu.make_async_copy(total, line.at[gx], last_sem.at[0]),
        pltpu.make_async_copy(total.at[mine], rows.at[0], last_sem.at[1]),
        pltpu.make_async_copy(corner.at[0], rows.at[1], last_sem.at[2]),
    ]
    start(kept[:2])
    for c in sums[3:]:
        c.wait_recv()
    both = (second_in[0] + second_in[1]) + (second_in[2] + second_in[3])
    corner[0] = both[:, 0:128]
    corner[1] = both[:, 128:256]
    start(kept[2:])
    for i, to in enumerate(((0, -1), (-1, -1), (-1, 1))):
        c = remote(corner.at[1], rows.at[2 + i], s4.at[i], r4.at[i], near[to])
        c.start()
        sends.append(c)

    def finish(k, _):
        for c in ahead(k) + second(k) + third(k) + edges(k) + early(k) + corners(k) + late(k):
            c.wait_send()
        pltpu.make_async_copy(recv.at[:, k], keep.at[:, k], keep_sem.at[k]).wait()
        return 0

    lax.fori_loop(0, COMPS, finish, 0)
    for c in mats + sums:
        c.wait_send()
    for c in kept:
        c.wait()
    for c in sends:
        c.wait_recv()
    for c in sends:
        c.wait_send()


def main(deflation, region, lame_table, residual):
    field = (XQ, CY, VECS, 128)
    packed = (PARTS, COMPS, XQ, CY // 2, 16, 128)
    dma = pltpu.SemaphoreType.DMA
    return pl.pallas_call(
        main_kernel,
        name="main",
        out_shape=(
            jax.ShapeDtypeStruct(packed, BF16),
            jax.ShapeDtypeStruct((LINE, VECS, 128), F32),
            jax.ShapeDtypeStruct((5, 8, 128), F32),
        ),
        in_specs=[ANY] * 4,
        out_specs=[ANY, ANY, ANY],
        scratch_shapes=[
            pltpu.VMEM((OWN, COMPS, CX, CY, CZ), BF16),
            pltpu.VMEM((CX, CY, CZ), jnp.int32),
            pltpu.VMEM((2, REGIONS), F32),
            pltpu.VMEM((COMPS, CX, CY, CZ), F32),
            pltpu.VMEM((128, 128), BF16),
            pltpu.VMEM((2, 128, 256), F32),
            pltpu.VMEM(packed, BF16),
            pltpu.VMEM((PARTS, COMPS, 16, 128), BF16),
            pltpu.VMEM((3, XQ, CY, 128), F32),
            pltpu.VMEM((8, 128), F32),
            pltpu.VMEM(packed, BF16),
            pltpu.VMEM((PARTS, COMPS, 16, 128), BF16),
            pltpu.VMEM((COMPS, PARTS, CY // 4, 16, 128), BF16),
            pltpu.VMEM((COMPS, PARTS, XQ // 2, 16, 128), BF16),
            pltpu.VMEM((2, COMPS, PARTS, 16, 128), BF16),
            pltpu.VMEM((2, 2, CY, 128), F32),
            pltpu.VMEM((2, 2, XQ, 8, 128), F32),
            pltpu.VMEM((4, 2, 8, 128), F32),
            pltpu.VMEM((COMPS, PARTS, CY // 4, 16, 128), BF16),
            pltpu.VMEM((COMPS, PARTS, XQ // 2, 16, 128), BF16),
            pltpu.VMEM(field, F32),
            pltpu.VMEM(field, F32),
            pltpu.VMEM(field, F32),
            pltpu.VMEM((CY, VECS, 128), F32),
            pltpu.VMEM((XQ, VECS, 128), F32),
            pltpu.VMEM((XQ, CY + 2, VECS, 128), F32),
            pltpu.VMEM((CY, VECS, 128), F32),
            pltpu.VMEM((XQ + 2, 32, 128), F32),
            pltpu.VMEM((XQ + 2, 32, 128), F32),
            pltpu.VMEM((XQ, CY, 128), F32),
            pltpu.VMEM((XQ, CY, 128), F32),
            pltpu.VMEM((32, 128), F32),
            pltpu.VMEM((96, 2048), BF16),
            pltpu.VMEM((64, 32), F32),
            pltpu.VMEM((COMPS, 64, 1024), BF16),
            pltpu.VMEM((COMPS, 64, 512), BF16),
            pltpu.VMEM((COMPS, 2, 64, 128), BF16),
            pltpu.VMEM((VECS, 128), F32),
            pltpu.VMEM((VECS, 256), F32),
            pltpu.VMEM((PARTS, VECS, 128), F32),
            pltpu.VMEM((PARTS, 8, 256), F32),
            pltpu.VMEM((VECS, 128), F32),
            pltpu.VMEM((2, 8, 128), F32),
            dma((6,)),
            dma((12, COMPS)),
            dma((12, COMPS)),
            dma((COMPS, 4)),
            dma((COMPS, 4)),
            dma((8,)),
            dma((8,)),
            dma((2, COMPS)),
            dma((COMPS,)),
            dma((3,)),
            dma((3,)),
            dma((3,)),
            dma((3,)),
            dma((3,)),
            dma((LINE - 1,)),
            dma((LINE - 1,)),
            dma((3,)),
            dma((3,)),
        ],
        compiler_params=pltpu.CompilerParams(
            vmem_limit_bytes=LIMIT, collective_id=0, has_side_effects=True
        ),
    )(deflation, region, lame_table, residual)


def eliminate(blocks):
    step = COLUMNS[len(blocks)]
    m = [jnp.stack([b[8 * i : 8 * i + 8] for b in blocks]) for i in range(4)]
    sub = lax.broadcasted_iota(jnp.int32, m[0].shape, 1)

    def take(x, column, j, pivot):
        new = []
        for i in range(4):
            value = x[i] - column[i] * pivot
            new.append(jnp.where(sub == j % 8, pivot, value) if i == j // 8 else value)
        return new

    for start in range(0, VECS, step):
        columns = [[jnp.broadcast_to(x[:, :, j : j + 1], x.shape) for x in m] for j in range(start, start + step)]
        for i in range(step):
            j = start + i
            at, row = j // 8, j % 8
            column = columns[i]
            inverse = 1.0 / column[at][:, row : row + 1, :]
            for other in range(i + 1, step):
                pivot = columns[other][at][:, row : row + 1, :] * inverse
                columns[other] = take(columns[other], column, j, pivot)
            m = take(m, column, j, m[at][:, row : row + 1, :] * inverse)
    return [jnp.concatenate([m[i][b] for i in range(4)], axis=0) for b in range(len(blocks))]


def solve_kernel(line, rows, keep, blocks, solved, corr, recv, table, weights, corr_rows, sem):
    fetch = pltpu.make_async_copy(keep, recv, sem.at[0])
    fetch.start()
    gx, g = lax.axis_index("gx"), lax.axis_index("grp")
    lane = lanes(VECS)
    sub = lax.broadcasted_iota(jnp.int32, (VECS, 128), 0)

    def reduce_level(system):
        odd = eliminate(system[1::2])
        rest = []
        for i, m in enumerate(system[0::2]):
            coeff = roll(m, -32)[:, 0:64]
            if i > 0:
                b = odd[i - 1]
                left = jnp.where(lane < 32, roll(b, 64), jnp.where((lane >= 64) & (lane < 96), 0.0, b))
            else:
                left = jnp.zeros((VECS, 128), F32)
            b = odd[i]
            right = jnp.where(lane < 32, roll(b, -32), jnp.where((lane >= 32) & (lane < 64), 0.0, b))
            change = lax.dot_general(
                coeff, jnp.concatenate([left, right], axis=0), (((1,), (0,)), ((), ())),
                precision=lax.Precision.HIGHEST, preferred_element_type=F32)
            rest.append(jnp.where((lane >= 32) & (lane < 96), 0.0, m) - change)
        return odd, rest

    levels = []
    after = (lane >= 64) & (lane < 96)
    system = [jnp.where(after, line[(a + 1) % LINE], line[a]) for a in range(LINE)]
    while len(system) > 1:
        odd, system = reduce_level(system)
        levels.append(odd)
    last = eliminate(system)[0]

    def spread(column):
        return jnp.broadcast_to(column, (VECS, 128))

    def as_row(full, shift):
        return jnp.sum(jnp.where(lane == sub + shift, full, 0.0), axis=0, keepdims=True)

    values = [spread(last[:, 96:97])]
    for odd in reversed(levels):
        new = []
        for i, m in enumerate(odd):
            row = as_row(values[i], 32)
            if i + 1 < len(values):
                row = row + as_row(values[i + 1], 64)
            picked = jnp.where(lane == 96, m, jnp.where((lane >= 32) & (lane < 96), -m * row, 0.0))
            new.append(spread(jnp.sum(picked, axis=1, keepdims=True)))
        values = [v for pair in zip(values, new) for v in pair]
    for a in range(LINE):
        table[a] = values[a]
        solved[a : a + 1, :] = as_row(values[a], 0)[:, 0:32]

    weights[...] = table[gx]
    fetch.wait()

    def component(k, _):
        for xq in range(XQ):
            for y2 in range(CY // 2):
                even = jnp.zeros((8, 128), F32)
                odd = jnp.zeros((8, 128), F32)
                for src in range(PARTS):
                    v = recv[src, k, xq, y2].astype(F32)
                    w = weights[8 * src : 8 * src + 8, :]
                    even = even + w * v[:8]
                    odd = odd + w * v[8:]
                corr_rows[2 * y2 : 2 * y2 + 1, :] = jnp.sum(even, axis=0, keepdims=True)
                corr_rows[2 * y2 + 1 : 2 * y2 + 2, :] = jnp.sum(odd, axis=0, keepdims=True)
            whole = corr_rows[...]
            corr[k, xq] = whole[:, 0:64]
            corr[k, xq + XQ] = roll(whole, 64)[:, 0:64]
        return 0

    lax.fori_loop(0, COMPS, component, 0)
    mine = pl.ds(pl.multiple_of(8 * g, 8), 8)
    blocks[1, 1] = rows[0, :, 0:32]
    blocks[0, 1] = rows[0, :, 32:64]
    blocks[2, 1] = line[lax.rem(gx + 1, LINE), mine, :][:, 64:96]
    blocks[1, 0] = rows[1, :, 0:32]
    blocks[0, 0] = rows[1, :, 32:64]
    blocks[0, 2] = rows[1, :, 64:96]
    blocks[1, 2] = rows[2, :, 0:32]
    blocks[2, 2] = rows[3, :, 32:64]
    blocks[2, 0] = rows[4, :, 64:96]


def solve(line, rows, keep):
    return pl.pallas_call(
        solve_kernel,
        name="solve",
        out_shape=(
            jax.ShapeDtypeStruct((3, 3, OWN, VECS), F32),
            jax.ShapeDtypeStruct((LINE, VECS), F32),
            jax.ShapeDtypeStruct((COMPS, CX, CY, CZ // PARTS), F32),
        ),
        in_specs=[VMEM, VMEM, ANY],
        out_specs=[VMEM] * 3,
        scratch_shapes=[
            pltpu.VMEM((PARTS, COMPS, XQ, CY // 2, 16, 128), BF16),
            pltpu.VMEM((LINE, VECS, 128), F32),
            pltpu.VMEM((VECS, 128), F32),
            pltpu.VMEM((CY, 128), F32),
            pltpu.SemaphoreType.DMA((1,)),
        ],
        compiler_params=pltpu.CompilerParams(vmem_limit_bytes=LIMIT),
    )(line, rows, keep)


def on_device(deflation, region, lame_table, residual):
    keep, line, rows = main(deflation, region, lame_table.T, residual)
    blocks, solved, corr = solve(line, rows, keep)
    return blocks[None, None], solved[:, None, :], corr


def solution(mesh):
    placed = (P("grp", None, "gx", "gy", None), P("gx", "gy", None), P(), P(None, "gx", "gy", None))
    return jax.shard_map(
        on_device,
        mesh=mesh,
        in_specs=placed,
        out_specs=(
            P("gx", "gy", None, None, "grp", None),
            P(None, "gy", None),
            P(None, "gx", "gy", "grp"),
        ),
        check_vma=False,
    )
```

```python
import functools

import jax
import jax.numpy as jnp
from jax import lax
from jax.experimental import pallas as pl
from jax.experimental.pallas import tpu as pltpu
from jax.sharding import PartitionSpec as P

MESH = pl.DeviceIdType.MESH
F32 = jnp.float32
BF16 = jnp.bfloat16
VECS = 32
OWN = 8
PARTS = 4
COMPS = 3
CX = 8
CY = 16
CZ = 256
XQ = 4
REGIONS = 8
LINE = 16
CELLS = COMPS * CX * CY * CZ
COLUMNS = {8: 4, 4: 8, 2: 16, 1: 16}
AROUND = (4, 5, 3, 6, 2, 7, 1)
ANY = pl.BlockSpec(memory_space=pl.ANY)
VMEM = pl.BlockSpec(memory_space=pltpu.VMEM)
LIMIT = 60 * 1024 * 1024


def lanes(rows):
    return lax.broadcasted_iota(jnp.int32, (rows, 128), 1)


def roll(x, shift):
    return pltpu.roll(x, shift % 128, x.ndim - 1)


def filter_z(v, edge):
    lane = lanes(v.shape[0]) & 63
    before = jnp.where(lane == 0, edge, roll(v, 1))
    after = jnp.where(lane == 63, edge, roll(v, -1))
    return v + 0.5 * (before + after)


def halves(a, b):
    low = lanes(a.shape[0]) < 64
    return jnp.where(low, a, b)

def split(value):
    high = value.astype(BF16)
    return high, (value - high.astype(F32)).astype(BF16)


def split_rows(value):
    return jnp.concatenate(split(value), axis=0)


def dot_nt(a, b):
    return lax.dot_general(a, b, (((1,), (1,)), ((), ())), preferred_element_type=F32)


def filter_x(b):
    low = lanes(b[0].shape[0]) < 64
    zero = jnp.zeros_like(b[0])
    before = [jnp.where(low, zero, roll(b[3], 64))] + b[:3]
    after = b[1:] + [jnp.where(low, roll(b[0], 64), zero)]
    return [mid + 0.5 * (lo + hi) for mid, lo, hi in zip(b, before, after)]


def fold(a, b):
    low = lanes(a.shape[0]) < 64
    blocks = []
    for t in range(2):
        ta, tb = a[:, 128 * t : 128 * t + 128], b[:, 128 * t : 128 * t + 128]
        blocks.append(jnp.where(low, ta, roll(tb, 64)))
        blocks.append(jnp.where(low, roll(ta, 64), tb))
    return blocks


def fill_order(order):
    r = lax.broadcasted_iota(jnp.int32, (128, 128), 0)
    c = lax.broadcasted_iota(jnp.int32, (128, 128), 1)
    order[...] = jnp.where(c == (r & 7) * 16 + (r >> 3), 1.0, 0.0).astype(BF16)


def pack(k, vec, order, rows, send, edge):
    lane = lanes(8) & 63
    acc = [[jnp.zeros((8, 128), F32) for _ in range(2)] for _ in range(PARTS)]
    for xq in range(XQ):
        for half in range(2):
            plane = vec[:, k, xq + XQ * half].reshape(OWN * CY, CZ)
            rows[half] = jnp.dot(order[...], plane, preferred_element_type=F32)
        for y2 in range(CY // 2):
            both = []
            for yy in range(2):
                y = 2 * y2 + yy
                blocks = fold(rows[0, 8 * y : 8 * y + 8, :], rows[1, 8 * y : 8 * y + 8, :])
                e = 2 * (CY * (xq % 2) + y)
                for g in range(PARTS):
                    value = acc[g][xq // 2]
                    if g > 0:
                        value = jnp.where(lane == e, roll(blocks[g - 1], e + 65), value)
                    if g < PARTS - 1:
                        value = jnp.where(lane == ((e + 63) & 63), roll(blocks[g + 1], e + 63), value)
                    acc[g][xq // 2] = value
                both.append(blocks)
            for g in range(PARTS):
                send[g, k, xq, y2] = jnp.concatenate([both[0][g], both[1][g]], axis=0).astype(BF16)
    for g in range(PARTS):
        edge[g, k] = jnp.concatenate(acc[g], axis=0).astype(BF16)


def material(me, region, lame, mat):
    lane = lanes(CY) & 63
    for xq in range(XQ):
        for which in range(2):
            tiles = []
            for half in range(2):
                kind = region[xq + XQ * half]
                value = jnp.zeros((CY, CZ), F32)
                for label in range(REGIONS):
                    entry = jnp.broadcast_to(lame[which : which + 1, label : label + 1], (CY, CZ))
                    value = jnp.where(kind == label, entry, value)
                tiles.append(value)
            blocks = fold(*tiles)
            own = jnp.zeros((CY, 128), F32)
            rim = jnp.zeros((CY, 128), F32)
            for g in range(PARTS):
                here = jnp.full((CY, 128), me, jnp.int32) == g
                own = jnp.where(here, blocks[g], own)
                if which == 0 and g > 0:
                    rim = jnp.where(here & (lane == 0), roll(blocks[g - 1], 65), rim)
                if which == 0 and g < PARTS - 1:
                    rim = jnp.where(here & (lane == 63), roll(blocks[g + 1], 63), rim)
            if which == 0:
                mat[0, xq] = own
                mat[1, xq] = rim
            else:
                mat[2, xq] = own


def right_side(vec, res, rhs):
    def component(i, totals):
        k, x = i // CX, i % CX
        new = []
        for p in range(OWN):
            value = vec[p, k, x].astype(F32) * res[k, x]
            value = (value[0:8, 0:128] + value[0:8, 128:256]) + (value[8:16, 0:128] + value[8:16, 128:256])
            new.append(totals[p] + value)
        return tuple(new)

    totals = lax.fori_loop(0, COMPS * CX, component, tuple(jnp.zeros((8, 128), F32) for _ in range(OWN)))
    for p in range(OWN):
        value = jnp.sum(jnp.sum(totals[p], axis=0, keepdims=True), axis=1, keepdims=True)
        rhs[p : p + 1, :] = jnp.broadcast_to(value * (1.0 / CELLS), (1, 128))


def coefficients(live_x, live_y, mat, sx, sy, sc, se, sh, db, hb, tmp):
    for target, t in ((se, 0), (sh, 1)):
        target[...] = jnp.zeros_like(target)

        def wider(own, minus, plus):
            return roll(halves(own[3], minus), 64), roll(halves(plus, own[0]), 64)

        own = [mat[t, xq] for xq in range(XQ)]
        first, last = wider(own, sx[0, t] * live_x[0], sx[1, t] * live_x[1])
        for xq, value in enumerate([first] + own + [last]):
            target[xq, 8:24, :] = value
        for j, at, src in ((0, 7, 7), (1, 24, 0)):
            own = [sy[j, t, xq, src : src + 1, :] * live_y[j] for xq in range(XQ)]
            first, last = wider(
                own,
                sc[j, t, src : src + 1, :] * (live_x[0] * live_y[j]),
                sc[2 + j, t, src : src + 1, :] * (live_x[1] * live_y[j]),
            )
            for xq, value in enumerate([first] + own + [last]):
                target[xq, at : at + 1, :] = value
    fz = [filter_z(se[xq], sh[xq]) for xq in range(XQ + 2)]
    for xq in range(XQ):
        tmp[...] = fz[xq + 1] + 0.5 * (fz[xq] + fz[xq + 2])
        smooth = tmp[8:24, :] + 0.5 * (tmp[7:23, :] + tmp[9:25, :])
        bulk = mat[2, xq]
        db[xq] = 0.5 * (0.5 + 8.0 * mat[0, xq] + smooth + bulk)
        hb[xq] = bulk * (1.0 / 6.0)


def rows_of(ref_at, yy):
    return jnp.concatenate([ref_at(src).astype(F32)[8 * yy : 8 * yy + 8] for src in range(PARTS)], axis=0)


def prepare(k, xqs, recv, zh, zf, hz, hx, hr, hy):
    for xq in xqs:
        for y2 in range(CY // 2):
            parts = [recv[src, k, xq, y2].astype(F32) for src in range(PARTS)]
            for yy in range(2):
                y = 2 * y2 + yy
                value = jnp.concatenate([p[8 * yy : 8 * yy + 8] for p in parts], axis=0)
                zf[xq, y] = value
                e = 2 * (CY * (xq % 2) + y)
                blocks = [
                    roll(zh[src, k].astype(F32)[8 * (xq // 2) : 8 * (xq // 2) + 8], -e) for src in range(PARTS)
                ]
                around = jnp.concatenate(blocks, axis=0)
                if xq == 0:
                    hx[y] = around
                if y == 0:
                    hr[xq] = around
                hz[xq, y] = filter_z(value, around)
    for xq in xqs:
        hy[xq, 0] = 0.5 * hz[xq, 0]
        hy[xq, CY + 1] = 0.5 * hz[xq, CY - 1]
        for y in range(CY):
            sides = [hz[xq, y + d] for d in (-1, 1) if 0 <= y + d < CY]
            both = sides[0] + sides[1] if len(sides) == 2 else sides[0]
            hy[xq, y + 1] = hz[xq, y] + 0.5 * both


def combine(zf, zsum, hy, se, db, hb, wide, acc):
    for y4 in range(CY // 4):
        for y in range(4 * y4, 4 * y4 + 4):
            smooth = filter_x([hy[xq, y + 1] for xq in range(XQ)])
            for xq in range(XQ):
                v = zf[xq, y]
                before = zsum[xq, y]
                zsum[xq, y] = before + v
                w = db[xq, y : y + 1, :] * v - hb[xq, y : y + 1, :] * (v + 2.0 * before)
                w = w - se[xq + 1, y + 8 : y + 9, :] * smooth[xq]
                high, rest = split(w)
                at = 128 * (XQ * (y - 4 * y4) + xq)
                wide[0:32, at : at + 128] = high
                wide[32:64, at : at + 128] = rest
                wide[64:96, at : at + 128] = v.astype(BF16)
        acc[...] += dot_nt(wide[0:64, :], wide[64:96, :])


def row_before(k, zf, hr, hy, se, sh, ly):
    smooth = filter_x([hy[xq, 0] for xq in range(XQ)])
    scaled = []
    for xq in range(XQ):
        u = se[xq + 1, 8:9, :] * zf[xq, 0]
        scaled.append(filter_z(u, sh[xq + 1, 8:9, :] * hr[xq]))
    scaled = filter_x(scaled)
    for xq in range(XQ):
        ly[k, :, 128 * xq : 128 * xq + 128] = split_rows(-(se[xq + 1, 7:8, :] * smooth[xq] + 0.5 * scaled[xq]))


def plane_before(k, zf, hx, hy, hp, se, sh, lx, lc):
    low = lanes(VECS) < 64
    zero = jnp.zeros((VECS, 128), F32)
    for y in range(CY):
        hp[y] = filter_z(se[1, y + 8 : y + 9, :] * zf[0, y], sh[1, y + 8 : y + 9, :] * hx[y])

    def plane(y):
        if y < 0:
            second = 0.5 * hp[0]
        elif y >= CY:
            second = 0.5 * hp[CY - 1]
        else:
            sides = [hp[y + d] for d in (-1, 1) if 0 <= y + d < CY]
            second = hp[y] + 0.5 * (sides[0] + sides[1] if len(sides) == 2 else sides[0])
        return -0.5 * (se[0, y + 8 : y + 9, :] * hy[0, y + 1] + second)

    for y in range(CY // 2):
        lx[k, :, 128 * y : 128 * y + 128] = split_rows(jnp.where(low, plane(y), roll(plane(y + CY // 2), 64)))
    lc[k, 0] = split_rows(jnp.where(low, zero, roll(plane(-1), 64)))
    lc[k, 1] = split_rows(jnp.where(low, plane(CY), zero))


def both_parts(value):
    return value[0:32, :] + value[32:64, :]


def plane_products(lx, xf):
    def component(k, total):
        right = [rows_of(lambda src: xf[k, src, y // 2], y % 2).astype(BF16) for y in range(CY // 2)]
        return total + dot_nt(lx[k], jnp.concatenate(right, axis=1))

    return both_parts(lax.fori_loop(0, COMPS, component, jnp.zeros((64, 32), F32)))


def other_products(ly, lc, yf, cf):
    def component(k, sums):
        right = [rows_of(lambda src: yf[k, src, xq // 2], xq % 2).astype(BF16) for xq in range(XQ)]
        new = [dot_nt(ly[k], jnp.concatenate(right, axis=1))]
        for j, yy in ((0, 1), (1, 0)):
            new.append(dot_nt(lc[k, j], rows_of(lambda src: cf[j, k, src], yy).astype(BF16)))
        return tuple(a + b for a, b in zip(sums, new))

    sums = lax.fori_loop(0, COMPS, component, tuple(jnp.zeros((64, 32), F32) for _ in range(3)))
    return [both_parts(v) for v in sums]


def pack_plane(k, recv, xs):
    low = lanes(16) < 64
    for src in range(PARTS):
        for j in range(CY // 4):
            a = recv[src, k, 3, j].astype(F32)
            b = recv[src, k, 3, j + CY // 4].astype(F32)
            xs[k, src, j] = jnp.where(low, roll(a, 64), b).astype(BF16)


def pack_row(k, recv, ys):
    for src in range(PARTS):
        for j in range(XQ // 2):
            pair = [recv[src, k, 2 * j + i, CY // 2 - 1].astype(F32)[8:16] for i in range(2)]
            ys[k, src, j] = jnp.concatenate(pair, axis=0).astype(BF16)


SIDES = ((-1, 0), (1, 0), (0, -1), (0, 1), (-1, -1), (-1, 1), (1, -1), (1, 1))
TILE = {-1: 0, 1: 3}
ROW = {-1: 0, 1: 8}


def main_kernel(
    vec_hbm, region_hbm, lame_hbm, res_hbm, keep, line, rows,
    vec, region, lame, res, order, planes, send, edge, mat, rhs, recv, zh, xf, yf, cf, sx, sy, sc, xs, ys,
    zf, zsum, hz, hx, hr, hy, hp, se, sh, db, hb, tmp, wide, acc_c, lx, ly, lc,
    part, rest, first_in, second_in, total, corner,
    in_sem, zs, zr, hs, hv, ms, mr, own_sem, keep_sem, last_sem, s1, r1, s2, r2, s3, r3, s4, r4,
):
    gx, gy, g = lax.axis_index("gx"), lax.axis_index("gy"), lax.axis_index("grp")
    nx, ny = LINE, 4
    up, down, far = lax.rem(g + 1, 4), lax.rem(g + 3, 4), lax.rem(g + 2, 4)
    near = {}
    for dx, dy in SIDES:
        near[dx, dy] = {"gx": lax.rem(gx + dx + nx, nx), "gy": lax.rem(gy + dy + ny, ny)}

    def remote(src, dst, send_sem, recv_sem, device):
        return pltpu.make_async_remote_copy(
            src_ref=src, dst_ref=dst, send_sem=send_sem, recv_sem=recv_sem,
            device_id=device, device_id_type=MESH,
        )

    barrier = pltpu.get_barrier_semaphore()
    for other in (far, up, down):
        pl.semaphore_signal(barrier, inc=1, device_id={"grp": other}, device_id_type=MESH)
    for side in SIDES:
        if side[1] != 0:
            pl.semaphore_signal(barrier, inc=1, device_id=near[side], device_id_type=MESH)
    half, place = gx // 8, lax.rem(gx, 8)
    mates = [8 * (1 - half) + lax.rem(place + i, 8) for i in (*AROUND, 0)]
    mates += [8 * half + lax.rem(place + i, 8) for i in AROUND]
    for mate in mates:
        pl.semaphore_signal(barrier, inc=1, device_id={"gx": mate}, device_id_type=MESH)

    def load(k):
        return pltpu.make_async_copy(vec_hbm.at[:, k], vec.at[:, k], in_sem.at[k])

    loads = [
        pltpu.make_async_copy(region_hbm, region, in_sem.at[3]),
        pltpu.make_async_copy(lame_hbm, lame, in_sem.at[4]),
        pltpu.make_async_copy(res_hbm, res, in_sem.at[5]),
    ]
    for k in range(COMPS):
        load(k).start()
    for c in loads:
        c.start()
    fill_order(order)

    def zcopy(src, dst, kind, k, other):
        return remote(src, dst, zs.at[kind, k], zr.at[kind, k], {"grp": other})

    def ahead(k):
        last = pl.ds(XQ - 1, 1)
        return [zcopy(send.at[o, k, last], recv.at[g, k, last], i, k, o) for i, o in enumerate((far, up, down))]

    def second(k):
        part = pl.ds(0, 2)
        return [zcopy(send.at[o, k, part], recv.at[g, k, part], 3 + i, k, o) for i, o in enumerate((far, up, down))]

    def third(k):
        part = pl.ds(2, 1)
        return [zcopy(send.at[o, k, part], recv.at[g, k, part], 9 + i, k, o) for i, o in enumerate((far, up, down))]

    def edges(k):
        return [zcopy(edge.at[o, k], zh.at[g, k], 6 + i, k, o) for i, o in enumerate((far, up, down))]

    def own(k):
        return [
            pltpu.make_async_copy(send.at[g, k], recv.at[g, k], own_sem.at[0, k]),
            pltpu.make_async_copy(edge.at[g, k], zh.at[g, k], own_sem.at[1, k]),
        ]

    def start(copies):
        for c in copies:
            c.start()

    load(0).wait()
    pack(0, vec, order, planes, send, edge)
    pl.semaphore_wait(barrier, 3 + 6 + nx - 1)
    start(ahead(0) + edges(0) + second(0) + third(0) + own(0))

    def pack_more(k, _):
        load(k).wait()
        pack(k, vec, order, planes, send, edge)
        start(ahead(k) + edges(k) + own(k))
        return 0

    lax.fori_loop(1, COMPS, pack_more, 0)
    for c in loads:
        c.wait()
    material(g, region, lame, mat)
    mats = []

    def mcopy(src, dst, side):
        i = len(mats)
        mats.append(remote(src, dst, ms.at[i], mr.at[i], near[side]))

    for dx in (-1, 1):
        mcopy(mat.at[pl.ds(0, 2), TILE[dx]], sx.at[1 if dx < 0 else 0], (dx, 0))
    for dy in (-1, 1):
        mcopy(mat.at[pl.ds(0, 2), :, pl.ds(ROW[dy], 8)], sy.at[1 if dy < 0 else 0], (0, dy))
    for dx in (-1, 1):
        for dy in (-1, 1):
            slot = (2 if dx < 0 else 0) + (1 if dy < 0 else 0)
            mcopy(mat.at[pl.ds(0, 2), TILE[dx], pl.ds(ROW[dy], 8)], sc.at[slot], (dx, dy))
    for c in mats:
        c.start()
    right_side(vec, res, rhs)
    for c in mats:
        c.wait_recv()
    one = jnp.ones((1, 128), F32)
    none = jnp.zeros((1, 128), F32)
    live_x = (jnp.where(gx > 0, one, none), jnp.where(gx < nx - 1, one, none))
    live_y = (jnp.where(gy > 0, one, none), jnp.where(gy < ny - 1, one, none))
    coefficients(live_x, live_y, mat, sx, sy, sc, se, sh, db, hb, tmp)
    for ref in (zsum, acc_c):
        ref[...] = jnp.zeros_like(ref)

    def hcopy(a, b, i, k, side):
        return remote(a, b, hs.at[k, i], hv.at[k, i], near[side])

    def early(k):
        return [hcopy(xs.at[k], xf.at[k], 0, k, (1, 0))]

    def corners(k):
        return [
            hcopy(xf.at[k, :, 3], cf.at[0, k], 1, k, (0, 1)),
            hcopy(xf.at[k, :, 0], cf.at[1, k], 2, k, (0, -1)),
        ]

    def late(k):
        return [hcopy(ys.at[k], yf.at[k], 3, k, (0, 1))]

    def planes_first(k, _):
        for c in own(k):
            c.wait()
        for c in ahead(k):
            c.wait_recv()
        pack_plane(k, recv, xs)
        start(early(k))
        return 0

    scale = 1.0 / CELLS
    mine = pl.ds(pl.multiple_of(8 * g, 8), 8)
    planes_first(0, 0)

    def component(k, _):
        for c in second(k) + edges(k):
            c.wait_recv()
        prepare(k, (3, 0, 1), recv, zh, zf, hz, hx, hr, hy)
        plane_before(k, zf, hx, hy, hp, se, sh, lx, lc)

        @pl.when(k == 0)
        def _():
            start(second(1))
            lax.fori_loop(1, COMPS, planes_first, 0)
            start(third(1) + second(2) + third(2))

        @pl.when(k == 1)
        def _():
            for i in range(COMPS):
                early(i)[0].wait_recv()
                start(corners(i))

        @pl.when(k == COMPS - 1)
        def _():
            lower = plane_products(lx, xf) * (scale * live_x[0][:, 0:32])
            part[...] = jnp.zeros_like(part)
            part[:, 32:64] = lower
            part[:, 64:96] = lower.T
            part[mine, 96:128] = rhs[:, 0:32]

        for c in third(k):
            c.wait_recv()
        pack_row(k, recv, ys)
        start(late(k))
        prepare(k, (2,), recv, zh, zf, hz, hx, hr, hy)
        combine(zf, zsum, hy, se, db, hb, wide, acc_c)

        @pl.when(k < COMPS - 1)
        def _():
            row_before(k, zf, hr, hy, se, sh, ly)

        return 0

    lax.fori_loop(0, COMPS, component, 0)

    inner = both_parts(acc_c[...])
    part[:, 0:32] = (inner + inner.T) * scale

    sums = []
    for i, other in enumerate((far, up, down)):
        sums.append(remote(part, first_in.at[g], s1.at[i], r1.at[i], {"grp": other}))
    start(sums)
    row_before(COMPS - 1, zf, hr, hy, se, sh, ly)
    for k in range(COMPS):
        for c in corners(k) + late(k):
            c.wait_recv()
    side, *diagonal = other_products(ly, lc, yf, cf)
    side = side * (scale * live_y[0][:, 0:32])
    rest[...] = jnp.zeros_like(rest)
    rest[:, 0:32] = side
    rest[:, 128:160] = side.T
    for j in range(2):
        value = diagonal[j] * (scale * (live_x[0] * live_y[j])[:, 0:32])
        rest[:, 32 + 32 * j : 64 + 32 * j] = value
        rest[:, 160 + 32 * j : 192 + 32 * j] = value.T
    for i, other in enumerate((far, up, down)):
        theirs = pl.ds(pl.multiple_of(8 * other, 8), 8)
        sums.append(remote(rest.at[theirs], second_in.at[g], s2.at[i], r2.at[i], {"grp": other}))
    start(sums[3:])
    first_in[pl.ds(g, 1)] = part[...].reshape(1, VECS, 128)
    second_in[pl.ds(g, 1)] = rest[mine, :].reshape(1, 8, 256)
    for c in sums[:3]:
        c.wait_recv()
    total[...] = (first_in[0] + first_in[1]) + (first_in[2] + first_in[3])
    sends = []
    for i, mate in enumerate(mates):
        c = remote(total, line.at[gx], s3.at[i], r3.at[i], {"gx": mate})
        c.start()
        sends.append(c)
    kept = [
        pltpu.make_async_copy(total, line.at[gx], last_sem.at[0]),
        pltpu.make_async_copy(total.at[mine], rows.at[0], last_sem.at[1]),
        pltpu.make_async_copy(corner.at[0], rows.at[1], last_sem.at[2]),
    ]
    start(kept[:2])
    start(pltpu.make_async_copy(recv.at[:, k], keep.at[:, k], keep_sem.at[k]) for k in range(COMPS))
    for c in sums[3:]:
        c.wait_recv()
    both = (second_in[0] + second_in[1]) + (second_in[2] + second_in[3])
    corner[0] = both[:, 0:128]
    corner[1] = both[:, 128:256]
    start(kept[2:])
    for i, to in enumerate(((0, -1), (-1, -1), (-1, 1))):
        c = remote(corner.at[1], rows.at[2 + i], s4.at[i], r4.at[i], near[to])
        c.start()
        sends.append(c)

    def finish(k, _):
        for c in ahead(k) + second(k) + third(k) + edges(k) + early(k) + corners(k) + late(k):
            c.wait_send()
        pltpu.make_async_copy(recv.at[:, k], keep.at[:, k], keep_sem.at[k]).wait()
        return 0

    lax.fori_loop(0, COMPS, finish, 0)
    for c in mats + sums:
        c.wait_send()
    for c in kept:
        c.wait()
    for c in sends:
        c.wait_recv()
    for c in sends:
        c.wait_send()


def main(deflation, region, lame_table, residual):
    field = (XQ, CY, VECS, 128)
    packed = (PARTS, COMPS, XQ, CY // 2, 16, 128)
    dma = pltpu.SemaphoreType.DMA
    return pl.pallas_call(
        main_kernel,
        name="main",
        out_shape=(
            jax.ShapeDtypeStruct(packed, BF16),
            jax.ShapeDtypeStruct((LINE, VECS, 128), F32),
            jax.ShapeDtypeStruct((5, 8, 128), F32),
        ),
        in_specs=[ANY] * 4,
        out_specs=[ANY, ANY, ANY],
        scratch_shapes=[
            pltpu.VMEM((OWN, COMPS, CX, CY, CZ), BF16),
            pltpu.VMEM((CX, CY, CZ), jnp.int32),
            pltpu.VMEM((2, REGIONS), F32),
            pltpu.VMEM((COMPS, CX, CY, CZ), F32),
            pltpu.VMEM((128, 128), BF16),
            pltpu.VMEM((2, 128, 256), F32),
            pltpu.VMEM(packed, BF16),
            pltpu.VMEM((PARTS, COMPS, 16, 128), BF16),
            pltpu.VMEM((3, XQ, CY, 128), F32),
            pltpu.VMEM((8, 128), F32),
            pltpu.VMEM(packed, BF16),
            pltpu.VMEM((PARTS, COMPS, 16, 128), BF16),
            pltpu.VMEM((COMPS, PARTS, CY // 4, 16, 128), BF16),
            pltpu.VMEM((COMPS, PARTS, XQ // 2, 16, 128), BF16),
            pltpu.VMEM((2, COMPS, PARTS, 16, 128), BF16),
            pltpu.VMEM((2, 2, CY, 128), F32),
            pltpu.VMEM((2, 2, XQ, 8, 128), F32),
            pltpu.VMEM((4, 2, 8, 128), F32),
            pltpu.VMEM((COMPS, PARTS, CY // 4, 16, 128), BF16),
            pltpu.VMEM((COMPS, PARTS, XQ // 2, 16, 128), BF16),
            pltpu.VMEM(field, F32),
            pltpu.VMEM(field, F32),
            pltpu.VMEM(field, F32),
            pltpu.VMEM((CY, VECS, 128), F32),
            pltpu.VMEM((XQ, VECS, 128), F32),
            pltpu.VMEM((XQ, CY + 2, VECS, 128), F32),
            pltpu.VMEM((CY, VECS, 128), F32),
            pltpu.VMEM((XQ + 2, 32, 128), F32),
            pltpu.VMEM((XQ + 2, 32, 128), F32),
            pltpu.VMEM((XQ, CY, 128), F32),
            pltpu.VMEM((XQ, CY, 128), F32),
            pltpu.VMEM((32, 128), F32),
            pltpu.VMEM((96, 2048), BF16),
            pltpu.VMEM((64, 32), F32),
            pltpu.VMEM((COMPS, 64, 1024), BF16),
            pltpu.VMEM((COMPS, 64, 512), BF16),
            pltpu.VMEM((COMPS, 2, 64, 128), BF16),
            pltpu.VMEM((VECS, 128), F32),
            pltpu.VMEM((VECS, 256), F32),
            pltpu.VMEM((PARTS, VECS, 128), F32),
            pltpu.VMEM((PARTS, 8, 256), F32),
            pltpu.VMEM((VECS, 128), F32),
            pltpu.VMEM((2, 8, 128), F32),
            dma((6,)),
            dma((12, COMPS)),
            dma((12, COMPS)),
            dma((COMPS, 4)),
            dma((COMPS, 4)),
            dma((8,)),
            dma((8,)),
            dma((2, COMPS)),
            dma((COMPS,)),
            dma((3,)),
            dma((3,)),
            dma((3,)),
            dma((3,)),
            dma((3,)),
            dma((LINE - 1,)),
            dma((LINE - 1,)),
            dma((3,)),
            dma((3,)),
        ],
        compiler_params=pltpu.CompilerParams(
            vmem_limit_bytes=LIMIT, collective_id=0, has_side_effects=True
        ),
    )(deflation, region, lame_table, residual)


def eliminate(blocks):
    step = COLUMNS[len(blocks)]
    m = [jnp.stack([b[8 * i : 8 * i + 8] for b in blocks]) for i in range(4)]
    sub = lax.broadcasted_iota(jnp.int32, m[0].shape, 1)

    def take(x, column, j, pivot):
        new = []
        for i in range(4):
            value = x[i] - column[i] * pivot
            new.append(jnp.where(sub == j % 8, pivot, value) if i == j // 8 else value)
        return new

    for start in range(0, VECS, step):
        columns = [[jnp.broadcast_to(x[:, :, j : j + 1], x.shape) for x in m] for j in range(start, start + step)]
        for i in range(step):
            j = start + i
            at, row = j // 8, j % 8
            column = columns[i]
            inverse = 1.0 / column[at][:, row : row + 1, :]
            for other in range(i + 1, step):
                pivot = columns[other][at][:, row : row + 1, :] * inverse
                columns[other] = take(columns[other], column, j, pivot)
            m = take(m, column, j, m[at][:, row : row + 1, :] * inverse)
    return [jnp.concatenate([m[i][b] for i in range(4)], axis=0) for b in range(len(blocks))]


def solve_kernel(line, rows, keep, blocks, solved, corr, recv, table, weights, corr_rows, sem):
    fetch = pltpu.make_async_copy(keep, recv, sem.at[0])
    fetch.start()
    gx, g = lax.axis_index("gx"), lax.axis_index("grp")
    lane = lanes(VECS)
    sub = lax.broadcasted_iota(jnp.int32, (VECS, 128), 0)

    def reduce_level(system):
        odd = eliminate(system[1::2])
        rest = []
        for i, m in enumerate(system[0::2]):
            coeff = roll(m, -32)[:, 0:64]
            if i > 0:
                b = odd[i - 1]
                left = jnp.where(lane < 32, roll(b, 64), jnp.where((lane >= 64) & (lane < 96), 0.0, b))
            else:
                left = jnp.zeros((VECS, 128), F32)
            b = odd[i]
            right = jnp.where(lane < 32, roll(b, -32), jnp.where((lane >= 32) & (lane < 64), 0.0, b))
            change = lax.dot_general(
                coeff, jnp.concatenate([left, right], axis=0), (((1,), (0,)), ((), ())),
                precision=lax.Precision.HIGHEST, preferred_element_type=F32)
            rest.append(jnp.where((lane >= 32) & (lane < 96), 0.0, m) - change)
        return odd, rest

    levels = []
    after = (lane >= 64) & (lane < 96)
    system = [jnp.where(after, line[(a + 1) % LINE], line[a]) for a in range(LINE)]
    while len(system) > 1:
        odd, system = reduce_level(system)
        levels.append(odd)
    last = eliminate(system)[0]

    def spread(column):
        return jnp.broadcast_to(column, (VECS, 128))

    def as_row(full, shift):
        return jnp.sum(jnp.where(lane == sub + shift, full, 0.0), axis=0, keepdims=True)

    values = [spread(last[:, 96:97])]
    for odd in reversed(levels):
        new = []
        for i, m in enumerate(odd):
            row = as_row(values[i], 32)
            if i + 1 < len(values):
                row = row + as_row(values[i + 1], 64)
            picked = jnp.where(lane == 96, m, jnp.where((lane >= 32) & (lane < 96), -m * row, 0.0))
            new.append(spread(jnp.sum(picked, axis=1, keepdims=True)))
        values = [v for pair in zip(values, new) for v in pair]
    for a in range(LINE):
        table[a] = values[a]
        solved[a : a + 1, :] = as_row(values[a], 0)[:, 0:32]

    weights[...] = table[gx]
    fetch.wait()

    def component(k, _):
        for xq in range(XQ):
            for y2 in range(CY // 2):
                even = jnp.zeros((8, 128), F32)
                odd = jnp.zeros((8, 128), F32)
                for src in range(PARTS):
                    v = recv[src, k, xq, y2].astype(F32)
                    w = weights[8 * src : 8 * src + 8, :]
                    even = even + w * v[:8]
                    odd = odd + w * v[8:]
                corr_rows[2 * y2 : 2 * y2 + 1, :] = jnp.sum(even, axis=0, keepdims=True)
                corr_rows[2 * y2 + 1 : 2 * y2 + 2, :] = jnp.sum(odd, axis=0, keepdims=True)
            whole = corr_rows[...]
            corr[k, xq] = whole[:, 0:64]
            corr[k, xq + XQ] = roll(whole, 64)[:, 0:64]
        return 0

    lax.fori_loop(0, COMPS, component, 0)
    mine = pl.ds(pl.multiple_of(8 * g, 8), 8)
    blocks[1, 1] = rows[0, :, 0:32]
    blocks[0, 1] = rows[0, :, 32:64]
    blocks[2, 1] = line[lax.rem(gx + 1, LINE), mine, :][:, 64:96]
    blocks[1, 0] = rows[1, :, 0:32]
    blocks[0, 0] = rows[1, :, 32:64]
    blocks[0, 2] = rows[1, :, 64:96]
    blocks[1, 2] = rows[2, :, 0:32]
    blocks[2, 2] = rows[3, :, 32:64]
    blocks[2, 0] = rows[4, :, 64:96]


def solve(line, rows, keep):
    return pl.pallas_call(
        solve_kernel,
        name="solve",
        out_shape=(
            jax.ShapeDtypeStruct((3, 3, OWN, VECS), F32),
            jax.ShapeDtypeStruct((LINE, VECS), F32),
            jax.ShapeDtypeStruct((COMPS, CX, CY, CZ // PARTS), F32),
        ),
        in_specs=[VMEM, VMEM, ANY],
        out_specs=[VMEM] * 3,
        scratch_shapes=[
            pltpu.VMEM((PARTS, COMPS, XQ, CY // 2, 16, 128), BF16),
            pltpu.VMEM((LINE, VECS, 128), F32),
            pltpu.VMEM((VECS, 128), F32),
            pltpu.VMEM((CY, 128), F32),
            pltpu.SemaphoreType.DMA((1,)),
        ],
        compiler_params=pltpu.CompilerParams(vmem_limit_bytes=LIMIT),
    )(line, rows, keep)


def on_device(deflation, region, lame_table, residual):
    keep, line, rows = main(deflation, region, lame_table.T, residual)
    blocks, solved, corr = solve(line, rows, keep)
    return blocks[None, None], solved[:, None, :], corr


def solution(mesh):
    placed = (P("grp", None, "gx", "gy", None), P("gx", "gy", None), P(), P(None, "gx", "gy", None))
    return jax.shard_map(
        on_device,
        mesh=mesh,
        in_specs=placed,
        out_specs=(
            P("gx", "gy", None, None, "grp", None),
            P(None, "gy", None),
            P(None, "gx", "gy", "grp"),
        ),
        check_vma=False,
    )
```
